32 devices in a mesh: dp: 8 (over z, x), tensor: 4 (over y, core).
Axes of the slice: x: 2, y: 2, z: 4, core: 2. Of those that a mesh axis runs over, the one named last changes fastest.
Arguments:
- block_input: bfloat16 [8, 1024, 2048], P('dp'), may hold values from -6 to 6
- cotangent: bfloat16 [8, 1024, 2048], P('dp'), may hold values from -6 to 6
- positions: int32 [8, 1024], P('dp'), may hold values from 0 to 1023, as said below
- query_weight: float32 [2048, 2048], P('dp', 'tensor'), may hold values from -0.25 to 0.25
- keyval_weight: float32 [2048, 2, 512], P('dp', None, 'tensor'), may hold values from -0.125 to 0.125
- output_weight: float32 [2048, 2048], P('dp', 'tensor'), may hold values from -0.375 to 0.375
- gateup_weight: float32 [2048, 2, 8192], P('dp', None, 'tensor'), may hold values from -0.125 to 0.125
- down_weight: float32 [2048, 8192], P('dp', 'tensor'), may hold values from -0.0625 to 0.0625
- norm_gains: float32 [2, 2048], P(None, 'dp'), may hold values from 0.5 to 1.5
- query_first: float32 [2048, 2048], P('dp', 'tensor'), may hold values from -64 to 64
- keyval_first: float32 [2048, 2, 512], P('dp', None, 'tensor'), may hold values from -128 to 128
- output_first: float32 [2048, 2048], P('dp', 'tensor'), may hold values from -16 to 16
- gateup_first: float32 [2048, 2, 8192], P('dp', None, 'tensor'), may hold values from -16 to 16
- down_first: float32 [2048, 8192], P('dp', 'tensor'), may hold values from -32 to 32
- gains_first: float32 [2, 2048], P(None, 'dp'), may hold values from -96 to 96
- query_second: float32 [2048, 2048], P('dp', 'tensor'), may hold values from 212.992 to 3440.64
- keyval_second: float32 [2048, 2, 512], P('dp', None, 'tensor'), may hold values from 851.968 to 13762.56
- output_second: float32 [2048, 2048], P('dp', 'tensor'), may hold values from 19.16928 to 309.6576
- gateup_second: float32 [2048, 2, 8192], P('dp', None, 'tensor'), may hold values from 19.16928 to 309.6576
- down_second: float32 [2048, 8192], P('dp', 'tensor'), may hold values from 76.67712 to 1236.992
- gains_second: float32 [2, 2048], P(None, 'dp'), may hold values from 479.232 to 7741.44
Outputs:
- block_output: float32 [8, 1024, 2048], P('dp')
- input_grad: float32 [8, 1024, 2048], P('dp')
- query_grad: float32 [2048, 2048], P('dp', 'tensor')
- keyval_grad: float32 [2048, 2, 512], P('dp', None, 'tensor')
- output_grad: float32 [2048, 2048], P('dp', 'tensor')
- gateup_grad: float32 [2048, 2, 8192], P('dp', None, 'tensor')
- down_grad: float32 [2048, 8192], P('dp', 'tensor')
- gains_grad: float32 [2, 2048], P(None, 'dp')
- query_mean: float32 [2048, 2048], P('dp', 'tensor')
- keyval_mean: float32 [2048, 2, 512], P('dp', None, 'tensor')
- output_mean: float32 [2048, 2048], P('dp', 'tensor')
- gateup_mean: float32 [2048, 2, 8192], P('dp', None, 'tensor')
- down_mean: float32 [2048, 8192], P('dp', 'tensor')
- gains_mean: float32 [2, 2048], P(None, 'dp')
- query_square: float32 [2048, 2048], P('dp', 'tensor')
- keyval_square: float32 [2048, 2, 512], P('dp', None, 'tensor')
- output_square: float32 [2048, 2048], P('dp', 'tensor')
- gateup_square: float32 [2048, 2, 8192], P('dp', None, 'tensor')
- down_square: float32 [2048, 8192], P('dp', 'tensor')
- gains_square: float32 [2, 2048], P(None, 'dp')
- query_next: float32 [2048, 2048], P('dp', 'tensor')
- keyval_next: float32 [2048, 2, 512], P('dp', None, 'tensor')
- output_next: float32 [2048, 2048], P('dp', 'tensor')
- gateup_next: float32 [2048, 2, 8192], P('dp', None, 'tensor')
- down_next: float32 [2048, 8192], P('dp', 'tensor')
- gains_next: float32 [2, 2048], P(None, 'dp')
The draws below stay inside these ranges and needn't reach their ends.
Inputs may be any that keep to these rules, and one draw needn't show every extreme that they name: `positions`: each sequence is a pack of documents: a token's position counts the tokens before it in its own document, from 0 at the document's first token; at least one sequence is a single document.
All inputs are finite; a program needn't handle non-finite values.
Results may differ from the reference program's by a relative error of at most 0.02.
Values may be sent and summed in bfloat16 or wider, within the bound.
A program may use at most 256 MiB of HBM per device.

```python
import math
import jax
import jax.numpy as jnp
from jax import lax

D = 2048
FF = 8192
HQ = 32
KV = 8
HD = 64
LENGTH = 1024
STEP = 10
SEQS = 8


def draw_positions(key, part):
    key = jax.random.fold_in(key, 11)
    start_key, pick_key = jax.random.split(key)
    spacing = max(LENGTH // 4, 2)
    index = jnp.arange(LENGTH, dtype=jnp.int32)
    starts = jax.random.randint(start_key, (SEQS, LENGTH), 0, spacing) == 0
    starts = jnp.logical_or(starts, index[None, :] == 0)
    single = jax.random.randint(pick_key, (), 0, SEQS)
    sequence_index = jnp.arange(SEQS, dtype=jnp.int32)[:, None]
    starts = jnp.where(sequence_index == single, index[None, :] == 0, starts)
    begins = lax.cummax(jnp.where(starts, index[None, :], 0), axis=1)
    return (index[None, :] - begins).astype(jnp.int32)


def block_levels(stream_key, extent, pieces, least, high):
    def one(axis_at, blocks):
        steps = jax.random.uniform(jax.random.fold_in(jax.random.fold_in(stream_key, 6), axis_at), (blocks,), jnp.float32, least / len(pieces), high / len(pieces))
        return jnp.repeat(jnp.exp(steps), extent[axis_at] // blocks).reshape((-1,) + (1,) * (len(extent) - axis_at - 1))

    loudness = one(*pieces[0])
    for cut in pieces[1:]:
        loudness = loudness * one(*cut)
    return loudness


def bell_draw(stream_key, extent, spread, limit, cuts=(), kind=jnp.bfloat16):
    loudness = block_levels(stream_key, extent, cuts, -0.22, 0.18) if cuts else 1.0
    drawn = jax.random.normal(stream_key, extent, jnp.float32) * spread * loudness
    return jnp.minimum(jnp.maximum(drawn, -limit), limit).astype(kind)


def setup_inputs(seed: int = 0) -> dict:
    splits = jax.random.split(jax.random.key(seed), 22)
    return {
        "block_input": bell_draw(splits[0], (SEQS, LENGTH, D), 1.0, 6.0, ((0, 8),)),
        "cotangent": bell_draw(splits[1], (SEQS, LENGTH, D), 1.0, 6.0, ((0, 8),)),
        "positions": draw_positions(jax.random.fold_in(splits[21], 71), 0),
        "query_weight": bell_draw(splits[3], (D, HQ * HD), (D // 4) ** -0.5, 0.25, ((0, 8), (1, 4)), jnp.float32),
        "keyval_weight": bell_draw(splits[4], (D, 2, KV * HD), D ** -0.5, 0.125, ((0, 8), (2, 4)), jnp.float32),
        "output_weight": bell_draw(splits[5], (D, HQ * HD), (max(HQ * HD // 8, 1)) ** -0.5, 0.375, ((0, 8), (1, 4)), jnp.float32),
        "gateup_weight": bell_draw(splits[6], (D, 2, FF), D ** -0.5, 0.125, ((0, 8), (2, 4)), jnp.float32),
        "down_weight": bell_draw(splits[7], (D, FF), FF ** -0.5, 0.0625, ((0, 8), (1, 4)), jnp.float32),
        "norm_gains": jnp.clip(1.0 + 0.1 * jax.random.normal(splits[8], (2, D), jnp.float32), 0.5, 1.5),
        "query_first": bell_draw(splits[9], (D, HQ * HD), (0.11 * (SEQS * LENGTH) ** 0.5), 64.0, ((0, 8), (1, 4)), jnp.float32),
        "keyval_first": bell_draw(splits[10], (D, 2, KV * HD), (0.22 * (SEQS * LENGTH) ** 0.5), 128.0, ((0, 8), (2, 4)), jnp.float32),
        "output_first": bell_draw(splits[11], (D, HQ * HD), (0.033 * (SEQS * LENGTH) ** 0.5), 16.0, ((0, 8), (1, 4)), jnp.float32),
        "gateup_first": bell_draw(splits[12], (D, 2, FF), (0.033 * (SEQS * LENGTH) ** 0.5), 16.0, ((0, 8), (2, 4)), jnp.float32),
        "down_first": bell_draw(splits[13], (D, FF), (0.066 * (SEQS * LENGTH) ** 0.5), 32.0, ((0, 8), (1, 4)), jnp.float32),
        "gains_first": bell_draw(splits[14], (2, D), (0.165 * (SEQS * LENGTH) ** 0.5), 96.0, ((1, 8),), jnp.float32),
        "query_second": jnp.clip(jnp.exp(math.log(3440.64) - 2.7821581 * jax.random.uniform(splits[15], (D, HQ * HD), jnp.float32) ** block_levels(splits[15], (D, HQ * HD), ((0, 8), (1, 4)), -0.2, 0.2)), 212.992, 3440.64),
        "keyval_second": jnp.clip(jnp.exp(math.log(13762.56) - 2.7821581 * jax.random.uniform(splits[16], (D, 2, KV * HD), jnp.float32) ** block_levels(splits[16], (D, 2, KV * HD), ((0, 8), (2, 4)), -0.2, 0.2)), 851.968, 13762.56),
        "output_second": jnp.clip(jnp.exp(math.log(309.6576) - 2.7821582 * jax.random.uniform(splits[17], (D, HQ * HD), jnp.float32) ** block_levels(splits[17], (D, HQ * HD), ((0, 8), (1, 4)), -0.2, 0.2)), 19.16928, 309.6576),
        "gateup_second": jnp.clip(jnp.exp(math.log(309.6576) - 2.7821582 * jax.random.uniform(splits[18], (D, 2, FF), jnp.float32) ** block_levels(splits[18], (D, 2, FF), ((0, 8), (2, 4)), -0.2, 0.2)), 19.16928, 309.6576),
        "down_second": jnp.clip(jnp.exp(math.log(1236.992) - 2.7808345 * jax.random.uniform(splits[19], (D, FF), jnp.float32) ** block_levels(splits[19], (D, FF), ((0, 8), (1, 4)), -0.2, 0.2)), 76.67712, 1236.992),
        "gains_second": jnp.clip(jnp.exp(math.log(7741.44) - 2.7821582 * jax.random.uniform(splits[20], (2, D), jnp.float32) ** block_levels(splits[20], (2, D), ((1, 8),), -0.2, 0.2)), 479.232, 7741.44),
    }


NORM_EPS = 1e-05
ROPE_BASE = 500000.0
BETA_ONE = 0.9
BETA_TWO = 0.95
ADAM_EPS = 1e-08
MATRIX_RATE = 0.05
GAIN_RATE = 0.6
WEIGHT_DECAY = 0.1
MASKED = -1e+30
HIGH_PRECISION = lax.Precision.HIGHEST

@jax.custom_vjp
def low(v):
    return lax.optimization_barrier(v.astype(jnp.bfloat16)).astype(jnp.float32)

@jax.custom_vjp
def lower_precision_backward(v):
    return v

def low_keep(v):
    return (low(v), None)

def low_pass(kept, grad):
    return (grad,)

def back_keep(v):
    return (v, None)

def back_low(kept, grad):
    return (low(grad),)
low.defvjp(low_keep, low_pass)
lower_precision_backward.defvjp(back_keep, back_low)

def rms_norm(values, gain):
    factor = lax.rsqrt(lax.optimization_barrier(jnp.mean(values * values, axis=-1, keepdims=True)) + NORM_EPS)
    return values * factor * gain

def angle_tables(positions):
    half_steps = jnp.arange(HD // 2, dtype=jnp.float32)
    frequency = jnp.exp(half_steps * (-2.0 / HD) * math.log(ROPE_BASE))
    angles = positions.astype(jnp.float32)[..., None] * frequency
    cosine = jnp.cos(angles)
    sine = jnp.sin(angles)
    return (jnp.concatenate([cosine, cosine], axis=-1)[..., None, :], jnp.concatenate([sine, sine], axis=-1)[..., None, :])

def rotate(values, cosine, sine):
    middle_index = values.shape[-1] // 2
    turned = jnp.concatenate([-values[..., middle_index:], values[..., :middle_index]], axis=-1)
    return values * cosine + turned * sine

def attend_one(parts):
    query, key_rot, value = parts
    length = query.shape[0]
    grouped = query.reshape(length, KV, HQ // KV, HD)
    scores = lower_precision_backward(jnp.einsum('qkgd,lkd->kgql', grouped, key_rot, precision=HIGH_PRECISION) * HD ** (-0.5))
    row_index = lax.broadcasted_iota(jnp.int32, (length, length), 0)
    column_index = lax.broadcasted_iota(jnp.int32, (length, length), 1)
    scores = jnp.where(column_index <= row_index, scores, MASKED)
    probs = low(jax.nn.softmax(scores, axis=-1))
    mixed_heads = jnp.einsum('kgql,lkd->qkgd', probs, value, precision=HIGH_PRECISION)
    return mixed_heads.reshape(length, HQ * HD)

def forward(params, input_rows, positions):
    query_projection_weight, key_value_weight, output_projection_weight, gate_up_weight, down_projection_weight, gains = [low(weight) for weight in params]
    count = input_rows.shape[0]
    length = input_rows.shape[1]
    normalized_rows = low(rms_norm(input_rows, gains[0]))
    query_before_rotation = lower_precision_backward(jnp.einsum('vow,wz->voz', normalized_rows, query_projection_weight, precision=HIGH_PRECISION))
    key_value_before = lower_precision_backward(jnp.einsum('rmk,kij->rmij', normalized_rows, key_value_weight, precision=HIGH_PRECISION))
    cosine, sine = angle_tables(positions)
    query = low(rotate(query_before_rotation.reshape(count, length, HQ, HD), cosine, sine))
    key_rot = low(rotate(key_value_before[:, :, 0].reshape(count, length, KV, HD), cosine, sine))
    value = low(key_value_before[:, :, 1].reshape(count, length, KV, HD))
    mixed_heads = lax.map(jax.checkpoint(attend_one), (query, key_rot, value))
    mixed_heads = low(lower_precision_backward(mixed_heads))
    middle_rows = input_rows + lower_precision_backward(jnp.einsum('iaz,xz->iax', mixed_heads, output_projection_weight, precision=HIGH_PRECISION))
    normalized_second = low(rms_norm(middle_rows, gains[1]))
    gate_up_rows = lower_precision_backward(jnp.einsum('ang,gbo->anbo', normalized_second, gate_up_weight, precision=HIGH_PRECISION))
    hidden_rows = low(jax.nn.silu(gate_up_rows[:, :, 0]) * gate_up_rows[:, :, 1])
    return middle_rows + lower_precision_backward(jnp.einsum('eym,om->eyo', hidden_rows, down_projection_weight, precision=HIGH_PRECISION))

def adamw(weight, grad, first, second, rate, decay):
    first = BETA_ONE * first + (1.0 - BETA_ONE) * grad
    second = BETA_TWO * second + (1.0 - BETA_TWO) * grad * grad
    fixed_first = first / (1.0 - BETA_ONE ** STEP)
    fixed_second = second / (1.0 - BETA_TWO ** STEP)
    weight = weight - rate * (fixed_first / (jnp.sqrt(fixed_second) + ADAM_EPS) + decay * weight)
    return (first, second, weight)

def reference(block_input, cotangent, positions, query_weight, keyval_weight, output_weight, gateup_weight, down_weight, norm_gains, query_first, keyval_first, output_first, gateup_first, down_first, gains_first, query_second, keyval_second, output_second, gateup_second, down_second, gains_second):
    weights = (query_weight, keyval_weight, output_weight, gateup_weight, down_weight, norm_gains)
    group = math.gcd(SEQS, max(1, 4096 // LENGTH))
    rounds = SEQS // group

    def split(values):
        return values.reshape((rounds, group) + values.shape[1:])

    def accumulate(totals, item):
        input_rows, grad_out, places = item

        def apply(params, values):
            return forward(params, values, places)
        result, pullback = jax.vjp(apply, weights, input_rows)
        param_grads, inputs_grad = pullback(grad_out)
        return (jax.tree.map(jnp.add, totals, param_grads), (result, inputs_grad))
    zeros = tuple((jnp.zeros(weight.shape, jnp.float32) for weight in weights))
    grads, (outputs, inputs_grads) = lax.scan(accumulate, zeros, (split(block_input.astype(jnp.float32)), split(cotangent.astype(jnp.float32)), split(positions)))
    query_grad, keyval_grad, output_grad, gateup_grad, down_grad, gains_grad = grads
    query_mean, query_square, query_next = adamw(query_weight, query_grad, query_first, query_second, MATRIX_RATE, WEIGHT_DECAY)
    keyval_mean, keyval_square, keyval_next = adamw(keyval_weight, keyval_grad, keyval_first, keyval_second, MATRIX_RATE, WEIGHT_DECAY)
    output_mean, output_square, output_next = adamw(output_weight, output_grad, output_first, output_second, MATRIX_RATE, WEIGHT_DECAY)
    gateup_mean, gateup_square, gateup_next = adamw(gateup_weight, gateup_grad, gateup_first, gateup_second, MATRIX_RATE, WEIGHT_DECAY)
    down_mean, down_square, down_next = adamw(down_weight, down_grad, down_first, down_second, MATRIX_RATE, WEIGHT_DECAY)
    gains_mean, gains_square, gains_next = adamw(norm_gains, gains_grad, gains_first, gains_second, GAIN_RATE, 0.0)
    block_output = outputs.reshape(block_input.shape)
    input_grad = inputs_grads.reshape(block_input.shape)
    return (block_output, input_grad, query_grad, keyval_grad, output_grad, gateup_grad, down_grad, gains_grad, query_mean, keyval_mean, output_mean, gateup_mean, down_mean, gains_mean, query_square, keyval_square, output_square, gateup_square, down_square, gains_square, query_next, keyval_next, output_next, gateup_next, down_next, gains_next)
```

```python
import functools
import math

import jax
import jax.numpy as jnp
from jax import lax
from jax.experimental import pallas as pl
from jax.experimental.pallas import tpu as pltpu
from jax.sharding import PartitionSpec as P

HD = 64
STEP = 10

NORM_EPS = 1e-05
ROPE_BASE = 500000.0
BETA_ONE = 0.9
BETA_TWO = 0.95
ADAM_EPS = 1e-08
MATRIX_RATE = 0.05
GAIN_RATE = 0.6
WEIGHT_DECAY = 0.1
MASKED = -1e30

PAIR = 2
CHUNKS = 2

LOW = jnp.bfloat16
WIDE = jnp.float32
ROWS_BY_ROWS = (((1,), (1,)), ((), ()))
COLUMNS_BY_COLUMNS = (((0,), (0,)), ((), ()))


def dot(left, right, dims=(((1,), (0,)), ((), ()))):
    return lax.dot_general(left, right, dims, preferred_element_type=WIDE)


def swap(values, axis, mask):
    pairs = [(k, k ^ mask) for k in range(lax.axis_size(axis))]
    return lax.ppermute(values, axis, pairs)


def part(values, index, parts, dim):
    size = values.shape[dim] // parts
    return lax.dynamic_slice_in_dim(values, index * size, size, dim)


def join(mine, other, bit, dim):
    first = jnp.concatenate([mine, other], axis=dim)
    second = jnp.concatenate([other, mine], axis=dim)
    return jnp.where(bit == 0, first, second)


def angle_tables(positions):
    half_steps = jnp.arange(HD // 2, dtype=WIDE)
    frequency = jnp.exp(half_steps * (-2.0 / HD) * math.log(ROPE_BASE))
    angles = positions.astype(WIDE)[..., None] * frequency
    cosine = jnp.cos(angles)
    sine = jnp.sin(angles)
    return (
        jnp.concatenate([cosine, cosine], axis=-1)[..., None, :],
        jnp.concatenate([sine, sine], axis=-1)[..., None, :],
    )


def rotate(values, cosine, sine):
    middle_index = values.shape[-1] // 2
    turned = jnp.concatenate([-values[..., middle_index:], values[..., :middle_index]], axis=-1)
    return values * cosine + turned * sine


def rms_factor(values):
    return lax.rsqrt(jnp.mean(values * values, axis=-1, keepdims=True) + NORM_EPS)


def rms_backward(values, gain, grad):
    factor = rms_factor(values)
    scaled = grad * gain
    inner = jnp.mean(scaled * values, axis=-1, keepdims=True)
    grad_values = factor * scaled - values * (factor * factor * factor * inner)
    grad_gain = jnp.sum(grad * values * factor, axis=0)
    return grad_values, grad_gain


def attend_kernel(group, block, query_ref, key_ref, value_ref, mixed_ref, logsum_ref):
    length = query_ref.shape[1]
    keys = key_ref[0, 0]
    values = value_ref[0, 0]
    row_index = lax.broadcasted_iota(jnp.int32, (block, block), 0)
    column_index = lax.broadcasted_iota(jnp.int32, (block, block), 1)
    allowed = column_index <= row_index
    for head in range(group):
        columns = slice(head * HD, (head + 1) * HD)
        for start in range(0, length, block):
            rows = slice(start, start + block)
            query = query_ref[0, rows, columns] * HD ** (-0.5)
            last = jnp.where(allowed, dot(query, keys[rows], ROWS_BY_ROWS), MASKED)
            highest = jnp.max(last, axis=-1, keepdims=True)
            if start:
                early = dot(query, keys[:start], ROWS_BY_ROWS)
                highest = jnp.maximum(highest, jnp.max(early, axis=-1, keepdims=True))
                early = jnp.exp(early - highest)
            last = jnp.exp(last - highest)
            total = jnp.sum(last, axis=-1, keepdims=True)
            if start:
                total = total + jnp.sum(early, axis=-1, keepdims=True)
            share = 1.0 / total
            mixed = dot((last * share).astype(LOW), values[rows])
            if start:
                mixed = mixed + dot((early * share).astype(LOW), values[:start])
            mixed_ref[0, rows, columns] = mixed.astype(LOW)
            logsum_ref[0, 0, rows, head : head + 1] = highest + jnp.log(total)


def attend_back_kernel(
    group,
    block,
    query_ref,
    key_ref,
    value_ref,
    logsum_ref,
    grad_ref,
    query_grad_ref,
    key_grad_ref,
    value_grad_ref,
):
    length = query_ref.shape[1]
    keys = key_ref[0, 0]
    values = value_ref[0, 0]
    key_index = lax.broadcasted_iota(jnp.int32, (block, block), 0)
    query_index = lax.broadcasted_iota(jnp.int32, (block, block), 1)
    allowed = key_index <= query_index
    scale = HD ** (-0.5)
    key_grad_ref[...] = jnp.zeros_like(key_grad_ref)
    value_grad_ref[...] = jnp.zeros_like(value_grad_ref)
    for head in range(group):
        columns = slice(head * HD, (head + 1) * HD)
        for start in range(0, length, block):
            rows = slice(start, start + block)
            query = query_ref[0, rows, columns] * scale
            grad = grad_ref[0, rows, columns]
            logsum = logsum_ref[0, 0, head : head + 1, rows]
            spans = [(rows, True)]
            if start:
                spans.append((slice(0, start), False))
            probs, grad_probs = [], []
            for span, masked in spans:
                scores = dot(keys[span], query, ROWS_BY_ROWS)
                if masked:
                    scores = jnp.where(allowed, scores, MASKED)
                probs.append(jnp.exp(scores - logsum))
                grad_probs.append(dot(values[span], grad, ROWS_BY_ROWS))
            inner = sum(
                jnp.sum(one * two, axis=0, keepdims=True) for one, two in zip(probs, grad_probs)
            )
            query_grad = None
            for (span, _), one, two in zip(spans, probs, grad_probs):
                grad_scores = (one * (two - inner)).astype(LOW)
                piece = dot(grad_scores, keys[span], COLUMNS_BY_COLUMNS)
                query_grad = piece if query_grad is None else query_grad + piece
                key_grad_ref[0, 0, span] += dot(grad_scores, query)
                value_grad_ref[0, 0, span] += dot(one.astype(LOW), grad)
            query_grad_ref[0, rows, columns] = query_grad * scale


def attend(query, key, value):
    count, kv, length, _ = key.shape
    width = query.shape[2]
    group = width // (kv * HD)
    block = min(256, length)
    wide = pl.BlockSpec((1, length, group * HD), lambda s, j: (s, 0, j))
    narrow = pl.BlockSpec((1, 1, length, HD), lambda s, j: (s, j, 0, 0))
    sums = pl.BlockSpec((1, 1, length, group), lambda s, j: (s, j, 0, 0))
    work = count * kv * group * length * length
    return pl.pallas_call(
        functools.partial(attend_kernel, group, block),
        grid=(count, kv),
        in_specs=[wide, narrow, narrow],
        out_specs=[wide, sums],
        out_shape=[
            jax.ShapeDtypeStruct(query.shape, LOW),
            jax.ShapeDtypeStruct((count, kv, length, group), WIDE),
        ],
        compiler_params=pltpu.CompilerParams(vmem_limit_bytes=48 << 20),
        cost_estimate=pl.CostEstimate(
            flops=work * HD * 4, bytes_accessed=query.size * 8, transcendentals=work
        ),
    )(query, key, value)


def attend_back(query, key, value, logsum, grad):
    count, kv, length, _ = key.shape
    width = query.shape[2]
    group = width // (kv * HD)
    block = min(256, length)
    wide = pl.BlockSpec((1, length, group * HD), lambda s, j: (s, 0, j))
    narrow = pl.BlockSpec((1, 1, length, HD), lambda s, j: (s, j, 0, 0))
    sums = pl.BlockSpec((1, 1, group, length), lambda s, j: (s, j, 0, 0))
    work = count * kv * group * length * length
    return pl.pallas_call(
        functools.partial(attend_back_kernel, group, block),
        grid=(count, kv),
        in_specs=[wide, narrow, narrow, sums, wide],
        out_specs=[wide, narrow, narrow],
        out_shape=[
            jax.ShapeDtypeStruct(query.shape, WIDE),
            jax.ShapeDtypeStruct(key.shape, WIDE),
            jax.ShapeDtypeStruct(key.shape, WIDE),
        ],
        compiler_params=pltpu.CompilerParams(vmem_limit_bytes=48 << 20),
        cost_estimate=pl.CostEstimate(
            flops=work * HD * 10, bytes_accessed=query.size * 16, transcendentals=work
        ),
    )(query, key, value, jnp.swapaxes(logsum, 2, 3), grad)


def adamw(weight, grad, first, second, rate, decay):
    first = BETA_ONE * first + (1.0 - BETA_ONE) * grad
    second = BETA_TWO * second + (1.0 - BETA_TWO) * grad * grad
    fixed_first = first / (1.0 - BETA_ONE**STEP)
    fixed_second = second / (1.0 - BETA_TWO**STEP)
    weight = weight - rate * (fixed_first / (jnp.sqrt(fixed_second) + ADAM_EPS) + decay * weight)
    return (first, second, weight)


def gather_rows(pick):
    devices = lax.axis_size("dp")
    me = lax.axis_index("dp")
    blocks = {}
    for mask in range(0, devices, 2):
        block = pick(mask)
        blocks[mask] = swap(block, "dp", mask) if mask else block
    for mask in range(0, devices, 2):
        blocks[mask ^ 1] = swap(blocks[mask], "dp", 1)
    depth, width = blocks[0].shape
    full = jnp.zeros((devices * depth, width), blocks[0].dtype)
    for mask, block in blocks.items():
        full = lax.dynamic_update_slice_in_dim(full, block, (me ^ mask) * depth, 0)
    return full


def scatter_rows(rows_of):
    devices = lax.axis_size("dp")
    me = lax.axis_index("dp")
    sums = {}
    for mask in range(0, devices, 2):
        other = swap(rows_of(me ^ 1 ^ mask).astype(LOW), "dp", 1)
        sums[mask] = rows_of(me ^ mask).astype(WIDE) + other.astype(WIDE)
    terms = {0: sums[0]}
    for mask in range(2, devices, 2):
        terms[mask] = swap(sums[mask].astype(LOW), "dp", mask).astype(WIDE)
    return terms


def halve(partial, dim, axis, mask):
    bit = (lax.axis_index(axis) // mask) % 2
    sent = part(partial, 1 - bit, 2, dim).astype(LOW)
    return part(partial, bit, 2, dim).astype(WIDE) + swap(sent, axis, mask).astype(WIDE)


def double(values, dim, axis, mask):
    bit = (lax.axis_index(axis) // mask) % 2
    return join(values, swap(values, axis, mask), bit, dim)


def body(
    block_input,
    cotangent,
    positions,
    query_weight,
    keyval_weight,
    output_weight,
    gateup_weight,
    down_weight,
    norm_gains,
    query_first,
    keyval_first,
    output_first,
    gateup_first,
    down_first,
    gains_first,
    query_second,
    keyval_second,
    output_second,
    gateup_second,
    down_second,
    gains_second,
):
    count, length, width = block_input.shape
    rows = count * length
    depth = query_weight.shape[0]
    query_width = query_weight.shape[1]
    key_width = keyval_weight.shape[2]
    me = lax.axis_index("dp")
    pair_bit = (me // PAIR) % 2
    tensor_index = lax.axis_index("tensor")
    core, line = tensor_index % 2, tensor_index // 2

    def quarter(values, dim):
        return part(part(values, core, 2, dim), line, 2, dim)

    def reduce_tokens(partial):
        return halve(halve(partial, 0, "tensor", 1), 0, "tensor", 2)

    def spread_tokens(values):
        return double(double(values, 0, "tensor", 2), 0, "tensor", 1)

    def reduce_pair(partial):
        partial = halve(halve(partial, 1, "tensor", 1), 1, "tensor", 2)
        return halve(partial, 0, "dp", PAIR)[0]

    def spread_pair(values):
        both = double(values[None], 0, "dp", PAIR)
        return double(double(both, 1, "tensor", 2), 1, "tensor", 1)

    gains_full = norm_gains.astype(LOW)
    mask = 1
    while mask < lax.axis_size("dp"):
        gains_full = double(gains_full, 1, "dp", mask)
        mask *= 2
    gains_low = gains_full.astype(WIDE)

    proj_block = jnp.concatenate(
        [query_weight.astype(LOW), keyval_weight.reshape(depth, 2 * key_width).astype(LOW)], axis=1
    )
    proj_full = gather_rows(lambda m: proj_block)
    output_block = output_weight.astype(LOW)
    output_full = gather_rows(lambda m: output_block)

    half_width = down_weight.shape[1] // 2
    chunk_width = half_width // CHUNKS

    def hidden_block(chunk, m):
        start = (pair_bit ^ ((m // PAIR) % 2)) * half_width + chunk * chunk_width
        gateup = lax.dynamic_slice_in_dim(gateup_weight, start, chunk_width, 2)
        down = lax.dynamic_slice_in_dim(down_weight, start, chunk_width, 1)
        return jnp.concatenate(
            [gateup[:, 0].astype(LOW), gateup[:, 1].astype(LOW), down.astype(LOW)], axis=1
        )

    hidden_full = [
        gather_rows(functools.partial(hidden_block, chunk)) for chunk in range(CHUNKS)
    ]

    grad_out = cotangent.reshape(rows, width)
    other_out = spread_tokens(swap(quarter(grad_out, 0), "dp", PAIR))
    grad_both = join(grad_out, other_out, pair_bit, 0)

    input_rows = block_input.astype(WIDE).reshape(rows, width)
    normalized = (input_rows * rms_factor(input_rows) * gains_low[0]).astype(LOW)
    projected = dot(normalized, proj_full)
    heads, kv = query_width // HD, key_width // HD
    cosine, sine = angle_tables(positions.reshape(rows))
    query = rotate(projected[:, :query_width].reshape(rows, heads, HD), cosine, sine)
    query = query.astype(LOW).reshape(count, length, query_width)
    key_value = projected[:, query_width:].reshape(rows, 2, kv, HD)
    key = rotate(key_value[:, 0], cosine, sine).astype(LOW)
    key = key.reshape(count, length, kv, HD).swapaxes(1, 2)
    value = key_value[:, 1].astype(LOW).reshape(count, length, kv, HD).swapaxes(1, 2)
    mixed, logsum = attend(query, key, value)
    mixed_low = mixed.reshape(rows, query_width)
    branch = reduce_tokens(dot(mixed_low, output_full, ROWS_BY_ROWS))

    input_part = quarter(input_rows, 0)
    middle = input_part + branch
    normed_part = (middle * rms_factor(middle) * gains_low[1]).astype(LOW)
    normed_two = spread_pair(normed_part).reshape(2 * rows, width)

    hiddens, grad_gateups, hidden_terms = [], [], []
    for chunk in range(CHUNKS):
        gateup_full = hidden_full[chunk][:, : 2 * chunk_width]
        down_full = hidden_full[chunk][:, 2 * chunk_width :]
        gate_up = dot(normed_two, gateup_full)
        gate, upward = gate_up[:, :chunk_width], gate_up[:, chunk_width:]
        sigma = jax.nn.sigmoid(gate)
        hidden = (gate * sigma * upward).astype(LOW)
        grad_hidden = dot(grad_both, down_full)
        grad_gate = grad_hidden * upward * sigma * (1.0 + gate * (1.0 - sigma))
        grad_up = grad_hidden * gate * sigma
        grad_gateup = jnp.concatenate([grad_gate.astype(LOW), grad_up.astype(LOW)], axis=1)
        gateup_grad = dot(normed_two, grad_gateup, COLUMNS_BY_COLUMNS).astype(LOW)
        down_grad = dot(grad_both, hidden, COLUMNS_BY_COLUMNS).astype(LOW)

        def hidden_rows(owner, gateup_grad=gateup_grad, down_grad=down_grad):
            return jnp.concatenate(
                [
                    lax.dynamic_slice_in_dim(gateup_grad, owner * depth, depth, 0),
                    lax.dynamic_slice_in_dim(down_grad, owner * depth, depth, 0),
                ],
                axis=1,
            )

        hidden_terms.append(scatter_rows(hidden_rows))
        hiddens.append(hidden)
        grad_gateups.append(grad_gateup)

    partial_two = sum(
        dot(grad_gateups[chunk], hidden_full[chunk][:, : 2 * chunk_width], ROWS_BY_ROWS)
        for chunk in range(CHUNKS)
    )
    grad_normed_two = reduce_pair(partial_two.reshape(2, rows, width))
    partial_out = sum(
        dot(hiddens[chunk], hidden_full[chunk][:, 2 * chunk_width :], ROWS_BY_ROWS)
        for chunk in range(CHUNKS)
    )
    branch_two = reduce_pair(partial_out.reshape(2, rows, width))
    block_output = spread_tokens((middle + branch_two).astype(LOW)).astype(WIDE)

    grad_middle_part, gain_two = rms_backward(middle, gains_low[1], grad_normed_two)
    grad_middle = quarter(grad_out, 0).astype(WIDE) + grad_middle_part
    grad_middle_low = spread_tokens(grad_middle.astype(LOW))
    output_grad = dot(grad_middle_low, mixed_low, COLUMNS_BY_COLUMNS)
    grad_mixed = dot(grad_middle_low, output_full).astype(LOW)
    query_grads, key_grads, value_grads = attend_back(
        query, key, value, logsum, grad_mixed.reshape(count, length, query_width)
    )
    grad_query = rotate(query_grads.reshape(rows, heads, HD), cosine, -sine)
    grad_key = rotate(key_grads.swapaxes(1, 2).reshape(rows, kv, HD), cosine, -sine)
    grad_projected = jnp.concatenate(
        [
            grad_query.reshape(rows, query_width).astype(LOW),
            grad_key.reshape(rows, key_width).astype(LOW),
            value_grads.swapaxes(1, 2).reshape(rows, key_width).astype(LOW),
        ],
        axis=1,
    )
    partial_one = dot(grad_projected, proj_full, ROWS_BY_ROWS)
    proj_grad = dot(normalized, grad_projected, COLUMNS_BY_COLUMNS)
    grad_normed = reduce_tokens(partial_one)
    grad_input_part, gain_one = rms_backward(input_part, gains_low[0], grad_normed)
    input_grad = spread_tokens((grad_middle + grad_input_part).astype(LOW)).astype(WIDE)
    gains_sum = lax.psum(jnp.stack([gain_one, gain_two]), ("dp", "tensor"))
    gains_reduced = lax.dynamic_slice_in_dim(gains_sum, me * depth, depth, 1)

    def rows_of(grad):
        return lambda owner: lax.dynamic_slice_in_dim(grad, owner * depth, depth, 0)

    output_reduced = sum(scatter_rows(rows_of(output_grad)).values())
    proj_reduced = sum(scatter_rows(rows_of(proj_grad)).values())
    query_reduced = proj_reduced[:, :query_width]
    keyval_reduced = proj_reduced[:, query_width:].reshape(depth, 2, key_width)
    mine, other = [], []
    for terms in hidden_terms:
        mine.append(sum(term for m, term in terms.items() if not m & PAIR))
        other.append(sum(term for m, term in terms.items() if m & PAIR))

    def hidden_columns(index):
        columns = slice(index * chunk_width, (index + 1) * chunk_width)
        return join(
            jnp.concatenate([terms[:, columns] for terms in mine], axis=1),
            jnp.concatenate([terms[:, columns] for terms in other], axis=1),
            pair_bit,
            1,
        )

    gateup_reduced = jnp.stack([hidden_columns(0), hidden_columns(1)], axis=1)
    down_reduced = hidden_columns(2)

    query_mean, query_square, query_next = adamw(
        query_weight, query_reduced, query_first, query_second, MATRIX_RATE, WEIGHT_DECAY
    )
    keyval_mean, keyval_square, keyval_next = adamw(
        keyval_weight, keyval_reduced, keyval_first, keyval_second, MATRIX_RATE, WEIGHT_DECAY
    )
    output_mean, output_square, output_next = adamw(
        output_weight, output_reduced, output_first, output_second, MATRIX_RATE, WEIGHT_DECAY
    )
    gateup_mean, gateup_square, gateup_next = adamw(
        gateup_weight, gateup_reduced, gateup_first, gateup_second, MATRIX_RATE, WEIGHT_DECAY
    )
    down_mean, down_square, down_next = adamw(
        down_weight, down_reduced, down_first, down_second, MATRIX_RATE, WEIGHT_DECAY
    )
    gains_mean, gains_square, gains_next = adamw(
        norm_gains, gains_reduced, gains_first, gains_second, GAIN_RATE, 0.0
    )
    return (
        block_output.reshape(count, length, width),
        input_grad.reshape(count, length, width),
        query_reduced,
        keyval_reduced,
        output_reduced,
        gateup_reduced,
        down_reduced,
        gains_reduced,
        query_mean,
        keyval_mean,
        output_mean,
        gateup_mean,
        down_mean,
        gains_mean,
        query_square,
        keyval_square,
        output_square,
        gateup_square,
        down_square,
        gains_square,
        query_next,
        keyval_next,
        output_next,
        gateup_next,
        down_next,
        gains_next,
    )


def solution(mesh):
    in_specs = (
        P("dp", None, None),
        P("dp", None, None),
        P("dp", None),
        P("dp", "tensor"),
        P("dp", None, "tensor"),
        P("dp", "tensor"),
        P("dp", None, "tensor"),
        P("dp", "tensor"),
        P(None, "dp"),
        P("dp", "tensor"),
        P("dp", None, "tensor"),
        P("dp", "tensor"),
        P("dp", None, "tensor"),
        P("dp", "tensor"),
        P(None, "dp"),
        P("dp", "tensor"),
        P("dp", None, "tensor"),
        P("dp", "tensor"),
        P("dp", None, "tensor"),
        P("dp", "tensor"),
        P(None, "dp"),
    )
    out_specs = (
        P("dp", None, None),
        P("dp", None, None),
        P("dp", "tensor"),
        P("dp", None, "tensor"),
        P("dp", "tensor"),
        P("dp", None, "tensor"),
        P("dp", "tensor"),
        P(None, "dp"),
        P("dp", "tensor"),
        P("dp", None, "tensor"),
        P("dp", "tensor"),
        P("dp", None, "tensor"),
        P("dp", "tensor"),
        P(None, "dp"),
        P("dp", "tensor"),
        P("dp", None, "tensor"),
        P("dp", "tensor"),
        P("dp", None, "tensor"),
        P("dp", "tensor"),
        P(None, "dp"),
        P("dp", "tensor"),
        P("dp", None, "tensor"),
        P("dp", "tensor"),
        P("dp", None, "tensor"),
        P("dp", "tensor"),
        P(None, "dp"),
    )
    return jax.shard_map(body, mesh=mesh, in_specs=in_specs, out_specs=out_specs, check_vma=False)
```

```python
import functools
import math

import jax
import jax.numpy as jnp
from jax import lax
from jax.experimental import pallas as pl
from jax.experimental.pallas import tpu as pltpu
from jax.sharding import PartitionSpec as P

HD = 64
STEP = 10

NORM_EPS = 1e-05
ROPE_BASE = 500000.0
BETA_ONE = 0.9
BETA_TWO = 0.95
ADAM_EPS = 1e-08
MATRIX_RATE = 0.05
GAIN_RATE = 0.6
WEIGHT_DECAY = 0.1
MASKED = -1e30

PAIR = 2
CHUNKS = 4

LOW = jnp.bfloat16
WIDE = jnp.float32
ROWS_BY_ROWS = (((1,), (1,)), ((), ()))
COLUMNS_BY_COLUMNS = (((0,), (0,)), ((), ()))


def dot(left, right, dims=(((1,), (0,)), ((), ()))):
    return lax.dot_general(left, right, dims, preferred_element_type=WIDE)


def swap(values, axis, mask):
    pairs = [(k, k ^ mask) for k in range(lax.axis_size(axis))]
    return lax.ppermute(values, axis, pairs)


def part(values, index, parts, dim):
    size = values.shape[dim] // parts
    return lax.dynamic_slice_in_dim(values, index * size, size, dim)


def join(mine, other, bit, dim):
    first = jnp.concatenate([mine, other], axis=dim)
    second = jnp.concatenate([other, mine], axis=dim)
    return jnp.where(bit == 0, first, second)


def angle_tables(positions):
    half_steps = jnp.arange(HD // 2, dtype=WIDE)
    frequency = jnp.exp(half_steps * (-2.0 / HD) * math.log(ROPE_BASE))
    angles = positions.astype(WIDE)[..., None] * frequency
    cosine = jnp.cos(angles)
    sine = jnp.sin(angles)
    return (
        jnp.concatenate([cosine, cosine], axis=-1)[..., None, :],
        jnp.concatenate([sine, sine], axis=-1)[..., None, :],
    )


def rotate(values, cosine, sine):
    middle_index = values.shape[-1] // 2
    turned = jnp.concatenate([-values[..., middle_index:], values[..., :middle_index]], axis=-1)
    return values * cosine + turned * sine


def rms_factor(values):
    return lax.rsqrt(jnp.mean(values * values, axis=-1, keepdims=True) + NORM_EPS)


def rms_backward(values, gain, grad):
    factor = rms_factor(values)
    scaled = grad * gain
    inner = jnp.mean(scaled * values, axis=-1, keepdims=True)
    grad_values = factor * scaled - values * (factor * factor * factor * inner)
    grad_gain = jnp.sum(grad * values * factor, axis=0)
    return grad_values, grad_gain


def attend_back_kernel(
    group,
    block,
    query_ref,
    key_ref,
    value_ref,
    logsum_ref,
    grad_ref,
    query_grad_ref,
    key_grad_ref,
    value_grad_ref,
):
    length = query_ref.shape[1]
    keys = key_ref[0, 0]
    values = value_ref[0, 0]
    key_index = lax.broadcasted_iota(jnp.int32, (block, block), 0)
    query_index = lax.broadcasted_iota(jnp.int32, (block, block), 1)
    allowed = key_index <= query_index
    scale = HD ** (-0.5)
    key_grad_ref[...] = jnp.zeros_like(key_grad_ref)
    value_grad_ref[...] = jnp.zeros_like(value_grad_ref)
    for head in range(group):
        columns = slice(head * HD, (head + 1) * HD)
        for start in range(0, length, block):
            rows = slice(start, start + block)
            query = query_ref[0, rows, columns] * scale
            grad = grad_ref[0, rows, columns]
            logsum = logsum_ref[0, 0, head : head + 1, rows]
            spans = [(rows, True)]
            if start:
                spans.append((slice(0, start), False))
            probs, grad_probs = [], []
            for span, masked in spans:
                scores = dot(keys[span], query, ROWS_BY_ROWS)
                if masked:
                    scores = jnp.where(allowed, scores, MASKED)
                probs.append(jnp.exp(scores - logsum))
                grad_probs.append(dot(values[span], grad, ROWS_BY_ROWS))
            inner = sum(
                jnp.sum(one * two, axis=0, keepdims=True) for one, two in zip(probs, grad_probs)
            )
            query_grad = None
            for (span, _), one, two in zip(spans, probs, grad_probs):
                grad_scores = (one * (two - inner)).astype(LOW)
                piece = dot(grad_scores, keys[span], COLUMNS_BY_COLUMNS)
                query_grad = piece if query_grad is None else query_grad + piece
                key_grad_ref[0, 0, span] += dot(grad_scores, query)
                value_grad_ref[0, 0, span] += dot(one.astype(LOW), grad)
            query_grad_ref[0, rows, columns] = query_grad * scale


def attend_back(query, key, value, logsum, grad):
    count, kv, length, _ = key.shape
    width = query.shape[2]
    group = width // (kv * HD)
    block = min(256, length)
    wide = pl.BlockSpec((1, length, group * HD), lambda s, j: (s, 0, j))
    narrow = pl.BlockSpec((1, 1, length, HD), lambda s, j: (s, j, 0, 0))
    sums = pl.BlockSpec((1, 1, group, length), lambda s, j: (s, j, 0, 0))
    work = count * kv * group * length * length
    return pl.pallas_call(
        functools.partial(attend_back_kernel, group, block),
        grid=(count, kv),
        in_specs=[wide, narrow, narrow, sums, wide],
        out_specs=[wide, narrow, narrow],
        out_shape=[
            jax.ShapeDtypeStruct(query.shape, WIDE),
            jax.ShapeDtypeStruct(key.shape, WIDE),
            jax.ShapeDtypeStruct(key.shape, WIDE),
        ],
        compiler_params=pltpu.CompilerParams(vmem_limit_bytes=48 << 20),
        cost_estimate=pl.CostEstimate(
            flops=work * HD * 10, bytes_accessed=query.size * 16, transcendentals=work
        ),
    )(query, key, value, jnp.swapaxes(logsum, 2, 3), grad)


def attend_group(j, group, block, count, length, query_ref, key_ref, value_ref, mixed_ref, logsum_ref):
    row_index = lax.broadcasted_iota(jnp.int32, (block, block), 0)
    column_index = lax.broadcasted_iota(jnp.int32, (block, block), 1)
    allowed = column_index <= row_index
    for sequence in range(count):
        base = sequence * length
        for head in range(group):
            columns = slice((j * group + head) * HD, (j * group + head + 1) * HD)
            for start in range(base, base + length, block):
                rows = slice(start, start + block)
                before = slice(base, start)
                query = query_ref[rows, columns] * HD ** (-0.5)
                last = jnp.where(allowed, dot(query, key_ref[j, rows], ROWS_BY_ROWS), MASKED)
                highest = jnp.max(last, axis=-1, keepdims=True)
                if start > base:
                    early = dot(query, key_ref[j, before], ROWS_BY_ROWS)
                    highest = jnp.maximum(highest, jnp.max(early, axis=-1, keepdims=True))
                    early = jnp.exp(early - highest)
                last = jnp.exp(last - highest)
                total = jnp.sum(last, axis=-1, keepdims=True)
                if start > base:
                    total = total + jnp.sum(early, axis=-1, keepdims=True)
                share = 1.0 / total
                mixed = dot((last * share).astype(LOW), value_ref[j, rows])
                if start > base:
                    mixed = mixed + dot((early * share).astype(LOW), value_ref[j, before])
                mixed_ref[rows, columns] = mixed.astype(LOW)
                logsum_ref[j, rows, head : head + 1] = highest + jnp.log(total)


MESH = pl.DeviceIdType.MESH
MEGABYTE = 1 << 20


def flip(index, mask):
    bit = 1
    while bit <= mask:
        if mask & bit:
            index = index + bit - 2 * bit * lax.rem(lax.div(index, bit), 2)
        bit *= 2
    return index


def remote(source, target, sems, axis, mask):
    return pltpu.make_async_remote_copy(
        src_ref=source,
        dst_ref=target,
        send_sem=sems[0],
        recv_sem=sems[1],
        device_id={axis: flip(lax.axis_index(axis), mask)},
        device_id_type=MESH,
    )


def greet(partners):
    barrier = pltpu.get_barrier_semaphore()
    for axis, mask in partners:
        pl.semaphore_signal(
            barrier,
            inc=1,
            device_id={axis: flip(lax.axis_index(axis), mask)},
            device_id_type=MESH,
        )
    pl.semaphore_wait(barrier, len(partners))


class Gather:
    def __init__(self, masks, source, place, sems):
        self.masks, self.source, self.place, self.sems = masks, source, place, sems
        self.me = lax.axis_index("dp")
        self.started = []

    def sem(self, phase, mask):
        send, recv = self.sems
        return send.at[phase, mask // 2], recv.at[phase, mask // 2]

    def start(self):
        for mask in self.masks[1:]:
            copy = remote(
                self.source(mask), self.place(self.me), self.sem(0, mask), "dp", mask
            )
            copy.start()
            self.started.append(copy)

    def start_own(self):
        copy = remote(self.source(0), self.place(self.me), self.sem(1, 0), "dp", 1)
        copy.start()
        self.started.append(copy)

    def forward(self, mask):
        here = self.place(flip(self.me, mask))
        remote(here, here, self.sem(0, mask), "dp", mask).wait_recv()
        copy = remote(here, here, self.sem(1, mask), "dp", 1)
        copy.start()
        self.started.append(copy)

    def arrive(self, mask):
        here = self.place(flip(self.me, mask ^ 1))
        remote(here, here, self.sem(1, mask), "dp", 1).wait_recv()

    def drain(self):
        for copy in self.started:
            copy.wait_send()


def rotated(values, cosine, sine, first):
    width = values.shape[1]
    turned = jnp.where(
        first, pltpu.roll(values, width - HD // 2, 1), pltpu.roll(values, HD // 2, 1)
    )
    return values * cosine + turned * sine


def first_kernel(
    sizes,
    x_ref,
    cot_ref,
    proj_ref,
    out_ref,
    hidden_ref,
    gains_ref,
    cosine_ref,
    sine_ref,
    normalized_ref,
    proj_full,
    out_full,
    gains_full,
    query_ref,
    key_ref,
    value_ref,
    mixed_ref,
    logsum_ref,
    middle_ref,
    hidden_full,
    other_cot,
    both_ref,
    core_out,
    core_in,
    held,
    line_out,
    line_in,
    normed,
    gains_slots,
    gather_send,
    gather_recv,
    hidden_send,
    hidden_recv,
    token_send,
    token_recv,
    local_sem,
):
    count, length = sizes
    rows, width = x_ref.shape
    devices = lax.axis_size("dp")
    masks = list(range(0, devices, 2))
    me = lax.axis_index("dp")
    tensor = lax.axis_index("tensor")
    core, line = lax.rem(tensor, 2), lax.div(tensor, 2)
    pair_bit = lax.rem(lax.div(me, PAIR), 2)
    depth = proj_ref.shape[0]
    chunks = hidden_ref.shape[1]
    half, piece = rows // 2, rows // 4
    greet([("dp", mask) for mask in masks[1:] + [1]] + [("tensor", 1), ("tensor", 2)])

    def block_rows(ref):
        return lambda owner: ref.at[pl.ds(pl.multiple_of(owner * depth, depth), depth)]

    def pair_half(mask):
        return pair_bit if not mask & PAIR else 1 - pair_bit

    gains = Gather(
        masks,
        lambda mask: gains_ref,
        lambda owner: gains_slots.at[owner],
        (gather_send.at[0], gather_recv.at[0]),
    )
    proj = Gather(
        masks,
        lambda mask: proj_ref,
        block_rows(proj_full),
        (gather_send.at[1], gather_recv.at[1]),
    )
    out = Gather(
        masks, lambda mask: out_ref, block_rows(out_full), (gather_send.at[2], gather_recv.at[2])
    )
    hidden = [
        Gather(
            masks,
            lambda mask, chunk=chunk: hidden_ref.at[pair_half(mask), chunk],
            block_rows(hidden_full.at[chunk]),
            (hidden_send.at[chunk], hidden_recv.at[chunk]),
        )
        for chunk in range(chunks)
    ]
    tokens = []

    def send_tokens(source, target, index, axis, mask):
        copy = remote(source, target, (token_send.at[index], token_recv.at[index]), axis, mask)
        copy.start()
        tokens.append(copy)

    def wait_tokens(target, index, axis, mask):
        remote(
            target, target, (token_send.at[index], token_recv.at[index]), axis, mask
        ).wait_recv()

    def piece_rows(ref, core_at, line_at):
        return ref.at[pl.ds(pl.multiple_of(core_at * half + line_at * piece, piece), piece)]

    def half_rows(ref, core_at):
        return ref.at[pl.ds(pl.multiple_of(core_at * half, half), half)]

    gains.start()
    gains.start_own()
    proj.start()
    proj.start_own()
    here = piece_rows(other_cot, core, line)
    send_tokens(piece_rows(cot_ref, core, line), here, 0, "dp", PAIR)
    out.start()
    out.start_own()
    hidden[0].start()
    hidden[0].start_own()
    own = [
        pltpu.make_async_copy(gains_ref, gains.place(me), local_sem.at[0]),
        pltpu.make_async_copy(proj_ref, proj.place(me), local_sem.at[1]),
        pltpu.make_async_copy(out_ref, out.place(me), local_sem.at[2]),
    ]
    for copy in own:
        copy.start()
    own_hidden = [
        pltpu.make_async_copy(gather.source(0), gather.place(me), local_sem.at[3 + chunk])
        for chunk, gather in enumerate(hidden)
    ]
    for copy in own_hidden:
        copy.start()

    def pump(chunk):
        for mask in masks[1:]:
            hidden[chunk].forward(mask)
        if chunk + 2 < chunks:
            hidden[chunk + 2].start()
            hidden[chunk + 2].start_own()

    for mask in masks[1:]:
        gains.forward(mask)
    for mask in masks:
        gains.arrive(mask)
    for copy in own:
        copy.wait()
    gains_full[...] = jnp.concatenate([gains_slots[j] for j in range(devices)], axis=1)
    tile = rows // 4

    def norm_tile(index, carry):
        at = pl.ds(pl.multiple_of(index * tile, tile), tile)
        values = x_ref[at].astype(WIDE)
        normalized_ref[at] = (values * rms_factor(values) * gains_full[0:1]).astype(LOW)
        return carry

    lax.fori_loop(0, 4, norm_tile, 0)
    for mask in masks[1:]:
        proj.forward(mask)
    if chunks > 1:
        hidden[1].start()
        hidden[1].start_own()
    for mask in masks:
        proj.arrive(mask)
    query_width = query_ref.shape[1]
    kv = key_ref.shape[0]
    group = query_width // (kv * HD)

    def project_tile(index, carry):
        at = pl.ds(pl.multiple_of(index * tile, tile), tile)
        pre = dot(normalized_ref[at], proj_full[...])
        cosine, sine = cosine_ref[at], sine_ref[at]

        def turn(values):
            times = values.shape[1] // cosine.shape[1]
            lanes = lax.broadcasted_iota(jnp.int32, values.shape, 1)
            return rotated(
                values,
                jnp.concatenate([cosine] * times, axis=1),
                jnp.concatenate([sine] * times, axis=1),
                lax.rem(lanes, HD) < HD // 2,
            ).astype(LOW)

        query_ref[at] = turn(pre[:, :query_width])
        keys = turn(pre[:, query_width : query_width + kv * HD])
        values = pre[:, query_width + kv * HD :].astype(LOW)
        for j in range(kv):
            key_ref[j, at] = keys[:, j * HD : (j + 1) * HD]
            value_ref[j, at] = values[:, j * HD : (j + 1) * HD]
        return carry

    lax.fori_loop(0, 4, project_tile, 0)

    wait_tokens(here, 0, "dp", PAIR)
    send_tokens(here, here, 1, "tensor", 2)
    send_tokens(here, here, 2, "tensor", 1)

    block = min(256, length)
    for j in range(kv):
        attend_group(
            j, group, block, count, length, query_ref, key_ref, value_ref, mixed_ref, logsum_ref
        )
        if j == 0:
            for mask in masks[1:]:
                out.forward(mask)

    there = piece_rows(other_cot, core, 1 - line)
    wait_tokens(there, 1, "tensor", 2)
    send_tokens(there, there, 3, "tensor", 1)

    for mask in masks:
        out.arrive(mask)
    strips = core_out.shape[0]
    strip = width // strips
    for s in range(strips):
        weight = out_full[s * strip : (s + 1) * strip]
        far = mixed_ref[pl.ds(pl.multiple_of((1 - core) * half, half), half)]
        core_out[s] = dot(far, weight, ROWS_BY_ROWS).astype(LOW)
        send_tokens(core_out.at[s], core_in.at[s], 8 + s, "tensor", 1)
    for s in range(strips):
        weight = out_full[s * strip : (s + 1) * strip]
        near = mixed_ref[pl.ds(pl.multiple_of(core * half, half), half)]
        held[s] = dot(near, weight, ROWS_BY_ROWS)
        wait_tokens(core_in.at[s], 8 + s, "tensor", 1)
        at = pl.ds(pl.multiple_of((1 - line) * piece, piece), piece)
        line_out[s] = (held[s, at] + core_in[s, at].astype(WIDE)).astype(LOW)
        send_tokens(line_out.at[s], line_in.at[s], 8 + strips + s, "tensor", 2)
    pump(0)
    at = pl.ds(pl.multiple_of(line * piece, piece), piece)
    own_rows = pl.ds(pl.multiple_of(core * half + line * piece, piece), piece)
    for s in range(strips):
        wait_tokens(line_in.at[s], 8 + strips + s, "tensor", 2)
        columns = slice(s * strip, (s + 1) * strip)
        middle_ref[:, columns] = (
            x_ref[own_rows, columns].astype(WIDE)
            + held[s, at]
            + core_in[s, at].astype(WIDE)
            + line_in[s].astype(WIDE)
        )
    middle = middle_ref[...]
    normed[...] = (middle * rms_factor(middle) * gains_full[1:2]).astype(LOW)

    near, far = both_ref.at[0], both_ref.at[1]
    place = piece_rows(near, core, line)
    send_tokens(normed, piece_rows(far, core, line), 4, "dp", PAIR)
    send_tokens(normed, place, 5, "tensor", 2)
    send_tokens(normed, place, 6, "tensor", 1)
    last = pltpu.make_async_copy(normed, place, local_sem.at[3 + chunks])
    last.start()
    place = piece_rows(near, core, 1 - line)
    wait_tokens(place, 5, "tensor", 2)
    send_tokens(place, place, 7, "tensor", 1)
    if chunks > 1:
        pump(1)
    base = 8 + 2 * strips
    place = piece_rows(far, core, line)
    wait_tokens(place, 4, "dp", PAIR)
    send_tokens(place, place, base, "tensor", 2)
    send_tokens(place, place, base + 1, "tensor", 1)
    for chunk in range(2, chunks):
        pump(chunk)
        if chunk == 2:
            place = piece_rows(far, core, 1 - line)
            wait_tokens(place, base, "tensor", 2)
            send_tokens(place, place, base + 2, "tensor", 1)
    if chunks < 3:
        place = piece_rows(far, core, 1 - line)
        wait_tokens(place, base, "tensor", 2)
        send_tokens(place, place, base + 2, "tensor", 1)

    wait_tokens(piece_rows(other_cot, 1 - core, line), 2, "tensor", 1)
    wait_tokens(piece_rows(other_cot, 1 - core, 1 - line), 3, "tensor", 1)
    wait_tokens(piece_rows(near, 1 - core, line), 6, "tensor", 1)
    wait_tokens(piece_rows(near, 1 - core, 1 - line), 7, "tensor", 1)
    wait_tokens(piece_rows(far, 1 - core, line), base + 1, "tensor", 1)
    wait_tokens(piece_rows(far, 1 - core, 1 - line), base + 2, "tensor", 1)
    for gather in hidden:
        for mask in masks:
            gather.arrive(mask)
    for copy in own_hidden:
        copy.wait()
    last.wait()
    for gather in [gains, proj, out] + hidden:
        gather.drain()
    for copy in tokens:
        copy.wait_send()


def first_half(x, cot, proj, out, hidden, gains, cosine, sine, kv, count):
    rows, width = x.shape
    devices = lax.axis_size("dp")
    spans = devices // 2
    depth = proj.shape[0]
    chunks = hidden.shape[1]
    query_width = out.shape[1]
    group = query_width // (kv * HD)
    half, piece = rows // 2, rows // 4
    strips = 4
    strip = width // strips
    vmem = pl.BlockSpec(memory_space=pltpu.VMEM)
    anywhere = pl.BlockSpec(memory_space=pl.ANY)
    shape = jax.ShapeDtypeStruct
    n_tokens = 8 + 2 * strips + 3
    return pl.pallas_call(
        functools.partial(first_kernel, (count, rows // count)),
        in_specs=[vmem, anywhere, vmem, vmem, anywhere, vmem, vmem, vmem],
        out_specs=[vmem] * 10 + [anywhere] * 3,
        out_shape=[
            shape((rows, width), LOW),
            shape((devices * depth, proj.shape[1]), LOW),
            shape((devices * depth, query_width), LOW),
            shape((gains.shape[0], width), WIDE),
            shape((rows, query_width), LOW),
            shape((kv, rows, HD), LOW),
            shape((kv, rows, HD), LOW),
            shape((rows, query_width), LOW),
            shape((kv, rows, group), WIDE),
            shape((piece, width), WIDE),
            shape((chunks, devices * depth, hidden.shape[3]), LOW),
            shape((rows, width), LOW),
            shape((2, rows, width), LOW),
        ],
        scratch_shapes=[
            pltpu.VMEM((strips, half, strip), LOW),
            pltpu.VMEM((strips, half, strip), LOW),
            pltpu.VMEM((strips, half, strip), WIDE),
            pltpu.VMEM((strips, piece, strip), LOW),
            pltpu.VMEM((strips, piece, strip), LOW),
            pltpu.VMEM((piece, width), LOW),
            pltpu.VMEM((devices,) + gains.shape, WIDE),
            pltpu.SemaphoreType.DMA((3, 2, spans)),
            pltpu.SemaphoreType.DMA((3, 2, spans)),
            pltpu.SemaphoreType.DMA((chunks, 2, spans)),
            pltpu.SemaphoreType.DMA((chunks, 2, spans)),
            pltpu.SemaphoreType.DMA((n_tokens,)),
            pltpu.SemaphoreType.DMA((n_tokens,)),
            pltpu.SemaphoreType.DMA((4 + chunks,)),
        ],
        compiler_params=pltpu.CompilerParams(
            collective_id=0, has_side_effects=True, vmem_limit_bytes=56 * MEGABYTE
        ),
        name="gather_and_attend",
    )(x, cot, proj, out, hidden, gains, cosine, sine)


def adamw(weight, grad, first, second, rate, decay):
    first = BETA_ONE * first + (1.0 - BETA_ONE) * grad
    second = BETA_TWO * second + (1.0 - BETA_TWO) * grad * grad
    fixed_first = first / (1.0 - BETA_ONE**STEP)
    fixed_second = second / (1.0 - BETA_TWO**STEP)
    weight = weight - rate * (fixed_first / (jnp.sqrt(fixed_second) + ADAM_EPS) + decay * weight)
    return (first, second, weight)


def scatter_rows(rows_of):
    devices = lax.axis_size("dp")
    me = lax.axis_index("dp")
    sums = {}
    for mask in range(0, devices, 2):
        other = swap(rows_of(me ^ 1 ^ mask).astype(LOW), "dp", 1)
        sums[mask] = rows_of(me ^ mask).astype(WIDE) + other.astype(WIDE)
    terms = {0: sums[0]}
    for mask in range(2, devices, 2):
        terms[mask] = swap(sums[mask].astype(LOW), "dp", mask).astype(WIDE)
    return terms


def halve(partial, dim, axis, mask):
    bit = (lax.axis_index(axis) // mask) % 2
    sent = part(partial, 1 - bit, 2, dim).astype(LOW)
    return part(partial, bit, 2, dim).astype(WIDE) + swap(sent, axis, mask).astype(WIDE)


def double(values, dim, axis, mask):
    bit = (lax.axis_index(axis) // mask) % 2
    return join(values, swap(values, axis, mask), bit, dim)


def body(
    block_input,
    cotangent,
    positions,
    query_weight,
    keyval_weight,
    output_weight,
    gateup_weight,
    down_weight,
    norm_gains,
    query_first,
    keyval_first,
    output_first,
    gateup_first,
    down_first,
    gains_first,
    query_second,
    keyval_second,
    output_second,
    gateup_second,
    down_second,
    gains_second,
):
    count, length, width = block_input.shape
    rows = count * length
    depth = query_weight.shape[0]
    query_width = query_weight.shape[1]
    key_width = keyval_weight.shape[2]
    me = lax.axis_index("dp")
    pair_bit = (me // PAIR) % 2
    tensor_index = lax.axis_index("tensor")
    core, line = tensor_index % 2, tensor_index // 2

    def quarter(values, dim):
        return part(part(values, core, 2, dim), line, 2, dim)

    def reduce_tokens(partial):
        return halve(halve(partial, 0, "tensor", 1), 0, "tensor", 2)

    def spread_tokens(values):
        return double(double(values, 0, "tensor", 2), 0, "tensor", 1)

    def reduce_pair(partial):
        partial = halve(halve(partial, 1, "tensor", 1), 1, "tensor", 2)
        other = swap(partial[1].astype(LOW), "dp", PAIR)
        return partial[0] + other.astype(WIDE)

    proj_block = jnp.concatenate(
        [query_weight.astype(LOW), keyval_weight.reshape(depth, 2 * key_width).astype(LOW)], axis=1
    )
    half_width = down_weight.shape[1] // 2
    chunk_width = half_width // CHUNKS
    hidden_block = jnp.concatenate(
        [
            part[:, None].reshape(depth, 2, CHUNKS, chunk_width)
            for part in (gateup_weight[:, 0], gateup_weight[:, 1], down_weight)
        ],
        axis=3,
    )
    hidden_block = hidden_block.astype(LOW).transpose(1, 2, 0, 3)
    gains_block = jnp.pad(norm_gains.astype(LOW).astype(WIDE), ((0, 6), (0, 0)))
    grad_out = cotangent.reshape(rows, width)
    heads, kv = query_width // HD, key_width // HD
    cosine, sine = angle_tables(positions.reshape(rows))
    signs = jnp.where(jnp.arange(HD) < HD // 2, -1.0, 1.0).astype(WIDE)
    (
        normalized,
        proj_full,
        output_full,
        gains_low,
        query,
        key,
        value,
        mixed_low,
        logsum,
        middle,
        hidden_full,
        other_out,
        normed_two,
    ) = first_half(
        block_input.reshape(rows, width),
        grad_out,
        proj_block,
        output_weight.astype(LOW),
        hidden_block,
        gains_block,
        jnp.tile(cosine[:, 0], (1, 2)),
        jnp.tile(sine[:, 0] * signs, (1, 2)),
        kv,
        count,
    )
    input_part = quarter(block_input.reshape(rows, width), 0).astype(WIDE)
    normed_two = normed_two.reshape(2 * rows, width)
    grad_both = jnp.concatenate([grad_out, other_out], axis=0)

    hiddens, grad_gateups, hidden_terms = [], [], []
    for chunk in range(CHUNKS):
        gateup_full = hidden_full[chunk][:, : 2 * chunk_width]
        down_full = hidden_full[chunk][:, 2 * chunk_width :]
        gate_up = dot(normed_two, gateup_full)
        gate, upward = gate_up[:, :chunk_width], gate_up[:, chunk_width:]
        sigma = jax.nn.sigmoid(gate)
        hidden = (gate * sigma * upward).astype(LOW)
        grad_hidden = dot(grad_both, down_full)
        grad_gate = grad_hidden * upward * sigma * (1.0 + gate * (1.0 - sigma))
        grad_up = grad_hidden * gate * sigma
        grad_gateup = jnp.concatenate([grad_gate.astype(LOW), grad_up.astype(LOW)], axis=1)
        gateup_grad = dot(normed_two, grad_gateup, COLUMNS_BY_COLUMNS).astype(LOW)
        down_grad = dot(grad_both, hidden, COLUMNS_BY_COLUMNS).astype(LOW)

        def hidden_rows(owner, gateup_grad=gateup_grad, down_grad=down_grad):
            return jnp.concatenate(
                [
                    lax.dynamic_slice_in_dim(gateup_grad, owner * depth, depth, 0),
                    lax.dynamic_slice_in_dim(down_grad, owner * depth, depth, 0),
                ],
                axis=1,
            )

        hidden_terms.append(scatter_rows(hidden_rows))
        hiddens.append(hidden)
        grad_gateups.append(grad_gateup)

    partial_two = sum(
        dot(grad_gateups[chunk], hidden_full[chunk][:, : 2 * chunk_width], ROWS_BY_ROWS)
        for chunk in range(CHUNKS)
    )
    grad_normed_two = reduce_pair(partial_two.reshape(2, rows, width))
    partial_out = sum(
        dot(hiddens[chunk], hidden_full[chunk][:, 2 * chunk_width :], ROWS_BY_ROWS)
        for chunk in range(CHUNKS)
    )
    branch_two = reduce_pair(partial_out.reshape(2, rows, width))
    block_output = spread_tokens((middle + branch_two).astype(LOW)).astype(WIDE)

    grad_middle_part, gain_two = rms_backward(middle, gains_low[1], grad_normed_two)
    grad_middle = quarter(grad_out, 0).astype(WIDE) + grad_middle_part
    grad_middle_low = spread_tokens(grad_middle.astype(LOW))
    output_grad = dot(grad_middle_low, mixed_low, COLUMNS_BY_COLUMNS)
    grad_mixed = dot(grad_middle_low, output_full).astype(LOW)
    def by_sequence(values):
        return values.reshape(kv, count, length, values.shape[-1]).swapaxes(0, 1)

    query_grads, key_grads, value_grads = attend_back(
        query.reshape(count, length, query_width),
        by_sequence(key),
        by_sequence(value),
        by_sequence(logsum),
        grad_mixed.reshape(count, length, query_width),
    )
    grad_query = rotate(query_grads.reshape(rows, heads, HD), cosine, -sine)
    grad_key = rotate(key_grads.swapaxes(1, 2).reshape(rows, kv, HD), cosine, -sine)
    grad_projected = jnp.concatenate(
        [
            grad_query.reshape(rows, query_width).astype(LOW),
            grad_key.reshape(rows, key_width).astype(LOW),
            value_grads.swapaxes(1, 2).reshape(rows, key_width).astype(LOW),
        ],
        axis=1,
    )
    partial_one = dot(grad_projected, proj_full, ROWS_BY_ROWS)
    proj_grad = dot(normalized, grad_projected, COLUMNS_BY_COLUMNS)
    grad_normed = reduce_tokens(partial_one)
    grad_input_part, gain_one = rms_backward(input_part, gains_low[0], grad_normed)
    input_grad = spread_tokens((grad_middle + grad_input_part).astype(LOW)).astype(WIDE)
    gains_sum = lax.psum(jnp.stack([gain_one, gain_two]), ("dp", "tensor"))
    gains_reduced = lax.dynamic_slice_in_dim(gains_sum, me * depth, depth, 1)

    def rows_of(grad):
        return lambda owner: lax.dynamic_slice_in_dim(grad, owner * depth, depth, 0)

    output_reduced = sum(scatter_rows(rows_of(output_grad)).values())
    proj_reduced = sum(scatter_rows(rows_of(proj_grad)).values())
    query_reduced = proj_reduced[:, :query_width]
    keyval_reduced = proj_reduced[:, query_width:].reshape(depth, 2, key_width)
    mine, other = [], []
    for terms in hidden_terms:
        mine.append(sum(term for m, term in terms.items() if not m & PAIR))
        other.append(sum(term for m, term in terms.items() if m & PAIR))

    def hidden_columns(index):
        columns = slice(index * chunk_width, (index + 1) * chunk_width)
        return join(
            jnp.concatenate([terms[:, columns] for terms in mine], axis=1),
            jnp.concatenate([terms[:, columns] for terms in other], axis=1),
            pair_bit,
            1,
        )

    gateup_reduced = jnp.stack([hidden_columns(0), hidden_columns(1)], axis=1)
    down_reduced = hidden_columns(2)

    query_mean, query_square, query_next = adamw(
        query_weight, query_reduced, query_first, query_second, MATRIX_RATE, WEIGHT_DECAY
    )
    keyval_mean, keyval_square, keyval_next = adamw(
        keyval_weight, keyval_reduced, keyval_first, keyval_second, MATRIX_RATE, WEIGHT_DECAY
    )
    output_mean, output_square, output_next = adamw(
        output_weight, output_reduced, output_first, output_second, MATRIX_RATE, WEIGHT_DECAY
    )
    gateup_mean, gateup_square, gateup_next = adamw(
        gateup_weight, gateup_reduced, gateup_first, gateup_second, MATRIX_RATE, WEIGHT_DECAY
    )
    down_mean, down_square, down_next = adamw(
        down_weight, down_reduced, down_first, down_second, MATRIX_RATE, WEIGHT_DECAY
    )
    gains_mean, gains_square, gains_next = adamw(
        norm_gains, gains_reduced, gains_first, gains_second, GAIN_RATE, 0.0
    )
    return (
        block_output.reshape(count, length, width),
        input_grad.reshape(count, length, width),
        query_reduced,
        keyval_reduced,
        output_reduced,
        gateup_reduced,
        down_reduced,
        gains_reduced,
        query_mean,
        keyval_mean,
        output_mean,
        gateup_mean,
        down_mean,
        gains_mean,
        query_square,
        keyval_square,
        output_square,
        gateup_square,
        down_square,
        gains_square,
        query_next,
        keyval_next,
        output_next,
        gateup_next,
        down_next,
        gains_next,
    )


def solution(mesh):
    in_specs = (
        P("dp", None, None),
        P("dp", None, None),
        P("dp", None),
        P("dp", "tensor"),
        P("dp", None, "tensor"),
        P("dp", "tensor"),
        P("dp", None, "tensor"),
        P("dp", "tensor"),
        P(None, "dp"),
        P("dp", "tensor"),
        P("dp", None, "tensor"),
        P("dp", "tensor"),
        P("dp", None, "tensor"),
        P("dp", "tensor"),
        P(None, "dp"),
        P("dp", "tensor"),
        P("dp", None, "tensor"),
        P("dp", "tensor"),
        P("dp", None, "tensor"),
        P("dp", "tensor"),
        P(None, "dp"),
    )
    out_specs = (
        P("dp", None, None),
        P("dp", None, None),
        P("dp", "tensor"),
        P("dp", None, "tensor"),
        P("dp", "tensor"),
        P("dp", None, "tensor"),
        P("dp", "tensor"),
        P(None, "dp"),
        P("dp", "tensor"),
        P("dp", None, "tensor"),
        P("dp", "tensor"),
        P("dp", None, "tensor"),
        P("dp", "tensor"),
        P(None, "dp"),
        P("dp", "tensor"),
        P("dp", None, "tensor"),
        P("dp", "tensor"),
        P("dp", None, "tensor"),
        P("dp", "tensor"),
        P(None, "dp"),
        P("dp", "tensor"),
        P("dp", None, "tensor"),
        P("dp", "tensor"),
        P("dp", None, "tensor"),
        P("dp", "tensor"),
        P(None, "dp"),
    )
    return jax.shard_map(body, mesh=mesh, in_specs=in_specs, out_specs=out_specs, check_vma=False)
```

```python
import functools
import math

import jax
import jax.numpy as jnp
from jax import lax
from jax.experimental import pallas as pl
from jax.experimental.pallas import tpu as pltpu
from jax.sharding import PartitionSpec as P

HD = 64
STEP = 10

NORM_EPS = 1e-05
ROPE_BASE = 500000.0
BETA_ONE = 0.9
BETA_TWO = 0.95
ADAM_EPS = 1e-08
MATRIX_RATE = 0.05
GAIN_RATE = 0.6
WEIGHT_DECAY = 0.1
MASKED = -1e30

PAIR = 2
CHUNKS = 4

LOW = jnp.bfloat16
WIDE = jnp.float32
ROWS_BY_ROWS = (((1,), (1,)), ((), ()))
COLUMNS_BY_COLUMNS = (((0,), (0,)), ((), ()))


def dot(left, right, dims=(((1,), (0,)), ((), ()))):
    return lax.dot_general(left, right, dims, preferred_element_type=WIDE)


def swap(values, axis, mask):
    pairs = [(k, k ^ mask) for k in range(lax.axis_size(axis))]
    return lax.ppermute(values, axis, pairs)


def part(values, index, parts, dim):
    size = values.shape[dim] // parts
    return lax.dynamic_slice_in_dim(values, index * size, size, dim)


def join(mine, other, bit, dim):
    first = jnp.concatenate([mine, other], axis=dim)
    second = jnp.concatenate([other, mine], axis=dim)
    return jnp.where(bit == 0, first, second)


def angle_tables(positions):
    half_steps = jnp.arange(HD // 2, dtype=WIDE)
    frequency = jnp.exp(half_steps * (-2.0 / HD) * math.log(ROPE_BASE))
    angles = positions.astype(WIDE)[..., None] * frequency
    cosine = jnp.cos(angles)
    sine = jnp.sin(angles)
    return (
        jnp.concatenate([cosine, cosine], axis=-1)[..., None, :],
        jnp.concatenate([sine, sine], axis=-1)[..., None, :],
    )


def rotate(values, cosine, sine):
    middle_index = values.shape[-1] // 2
    turned = jnp.concatenate([-values[..., middle_index:], values[..., :middle_index]], axis=-1)
    return values * cosine + turned * sine


def rms_factor(values):
    return lax.rsqrt(jnp.mean(values * values, axis=-1, keepdims=True) + NORM_EPS)


def rms_backward(values, gain, grad):
    factor = rms_factor(values)
    scaled = grad * gain
    inner = jnp.mean(scaled * values, axis=-1, keepdims=True)
    grad_values = factor * scaled - values * (factor * factor * factor * inner)
    grad_gain = jnp.sum(grad * values * factor, axis=0)
    return grad_values, grad_gain


def attend_group(j, group, block, count, length, query_ref, key_ref, value_ref, mixed_ref, logsum_ref):
    row_index = lax.broadcasted_iota(jnp.int32, (block, block), 0)
    column_index = lax.broadcasted_iota(jnp.int32, (block, block), 1)
    allowed = column_index <= row_index
    for sequence in range(count):
        base = sequence * length
        for head in range(group):
            columns = slice((j * group + head) * HD, (j * group + head + 1) * HD)
            for start in range(base, base + length, block):
                rows = slice(start, start + block)
                before = slice(base, start)
                query = query_ref[rows, columns] * HD ** (-0.5)
                last = jnp.where(allowed, dot(query, key_ref[j, rows], ROWS_BY_ROWS), MASKED)
                highest = jnp.max(last, axis=-1, keepdims=True)
                if start > base:
                    early = dot(query, key_ref[j, before], ROWS_BY_ROWS)
                    highest = jnp.maximum(highest, jnp.max(early, axis=-1, keepdims=True))
                    early = jnp.exp(early - highest)
                last = jnp.exp(last - highest)
                total = jnp.sum(last, axis=-1, keepdims=True)
                if start > base:
                    total = total + jnp.sum(early, axis=-1, keepdims=True)
                share = 1.0 / total
                mixed = dot((last * share).astype(LOW), value_ref[j, rows])
                if start > base:
                    mixed = mixed + dot((early * share).astype(LOW), value_ref[j, before])
                mixed_ref[rows, columns] = mixed.astype(LOW)
                logsum_ref[j, rows, head : head + 1] = highest + jnp.log(total)


MESH = pl.DeviceIdType.MESH
MEGABYTE = 1 << 20


def flip(index, mask):
    bit = 1
    while bit <= mask:
        if mask & bit:
            index = index + bit - 2 * bit * lax.rem(lax.div(index, bit), 2)
        bit *= 2
    return index


def remote(source, target, sems, axis, mask):
    return pltpu.make_async_remote_copy(
        src_ref=source,
        dst_ref=target,
        send_sem=sems[0],
        recv_sem=sems[1],
        device_id={axis: flip(lax.axis_index(axis), mask)},
        device_id_type=MESH,
    )


def greet(partners):
    barrier = pltpu.get_barrier_semaphore()
    for axis, mask in partners:
        pl.semaphore_signal(
            barrier,
            inc=1,
            device_id={axis: flip(lax.axis_index(axis), mask)},
            device_id_type=MESH,
        )
    pl.semaphore_wait(barrier, len(partners))


class Gather:
    def __init__(self, masks, source, place, sems):
        self.masks, self.source, self.place, self.sems = masks, source, place, sems
        self.me = lax.axis_index("dp")
        self.started = []

    def sem(self, phase, mask):
        send, recv = self.sems
        return send.at[phase, mask // 2], recv.at[phase, mask // 2]

    def start(self):
        for mask in self.masks[1:]:
            copy = remote(
                self.source(mask), self.place(self.me), self.sem(0, mask), "dp", mask
            )
            copy.start()
            self.started.append(copy)

    def start_own(self):
        copy = remote(self.source(0), self.place(self.me), self.sem(1, 0), "dp", 1)
        copy.start()
        self.started.append(copy)

    def forward(self, mask):
        here = self.place(flip(self.me, mask))
        remote(here, here, self.sem(0, mask), "dp", mask).wait_recv()
        copy = remote(here, here, self.sem(1, mask), "dp", 1)
        copy.start()
        self.started.append(copy)

    def arrive(self, mask):
        here = self.place(flip(self.me, mask ^ 1))
        remote(here, here, self.sem(1, mask), "dp", 1).wait_recv()

    def drain(self):
        for copy in self.started:
            copy.wait_send()


def rotated(values, cosine, sine, first):
    width = values.shape[1]
    turned = jnp.where(
        first, pltpu.roll(values, width - HD // 2, 1), pltpu.roll(values, HD // 2, 1)
    )
    return values * cosine + turned * sine


def first_kernel(
    sizes,
    x_ref,
    cot_ref,
    proj_ref,
    out_ref,
    hidden_ref,
    gains_ref,
    cosine_ref,
    sine_ref,
    normalized_ref,
    proj_full,
    out_full,
    gains_full,
    query_ref,
    key_ref,
    value_ref,
    mixed_ref,
    logsum_ref,
    middle_ref,
    hidden_full,
    other_cot,
    both_ref,
    core_out,
    core_in,
    held,
    line_out,
    line_in,
    normed,
    gains_slots,
    gather_send,
    gather_recv,
    hidden_send,
    hidden_recv,
    token_send,
    token_recv,
    local_sem,
):
    count, length = sizes
    rows, width = x_ref.shape
    devices = lax.axis_size("dp")
    masks = list(range(0, devices, 2))
    me = lax.axis_index("dp")
    tensor = lax.axis_index("tensor")
    core, line = lax.rem(tensor, 2), lax.div(tensor, 2)
    pair_bit = lax.rem(lax.div(me, PAIR), 2)
    depth = proj_ref.shape[0]
    chunks = hidden_ref.shape[1]
    half, piece = rows // 2, rows // 4
    greet([("dp", mask) for mask in masks[1:] + [1]] + [("tensor", 1), ("tensor", 2)])

    def block_rows(ref):
        return lambda owner: ref.at[pl.ds(pl.multiple_of(owner * depth, depth), depth)]

    def pair_half(mask):
        return pair_bit if not mask & PAIR else 1 - pair_bit

    gains = Gather(
        masks,
        lambda mask: gains_ref,
        lambda owner: gains_slots.at[owner],
        (gather_send.at[0], gather_recv.at[0]),
    )
    proj = Gather(
        masks,
        lambda mask: proj_ref,
        block_rows(proj_full),
        (gather_send.at[1], gather_recv.at[1]),
    )
    out = Gather(
        masks, lambda mask: out_ref, block_rows(out_full), (gather_send.at[2], gather_recv.at[2])
    )
    hidden = [
        Gather(
            masks,
            lambda mask, chunk=chunk: hidden_ref.at[pair_half(mask), chunk],
            block_rows(hidden_full.at[chunk]),
            (hidden_send.at[chunk], hidden_recv.at[chunk]),
        )
        for chunk in range(chunks)
    ]
    tokens = []

    def send_tokens(source, target, index, axis, mask):
        copy = remote(source, target, (token_send.at[index], token_recv.at[index]), axis, mask)
        copy.start()
        tokens.append(copy)

    def wait_tokens(target, index, axis, mask):
        remote(
            target, target, (token_send.at[index], token_recv.at[index]), axis, mask
        ).wait_recv()

    def piece_rows(ref, core_at, line_at):
        return ref.at[pl.ds(pl.multiple_of(core_at * half + line_at * piece, piece), piece)]

    def half_rows(ref, core_at):
        return ref.at[pl.ds(pl.multiple_of(core_at * half, half), half)]

    gains.start()
    gains.start_own()
    proj.start()
    proj.start_own()
    here = piece_rows(other_cot, core, line)
    send_tokens(piece_rows(cot_ref, core, line), here, 0, "dp", PAIR)
    out.start()
    out.start_own()
    hidden[0].start()
    hidden[0].start_own()
    own = [
        pltpu.make_async_copy(gains_ref, gains.place(me), local_sem.at[0]),
        pltpu.make_async_copy(proj_ref, proj.place(me), local_sem.at[1]),
        pltpu.make_async_copy(out_ref, out.place(me), local_sem.at[2]),
    ]
    for copy in own:
        copy.start()
    own_hidden = [
        pltpu.make_async_copy(gather.source(0), gather.place(me), local_sem.at[3 + chunk])
        for chunk, gather in enumerate(hidden)
    ]
    for copy in own_hidden:
        copy.start()

    def pump(chunk):
        for mask in masks[1:]:
            hidden[chunk].forward(mask)
        if chunk + 2 < chunks:
            hidden[chunk + 2].start()
            hidden[chunk + 2].start_own()

    for mask in masks[1:]:
        gains.forward(mask)
    for mask in masks:
        gains.arrive(mask)
    for copy in own:
        copy.wait()
    gains_full[...] = jnp.concatenate([gains_slots[j] for j in range(devices)], axis=1)
    tile = rows // 4

    def norm_tile(index, carry):
        at = pl.ds(pl.multiple_of(index * tile, tile), tile)
        values = x_ref[at].astype(WIDE)
        normalized_ref[at] = (values * rms_factor(values) * gains_full[0:1]).astype(LOW)
        return carry

    lax.fori_loop(0, 4, norm_tile, 0)
    for mask in masks[1:]:
        proj.forward(mask)
    if chunks > 1:
        hidden[1].start()
        hidden[1].start_own()
    for mask in masks:
        proj.arrive(mask)
    query_width = query_ref.shape[1]
    kv = key_ref.shape[0]
    group = query_width // (kv * HD)

    def project_tile(index, carry):
        at = pl.ds(pl.multiple_of(index * tile, tile), tile)
        pre = dot(normalized_ref[at], proj_full[...])
        cosine, sine = cosine_ref[at], sine_ref[at]

        def turn(values):
            times = values.shape[1] // cosine.shape[1]
            lanes = lax.broadcasted_iota(jnp.int32, values.shape, 1)
            return rotated(
                values,
                jnp.concatenate([cosine] * times, axis=1),
                jnp.concatenate([sine] * times, axis=1),
                lax.rem(lanes, HD) < HD // 2,
            ).astype(LOW)

        query_ref[at] = turn(pre[:, :query_width])
        keys = turn(pre[:, query_width : query_width + kv * HD])
        values = pre[:, query_width + kv * HD :].astype(LOW)
        for j in range(kv):
            key_ref[j, at] = keys[:, j * HD : (j + 1) * HD]
            value_ref[j, at] = values[:, j * HD : (j + 1) * HD]
        return carry

    lax.fori_loop(0, 4, project_tile, 0)

    wait_tokens(here, 0, "dp", PAIR)
    send_tokens(here, here, 1, "tensor", 2)
    send_tokens(here, here, 2, "tensor", 1)

    block = min(256, length)
    for j in range(kv):
        attend_group(
            j, group, block, count, length, query_ref, key_ref, value_ref, mixed_ref, logsum_ref
        )
        if j == 0:
            for mask in masks[1:]:
                out.forward(mask)

    there = piece_rows(other_cot, core, 1 - line)
    wait_tokens(there, 1, "tensor", 2)
    send_tokens(there, there, 3, "tensor", 1)

    for mask in masks:
        out.arrive(mask)
    strips = core_out.shape[0]
    strip = width // strips
    for s in range(strips):
        weight = out_full[s * strip : (s + 1) * strip]
        far = mixed_ref[pl.ds(pl.multiple_of((1 - core) * half, half), half)]
        core_out[s] = dot(far, weight, ROWS_BY_ROWS).astype(LOW)
        send_tokens(core_out.at[s], core_in.at[s], 8 + s, "tensor", 1)
    for s in range(strips):
        weight = out_full[s * strip : (s + 1) * strip]
        near = mixed_ref[pl.ds(pl.multiple_of(core * half, half), half)]
        held[s] = dot(near, weight, ROWS_BY_ROWS)
        wait_tokens(core_in.at[s], 8 + s, "tensor", 1)
        at = pl.ds(pl.multiple_of((1 - line) * piece, piece), piece)
        line_out[s] = (held[s, at] + core_in[s, at].astype(WIDE)).astype(LOW)
        send_tokens(line_out.at[s], line_in.at[s], 8 + strips + s, "tensor", 2)
    pump(0)
    at = pl.ds(pl.multiple_of(line * piece, piece), piece)
    own_rows = pl.ds(pl.multiple_of(core * half + line * piece, piece), piece)
    for s in range(strips):
        wait_tokens(line_in.at[s], 8 + strips + s, "tensor", 2)
        columns = slice(s * strip, (s + 1) * strip)
        middle_ref[:, columns] = (
            x_ref[own_rows, columns].astype(WIDE)
            + held[s, at]
            + core_in[s, at].astype(WIDE)
            + line_in[s].astype(WIDE)
        )
    middle = middle_ref[...]
    normed[...] = (middle * rms_factor(middle) * gains_full[1:2]).astype(LOW)

    near, far = both_ref.at[0], both_ref.at[1]
    place = piece_rows(near, core, line)
    send_tokens(normed, piece_rows(far, core, line), 4, "dp", PAIR)
    send_tokens(normed, place, 5, "tensor", 2)
    send_tokens(normed, place, 6, "tensor", 1)
    last = pltpu.make_async_copy(normed, place, local_sem.at[3 + chunks])
    last.start()
    place = piece_rows(near, core, 1 - line)
    wait_tokens(place, 5, "tensor", 2)
    send_tokens(place, place, 7, "tensor", 1)
    if chunks > 1:
        pump(1)
    base = 8 + 2 * strips
    place = piece_rows(far, core, line)
    wait_tokens(place, 4, "dp", PAIR)
    send_tokens(place, place, base, "tensor", 2)
    send_tokens(place, place, base + 1, "tensor", 1)
    for chunk in range(2, chunks):
        pump(chunk)
        if chunk == 2:
            place = piece_rows(far, core, 1 - line)
            wait_tokens(place, base, "tensor", 2)
            send_tokens(place, place, base + 2, "tensor", 1)
    if chunks < 3:
        place = piece_rows(far, core, 1 - line)
        wait_tokens(place, base, "tensor", 2)
        send_tokens(place, place, base + 2, "tensor", 1)

    wait_tokens(piece_rows(other_cot, 1 - core, line), 2, "tensor", 1)
    wait_tokens(piece_rows(other_cot, 1 - core, 1 - line), 3, "tensor", 1)
    wait_tokens(piece_rows(near, 1 - core, line), 6, "tensor", 1)
    wait_tokens(piece_rows(near, 1 - core, 1 - line), 7, "tensor", 1)
    wait_tokens(piece_rows(far, 1 - core, line), base + 1, "tensor", 1)
    wait_tokens(piece_rows(far, 1 - core, 1 - line), base + 2, "tensor", 1)
    for gather in hidden:
        for mask in masks:
            gather.arrive(mask)
    for copy in own_hidden:
        copy.wait()
    last.wait()
    for gather in [gains, proj, out] + hidden:
        gather.drain()
    for copy in tokens:
        copy.wait_send()


def first_half(x, cot, proj, out, hidden, gains, cosine, sine, kv, count):
    rows, width = x.shape
    devices = lax.axis_size("dp")
    spans = devices // 2
    depth = proj.shape[0]
    chunks = hidden.shape[1]
    query_width = out.shape[1]
    group = query_width // (kv * HD)
    half, piece = rows // 2, rows // 4
    strips = 4
    strip = width // strips
    vmem = pl.BlockSpec(memory_space=pltpu.VMEM)
    anywhere = pl.BlockSpec(memory_space=pl.ANY)
    shape = jax.ShapeDtypeStruct
    n_tokens = 8 + 2 * strips + 3
    return pl.pallas_call(
        functools.partial(first_kernel, (count, rows // count)),
        in_specs=[vmem, anywhere, vmem, vmem, anywhere, vmem, vmem, vmem],
        out_specs=[vmem] * 10 + [anywhere] * 3,
        out_shape=[
            shape((rows, width), LOW),
            shape((devices * depth, proj.shape[1]), LOW),
            shape((devices * depth, query_width), LOW),
            shape((gains.shape[0], width), WIDE),
            shape((rows, query_width), LOW),
            shape((kv, rows, HD), LOW),
            shape((kv, rows, HD), LOW),
            shape((rows, query_width), LOW),
            shape((kv, rows, group), WIDE),
            shape((piece, width), WIDE),
            shape((chunks, devices * depth, hidden.shape[3]), LOW),
            shape((rows, width), LOW),
            shape((2, rows, width), LOW),
        ],
        scratch_shapes=[
            pltpu.VMEM((strips, half, strip), LOW),
            pltpu.VMEM((strips, half, strip), LOW),
            pltpu.VMEM((strips, half, strip), WIDE),
            pltpu.VMEM((strips, piece, strip), LOW),
            pltpu.VMEM((strips, piece, strip), LOW),
            pltpu.VMEM((piece, width), LOW),
            pltpu.VMEM((devices,) + gains.shape, WIDE),
            pltpu.SemaphoreType.DMA((3, 2, spans)),
            pltpu.SemaphoreType.DMA((3, 2, spans)),
            pltpu.SemaphoreType.DMA((chunks, 2, spans)),
            pltpu.SemaphoreType.DMA((chunks, 2, spans)),
            pltpu.SemaphoreType.DMA((n_tokens,)),
            pltpu.SemaphoreType.DMA((n_tokens,)),
            pltpu.SemaphoreType.DMA((4 + chunks,)),
        ],
        compiler_params=pltpu.CompilerParams(
            collective_id=0, has_side_effects=True, vmem_limit_bytes=56 * MEGABYTE
        ),
        name="gather_and_attend",
    )(x, cot, proj, out, hidden, gains, cosine, sine)


SLOTS = 2


class Scatter:
    def __init__(self, masks, product, landing, terms, stage, sems):
        self.masks, self.product, self.landing, self.terms = masks, product, landing, terms
        self.stage, self.sems = stage, sems
        self.me = lax.axis_index("dp")
        self.depth = product.shape[0] // lax.axis_size("dp")

    def rows(self, owner):
        return pl.ds(pl.multiple_of(owner * self.depth, self.depth), self.depth)

    def copy(self, phase, mask, source, target):
        send, recv, _ = self.sems
        at = mask // 2
        axis_mask = 1 if phase == 0 else mask
        return remote(source, target, (send.at[phase, at], recv.at[phase, at]), "dp", axis_mask)

    def start(self):
        for mask in self.masks[1:] + [0]:
            self.near_copy(mask).start()

    def near_copy(self, mask):
        source = self.product.at[self.rows(flip(self.me, mask ^ 1))]
        return self.copy(0, mask, source, self.landing.at[mask // 2])

    def far_copy(self, mask):
        source = self.product.at[self.rows(flip(self.me, mask))]
        target = self.terms.at[mask // 2]
        if mask:
            return self.copy(1, mask, source, target)
        return pltpu.make_async_copy(source, target, self.sems[2].at[2])

    def pump(self):
        local = self.sems[2]
        order = self.masks[1:] + [0]
        loads = []

        def load(index):
            landed = self.landing.at[order[index] // 2]
            self.copy(0, order[index], landed, landed).wait_recv()
            copy = pltpu.make_async_copy(landed, self.stage.at[index % 2], local.at[index % 2])
            copy.start()
            loads.append(copy)

        load(0)
        for index, mask in enumerate(order):
            if index + 1 < len(order):
                load(index + 1)
            loads[index].wait()
            at = self.rows(flip(self.me, mask))
            total = self.product[at].astype(WIDE) + self.stage[index % 2].astype(WIDE)
            self.product[at] = total.astype(LOW)
            self.far_copy(mask).start()

    def release(self):
        for mask in self.masks:
            self.near_copy(mask).wait_send()
        for mask in self.masks[1:]:
            self.far_copy(mask).wait_send()
        self.far_copy(0).wait()

    def arrive(self):
        for mask in self.masks[1:]:
            landed = self.terms.at[mask // 2]
            self.copy(1, mask, landed, landed).wait_recv()


def attend_back_group(
    j,
    group,
    block,
    count,
    length,
    query_ref,
    key_ref,
    value_ref,
    logsum_ref,
    grad_ref,
    query_grad_ref,
    key_grad_ref,
    value_grad_ref,
):
    key_index = lax.broadcasted_iota(jnp.int32, (block, block), 0)
    query_index = lax.broadcasted_iota(jnp.int32, (block, block), 1)
    allowed = key_index <= query_index
    scale = HD ** (-0.5)
    for sequence in range(count):
        base = sequence * length
        for head in range(group):
            columns = slice((j * group + head) * HD, (j * group + head + 1) * HD)
            for start in range(base, base + length, block):
                rows = slice(start, start + block)
                query = query_ref[rows, columns] * scale
                grad = grad_ref[rows, columns]
                logsum = logsum_ref[j, head : head + 1, rows]
                spans = [(rows, True)]
                if start > base:
                    spans.append((slice(base, start), False))
                probs, grad_probs = [], []
                for span, masked in spans:
                    scores = dot(key_ref[j, span], query, ROWS_BY_ROWS)
                    if masked:
                        scores = jnp.where(allowed, scores, MASKED)
                    probs.append(jnp.exp(scores - logsum))
                    grad_probs.append(dot(value_ref[j, span], grad, ROWS_BY_ROWS))
                inner = sum(
                    jnp.sum(one * two, axis=0, keepdims=True)
                    for one, two in zip(probs, grad_probs)
                )
                query_grad = None
                for (span, _), one, two in zip(spans, probs, grad_probs):
                    grad_scores = (one * (two - inner)).astype(LOW)
                    term = dot(grad_scores, key_ref[j, span], COLUMNS_BY_COLUMNS)
                    query_grad = term if query_grad is None else query_grad + term
                    key_grad_ref[j, span] += dot(grad_scores, query)
                    value_grad_ref[j, span] += dot(one.astype(LOW), grad)
                query_grad_ref[rows, columns] = query_grad * scale


def second_kernel(
    sizes,
    normed_ref,
    cot_ref,
    other_ref,
    hidden_ref,
    normalized_ref,
    proj_ref,
    out_ref,
    query_ref,
    key_ref,
    value_ref,
    mixed_ref,
    logsum_ref,
    middle_ref,
    x_ref,
    cosine_ref,
    sine_ref,
    gains_ref,
    hidden_terms,
    out_terms,
    proj_terms,
    output_ref,
    input_grad_ref,
    gains_sum,
    hidden_land,
    out_land,
    proj_land,
    middle_low,
    line_land,
    product,
    stage,
    core_out,
    core_in,
    held,
    keep,
    line_out,
    line_in,
    last_in,
    pair_in,
    flat,
    middle,
    grad_middle,
    low_out,
    low_grad,
    gain_steps,
    gain_land,
    scatter_send,
    scatter_recv,
    scatter_local,
    core_send,
    core_recv,
    line_send,
    line_recv,
    pair_send,
    pair_recv,
    spread_send,
    spread_recv,
    gain_send,
    gain_recv,
    load_sem,
    strip_sem,
    local_sem,
    credit,
):
    count, length = sizes
    rows, width = cot_ref.shape
    devices = lax.axis_size("dp")
    masks = list(range(0, devices, 2))
    me = lax.axis_index("dp")
    tensor = lax.axis_index("tensor")
    core, line = lax.rem(tensor, 2), lax.div(tensor, 2)
    chunks = hidden_ref.shape[0]
    unit = hidden_ref.shape[2] // 3
    half, piece = rows // 2, rows // 4
    strips, strip = keep.shape[0], keep.shape[2]
    query_width = query_ref.shape[1]
    kv = key_ref.shape[0]
    group = query_width // (kv * HD)
    greet([("dp", mask) for mask in masks[1:] + [1]] + [("tensor", 1), ("tensor", 2)])

    quarter = pl.ds(pl.multiple_of(core * half + line * piece, piece), piece)
    near_half = pl.multiple_of(core * half, half)
    far_half = pl.multiple_of((1 - core) * half, half)
    near_line = pl.ds(pl.multiple_of(line * piece, piece), piece)
    far_line = pl.ds(pl.multiple_of((1 - line) * piece, piece), piece)

    def place(ref, core_at, line_at):
        return ref.at[pl.ds(pl.multiple_of(core_at * half + line_at * piece, piece), piece)]

    def scatter(index, product_ref, landing, terms):
        depth, columns = landing.shape[1:]
        return Scatter(
            masks,
            product_ref,
            landing,
            terms,
            stage.at[:, :, :columns] if columns < stage.shape[2] else stage,
            (scatter_send.at[index], scatter_recv.at[index], scatter_local.at[index]),
        )

    hidden = [
        scatter(c, product.at[c % SLOTS], hidden_land.at[c], hidden_terms.at[c]) for c in range(chunks)
    ]

    def core_copy(slot, parts):
        return remote(
            core_out.at[slot, pl.ds(0, parts)],
            core_in.at[slot, pl.ds(0, parts)],
            (core_send.at[slot], core_recv.at[slot]),
            "tensor",
            1,
        )

    def line_copy(turn, s, parts, landing):
        return remote(
            line_out.at[s, pl.ds(0, parts)],
            landing.at[s],
            (line_send.at[turn, s], line_recv.at[turn, s]),
            "tensor",
            2,
        )

    def pair_copy(turn, s, landing):
        return remote(
            line_out.at[s, 1],
            landing.at[s],
            (pair_send.at[turn, s], pair_recv.at[turn, s]),
            "dp",
            PAIR,
        )

    def reduce_strips(turn, parts, term, prepare, landing):
        def one_strip(s, carry):
            slot = lax.rem(s, 2)
            prepare(s, slot)

            @pl.when(s >= 2)
            def _():
                core_copy(slot, parts).wait_send()

            for q in range(parts):
                core_out[slot, q] = term(q, far_half, s, slot).astype(LOW)
            if turn:
                pl.semaphore_wait(credit, 1)
            else:

                @pl.when(s >= 2)
                def _():
                    pl.semaphore_wait(credit, 1)

            copy = core_copy(slot, parts)
            copy.start()
            for q in range(parts):
                held[q] = term(q, near_half, s, slot)
            copy.wait_recv()
            for q in range(parts):
                line_out[s, q] = (held[q, far_line] + core_in[slot, q, far_line].astype(WIDE)).astype(
                    LOW
                )
            near = [
                held[q, near_line] + core_in[slot, q, near_line].astype(WIDE)
                for q in range(parts)
            ]
            keep[s] = near[0]
            if parts == 2:
                flat[:, pl.ds(pl.multiple_of(s * strip, strip), strip)] = near[1]
            pl.semaphore_signal(
                credit, inc=1, device_id={"tensor": flip(tensor, 1)}, device_id_type=MESH
            )
            line_copy(turn, s, parts, landing).start()
            return carry

        lax.fori_loop(0, strips, one_strip, 0)
        for slot in range(2):
            core_copy(slot, parts).wait_send()

    def strip_loads(s, slot):
        return [
            pltpu.make_async_copy(
                hidden_ref.at[c, pl.ds(pl.multiple_of(s * strip, strip), strip)],
                weights.at[pl.ds(pl.multiple_of((slot * chunks + c) * strip, strip), strip)],
                strip_sem.at[slot, c],
            )
            for c in range(chunks)
        ]

    def start_strip(s, slot):
        for copy in strip_loads(s, slot):
            copy.start()

    def prepare_strip(s, slot):
        @pl.when(s + 1 < strips)
        def _():
            start_strip(s + 1, 1 - slot)

        for copy in strip_loads(s, slot):
            copy.wait()

    def hidden_term(ref, first, wide):
        def term(q, start, s, slot):
            at = pl.ds(pl.multiple_of(q * rows + start, half), half)
            total = None
            for c in range(chunks):
                block = weights[
                    pl.ds(pl.multiple_of((slot * chunks + c) * strip, strip), strip),
                    first : first + wide,
                ]
                one = dot(ref[at, c * wide : (c + 1) * wide], block, ROWS_BY_ROWS)
                total = one if total is None else total + one
            return total

        return term

    def to_pair(turn, landing):
        for s in range(strips):
            copy = line_copy(turn, s, 2, landing)
            copy.wait_recv()
            copy.wait_send()
        if landing is not line_in:
            copy = pltpu.make_async_copy(landing, line_in, load_sem.at[0])
            copy.start()
            copy.wait()
        for s in range(strips):
            columns = slice(s * strip, (s + 1) * strip)
            line_out[s, 1] = (flat[:, columns] + line_in[s, 1].astype(WIDE)).astype(LOW)
            pair_copy(turn, s, pair_in.at[turn]).start()
            flat[:, columns] = keep[s] + line_in[s, 0].astype(WIDE)

    def from_pair(turn):
        for s in range(strips):
            copy = pair_copy(turn, s, pair_in.at[turn])
            copy.wait_recv()
            copy.wait_send()
            flat[:, s * strip : (s + 1) * strip] += pair_in[turn, s].astype(WIDE)

    tile = min(64, piece)

    def rms_back(values_of, gain, grads_of, store, gain_row):
        def one_tile(index, total):
            at = pl.ds(pl.multiple_of(index * tile, tile), tile)
            values, grads = values_of(at), grads_of(at)
            grad_values, grad_gain = rms_backward(values, gain, grads)
            store(at, grad_values)
            return total + grad_gain[None]

        zero = jnp.zeros((1, width), WIDE)
        gain_steps[0, gain_row : gain_row + 1] = lax.fori_loop(0, piece // tile, one_tile, zero)

    def spread_copy(index, source, target, mask):
        return remote(
            source, target, (spread_send.at[index], spread_recv.at[index]), "tensor", mask
        )

    def spread(base, source, target):
        here = place(target, core, line)
        spread_copy(base, source, here, 2).start()
        spread_copy(base + 1, source, here, 1).start()
        pltpu.make_async_copy(source, here, local_sem.at[base]).start()

    def spread_on(base, target):
        there = place(target, core, 1 - line)
        spread_copy(base, there, there, 2).wait_recv()
        spread_copy(base + 2, there, there, 1).start()

    def spread_release(base, source, target):
        here, there = place(target, core, line), place(target, core, 1 - line)
        spread_copy(base, source, here, 2).wait_send()
        spread_copy(base + 1, source, here, 1).wait_send()
        spread_copy(base + 2, there, there, 1).wait_send()
        pltpu.make_async_copy(source, here, local_sem.at[base]).wait()

    def spread_end(base, target):
        near, far = place(target, 1 - core, line), place(target, 1 - core, 1 - line)
        spread_copy(base + 1, near, near, 1).wait_recv()
        spread_copy(base + 2, far, far, 1).wait_recv()

    gain_masks = [("tensor", 1), ("tensor", 2)]
    bit = 1
    while bit < devices:
        gain_masks.append(("dp", bit))
        bit *= 2

    weights = None

    def feed_forward(normed, grads, weights_ref, gate_ref, hidden_out):
        nonlocal weights
        weights = weights_ref
        loads = [
            pltpu.make_async_copy(normed_ref.at[0], normed.at[pl.ds(0, rows)], load_sem.at[0]),
            pltpu.make_async_copy(normed_ref.at[1], normed.at[pl.ds(rows, rows)], load_sem.at[1]),
            pltpu.make_async_copy(cot_ref, grads.at[pl.ds(0, rows)], load_sem.at[2]),
            pltpu.make_async_copy(other_ref, grads.at[pl.ds(rows, rows)], load_sem.at[3]),
        ]

        def load_weights(c):
            return pltpu.make_async_copy(hidden_ref.at[c], weights, load_sem.at[4])

        load_weights(0).start()
        for copy in loads:
            copy.start()
        load_middle = pltpu.make_async_copy(middle_ref, middle, load_sem.at[5])
        load_middle.start()
        tokens = min(512, rows)

        def stage_one(c):
            load_weights(c).wait()

            def one_tile(index, carry):
                at = pl.ds(pl.multiple_of(index * tokens, tokens), tokens)
                gate_up = dot(normed[at], weights[:, : 2 * unit])
                grad_hidden = dot(grads[at], weights[:, 2 * unit :])
                gate, upward = gate_up[:, :unit], gate_up[:, unit:]
                sigma = jax.nn.sigmoid(gate)
                passed = gate * sigma
                hidden_out[at, c * unit : (c + 1) * unit] = (passed * upward).astype(LOW)
                grad_gate = grad_hidden * upward * sigma * (1.0 + gate * (1.0 - sigma))
                first = 2 * c * unit
                gate_ref[at, first : first + unit] = grad_gate.astype(LOW)
                gate_ref[at, first + unit : first + 2 * unit] = (grad_hidden * passed).astype(LOW)
                return carry

            lax.fori_loop(0, 2 * rows // tokens, one_tile, 0)
            if c + 1 < chunks:
                load_weights(c + 1).start()

        columns = min(256, width)

        def stage_two(c):
            if c >= SLOTS:
                hidden[c - SLOTS].release()

            def one_tile(index, carry):
                at = pl.ds(pl.multiple_of(index * columns, columns), columns)
                gate_up = dot(
                    normed[:, at], gate_ref[:, 2 * c * unit : 2 * (c + 1) * unit], COLUMNS_BY_COLUMNS
                )
                down = dot(grads[:, at], hidden_out[:, c * unit : (c + 1) * unit], COLUMNS_BY_COLUMNS)
                product[c % SLOTS, at, : 2 * unit] = gate_up.astype(LOW)
                product[c % SLOTS, at, 2 * unit :] = down.astype(LOW)
                return carry

            lax.fori_loop(0, width // columns, one_tile, 0)
            hidden[c].start()

        for copy in loads:
            copy.wait()
        gain_steps[0] = jnp.zeros(gain_steps.shape[1:], WIDE)
        stage_one(0)
        stage_two(0)
        for c in range(1, chunks):
            stage_one(c)
        start_strip(0, 0)
        hidden[0].pump()
        reduce_strips(0, 2, hidden_term(gate_ref, 0, 2 * unit), prepare_strip, line_in)
        stage_two(1)
        stage_two(2)
        to_pair(0, line_in)
        hidden[1].pump()
        from_pair(0)
        load_middle.wait()
        load_cot = pltpu.make_async_copy(cot_ref.at[quarter], low_grad, load_sem.at[6])
        load_cot.start()
        load_cot.wait()

        def store(at, grad_values):
            total = low_grad[at].astype(WIDE) + grad_values
            grad_middle[at] = total
            low_out[at] = total.astype(LOW)

        rms_back(lambda at: middle[at], gains_ref[1:2], lambda at: flat[at], store, 1)
        spread(0, low_out, middle_low)
        start_strip(0, 0)
        reduce_strips(1, 2, hidden_term(hidden_out, 2 * unit, unit), prepare_strip, line_land)
        spread_on(0, middle_low)
        stage_two(3)

    pl.run_scoped(
        feed_forward,
        pltpu.VMEM((2 * rows, width), LOW),
        pltpu.VMEM((2 * rows, width), LOW),
        pltpu.VMEM((width, 3 * unit), LOW),
        pltpu.VMEM((2 * rows, 2 * unit * chunks), LOW),
        pltpu.VMEM((2 * rows, unit * chunks), LOW),
    )

    def second_phase(
        grads,
        out_full,
        proj_full,
        query,
        key,
        value,
        mixed,
        normalized,
        grad_mixed,
        query_grad,
        key_grad,
        value_grad,
        projected,
        out_product,
        proj_product,
        cosines,
        sines,
    ):
        sources = [out_ref, query_ref, key_ref, value_ref, mixed_ref, proj_ref, normalized_ref]
        sources += [cosine_ref, sine_ref]
        targets = [out_full, query, key, value, mixed, proj_full, normalized, cosines, sines]
        loads = [
            pltpu.make_async_copy(source, target, load_sem.at[index])
            for index, (source, target) in enumerate(zip(sources, targets))
        ]
        for copy in loads:
            copy.start()
        key_grad[...] = jnp.zeros_like(key_grad)
        value_grad[...] = jnp.zeros_like(value_grad)
        spread_end(0, middle_low)
        spread_release(0, low_out, middle_low)
        load_grads = pltpu.make_async_copy(middle_low, grads, load_sem.at[len(loads)])
        load_grads.start()
        loads[0].wait()
        load_grads.wait()
        tokens = min(256, rows)

        def mixed_tile(index, carry):
            at = pl.ds(pl.multiple_of(index * tokens, tokens), tokens)
            grad_mixed[at] = dot(grads[at], out_full[...]).astype(LOW)
            return carry

        lax.fori_loop(0, rows // tokens, mixed_tile, 0)
        for copy in loads[1:5]:
            copy.wait()
        columns = min(256, width)

        def out_tile(index, carry):
            at = pl.ds(pl.multiple_of(index * columns, columns), columns)
            out_product[at] = dot(grads[:, at], mixed[...], COLUMNS_BY_COLUMNS).astype(LOW)
            return carry

        lax.fori_loop(0, width // columns, out_tile, 0)
        out = scatter(chunks, out_product, out_land, out_terms)
        out.start()
        block = min(256, length)
        for j in range(kv):
            attend_back_group(
                j,
                group,
                block,
                count,
                length,
                query,
                key,
                value,
                logsum_ref,
                grad_mixed,
                query_grad,
                key_grad,
                value_grad,
            )
            if j == 0:
                hidden[2].pump()
        to_pair(1, line_land)
        for copy in loads[5:]:
            copy.wait()

        def turn_tile(index, carry):
            at = pl.ds(pl.multiple_of(index * tokens, tokens), tokens)
            cosine, sine = cosines[at], -sines[at]

            def turn(values):
                times = values.shape[1] // cosine.shape[1]
                lanes = lax.broadcasted_iota(jnp.int32, values.shape, 1)
                return rotated(
                    values,
                    jnp.concatenate([cosine] * times, axis=1),
                    jnp.concatenate([sine] * times, axis=1),
                    lax.rem(lanes, HD) < HD // 2,
                ).astype(LOW)

            keys = jnp.concatenate([key_grad[j, at] for j in range(kv)], axis=1)
            values = jnp.concatenate([value_grad[j, at] for j in range(kv)], axis=1)
            projected[at, :query_width] = turn(query_grad[at])
            projected[at, query_width : query_width + kv * HD] = turn(keys)
            projected[at, query_width + kv * HD :] = values.astype(LOW)
            return carry

        lax.fori_loop(0, rows // tokens, turn_tile, 0)

        def proj_term(q, start, s, slot):
            return dot(
                projected[pl.ds(start, half)],
                proj_full[pl.ds(pl.multiple_of(s * strip, strip), strip)],
                ROWS_BY_ROWS,
            )

        reduce_strips(2, 1, proj_term, lambda s, slot: None, last_in)

        def proj_tile(index, carry):
            at = pl.ds(pl.multiple_of(index * columns, columns), columns)
            proj_product[at] = dot(normalized[:, at], projected[...], COLUMNS_BY_COLUMNS).astype(LOW)
            return carry

        lax.fori_loop(0, width // columns, proj_tile, 0)
        proj = scatter(chunks + 1, proj_product, proj_land, proj_terms)
        proj.start()
        hidden[3].pump()
        load_x = pltpu.make_async_copy(x_ref.at[quarter], low_grad, load_sem.at[1])
        load_x.start()
        for s in range(strips):
            copy = line_copy(2, s, 1, last_in)
            copy.wait_recv()
            copy.wait_send()
        load_x.wait()

        def grads_of(at):
            return jnp.concatenate(
                [keep[s, at] + last_in[s, 0, at].astype(WIDE) for s in range(strips)], axis=1
            )

        def store(at, grad_values):
            low_out[at] = (grad_middle[at] + grad_values).astype(LOW)

        rms_back(lambda at: low_grad[at].astype(WIDE), gains_ref[0:1], grads_of, store, 0)
        spread(3, low_out, input_grad_ref)

        from_pair(1)
        low_grad[...] = (middle[...] + flat[...]).astype(LOW)
        spread(6, low_grad, output_ref)
        out.pump()
        for index, (axis, mask) in enumerate(gain_masks):
            copy = remote(
                gain_steps.at[index],
                gain_land.at[index],
                (gain_send.at[index], gain_recv.at[index]),
                axis,
                mask,
            )
            copy.start()
            copy.wait_recv()
            gain_steps[index + 1] = gain_steps[index] + gain_land[index]
            copy.wait_send()
        gains_sum[...] = gain_steps[len(gain_masks)]
        spread_on(3, input_grad_ref)
        proj.pump()
        spread_on(6, output_ref)
        for gather in hidden + [out, proj]:
            gather.arrive()
        for gather in hidden[chunks - SLOTS :] + [out, proj]:
            gather.release()
        for base, source, target in ((3, low_out, input_grad_ref), (6, low_grad, output_ref)):
            spread_end(base, target)
            spread_release(base, source, target)
        pl.semaphore_wait(credit, 2)

    pl.run_scoped(
        second_phase,
        pltpu.VMEM((rows, width), LOW),
        pltpu.VMEM(out_ref.shape, LOW),
        pltpu.VMEM(proj_ref.shape, LOW),
        pltpu.VMEM(query_ref.shape, LOW),
        pltpu.VMEM(key_ref.shape, LOW),
        pltpu.VMEM(value_ref.shape, LOW),
        pltpu.VMEM(mixed_ref.shape, LOW),
        pltpu.VMEM(normalized_ref.shape, LOW),
        pltpu.VMEM(query_ref.shape, LOW),
        pltpu.VMEM(query_ref.shape, WIDE),
        pltpu.VMEM(key_ref.shape, WIDE),
        pltpu.VMEM(key_ref.shape, WIDE),
        pltpu.VMEM((rows, proj_ref.shape[1]), LOW),
        pltpu.VMEM(out_ref.shape, LOW),
        pltpu.VMEM(proj_ref.shape, LOW),
        pltpu.VMEM(cosine_ref.shape, WIDE),
        pltpu.VMEM(sine_ref.shape, WIDE),
    )


def second_half(
    normed, cot, other, hidden, normalized, proj, out, query, key, value, mixed, logsum, middle, x,
    cosine, sine, gains, count
):
    rows, width = cot.shape
    devices = lax.axis_size("dp")
    spans = devices // 2
    chunks = hidden.shape[0]
    assert chunks == 4
    depth = width // devices
    columns = hidden.shape[2]
    unit = columns // 3
    half, piece = rows // 2, rows // 4
    strip = width // (2 * chunks)
    strips = width // strip
    steps = 2 + devices.bit_length() - 1
    vmem = pl.BlockSpec(memory_space=pltpu.VMEM)
    anywhere = pl.BlockSpec(memory_space=pl.ANY)
    shape = jax.ShapeDtypeStruct
    dma = pltpu.SemaphoreType.DMA
    return pl.pallas_call(
        functools.partial(second_kernel, (count, rows // count)),
        in_specs=[anywhere] * 11 + [vmem] + [anywhere] * 4 + [vmem],
        out_specs=[anywhere] * 5 + [vmem] + [anywhere] * 5,
        out_shape=[
            shape((chunks, spans, depth, columns), LOW),
            shape((spans, depth, out.shape[1]), LOW),
            shape((spans, depth, proj.shape[1]), LOW),
            shape((rows, width), LOW),
            shape((rows, width), LOW),
            shape(gains.shape, WIDE),
            shape((chunks, spans, depth, columns), LOW),
            shape((spans, depth, out.shape[1]), LOW),
            shape((spans, depth, proj.shape[1]), LOW),
            shape((rows, width), LOW),
            shape((strips, 2, piece, strip), LOW),
        ],
        scratch_shapes=[
            pltpu.VMEM((SLOTS, width, columns), LOW),
            pltpu.VMEM((2, depth, columns), LOW),
            pltpu.VMEM((2, 2, half, strip), LOW),
            pltpu.VMEM((2, 2, half, strip), LOW),
            pltpu.VMEM((2, half, strip), WIDE),
            pltpu.VMEM((strips, piece, strip), WIDE),
            pltpu.VMEM((strips, 2, piece, strip), LOW),
            pltpu.VMEM((strips, 2, piece, strip), LOW),
            pltpu.VMEM((strips, 1, piece, strip), LOW),
            pltpu.VMEM((2, strips, piece, strip), LOW),
            pltpu.VMEM((piece, width), WIDE),
            pltpu.VMEM((piece, width), WIDE),
            pltpu.VMEM((piece, width), WIDE),
            pltpu.VMEM((piece, width), LOW),
            pltpu.VMEM((piece, width), LOW),
            pltpu.VMEM((steps + 1,) + gains.shape, WIDE),
            pltpu.VMEM((steps,) + gains.shape, WIDE),
            dma((chunks + 2, 2, spans)),
            dma((chunks + 2, 2, spans)),
            dma((chunks + 2, 3)),
            dma((2,)),
            dma((2,)),
            dma((3, strips)),
            dma((3, strips)),
            dma((2, strips)),
            dma((2, strips)),
            dma((9,)),
            dma((9,)),
            dma((steps,)),
            dma((steps,)),
            dma((10,)),
            dma((2, chunks)),
            dma((9,)),
            pltpu.SemaphoreType.REGULAR,
        ],
        compiler_params=pltpu.CompilerParams(
            collective_id=1, has_side_effects=True, vmem_limit_bytes=63 * MEGABYTE
        ),
        name="feed_forward_and_back",
    )(
        normed, cot, other, hidden, normalized, proj, out, query, key, value, mixed, logsum, middle,
        x, cosine, sine, gains
    )


def adamw(weight, grad, first, second, rate, decay):
    first = BETA_ONE * first + (1.0 - BETA_ONE) * grad
    second = BETA_TWO * second + (1.0 - BETA_TWO) * grad * grad
    fixed_first = first / (1.0 - BETA_ONE**STEP)
    fixed_second = second / (1.0 - BETA_TWO**STEP)
    weight = weight - rate * (fixed_first / (jnp.sqrt(fixed_second) + ADAM_EPS) + decay * weight)
    return (first, second, weight)


def body(
    block_input,
    cotangent,
    positions,
    query_weight,
    keyval_weight,
    output_weight,
    gateup_weight,
    down_weight,
    norm_gains,
    query_first,
    keyval_first,
    output_first,
    gateup_first,
    down_first,
    gains_first,
    query_second,
    keyval_second,
    output_second,
    gateup_second,
    down_second,
    gains_second,
):
    count, length, width = block_input.shape
    rows = count * length
    depth = query_weight.shape[0]
    query_width = query_weight.shape[1]
    key_width = keyval_weight.shape[2]
    me = lax.axis_index("dp")
    pair_bit = (me // PAIR) % 2

    proj_block = jnp.concatenate(
        [query_weight.astype(LOW), keyval_weight.reshape(depth, 2 * key_width).astype(LOW)], axis=1
    )
    half_width = down_weight.shape[1] // 2
    chunk_width = half_width // CHUNKS
    hidden_block = jnp.concatenate(
        [
            part[:, None].reshape(depth, 2, CHUNKS, chunk_width)
            for part in (gateup_weight[:, 0], gateup_weight[:, 1], down_weight)
        ],
        axis=3,
    )
    hidden_block = hidden_block.astype(LOW).transpose(1, 2, 0, 3)
    gains_block = jnp.pad(norm_gains.astype(LOW).astype(WIDE), ((0, 6), (0, 0)))
    grad_out = cotangent.reshape(rows, width)
    heads, kv = query_width // HD, key_width // HD
    cosine, sine = angle_tables(positions.reshape(rows))
    signs = jnp.where(jnp.arange(HD) < HD // 2, -1.0, 1.0).astype(WIDE)
    cosine_pair = jnp.tile(cosine[:, 0], (1, 2))
    sine_pair = jnp.tile(sine[:, 0] * signs, (1, 2))
    (
        normalized,
        proj_full,
        output_full,
        gains_low,
        query,
        key,
        value,
        mixed_low,
        logsum,
        middle,
        hidden_full,
        other_out,
        normed_two,
    ) = first_half(
        block_input.reshape(rows, width),
        grad_out,
        proj_block,
        output_weight.astype(LOW),
        hidden_block,
        gains_block,
        cosine_pair,
        sine_pair,
        kv,
        count,
    )
    hidden_terms, output_terms, proj_terms, block_output, input_grad, gains_sum = second_half(
        normed_two,
        grad_out,
        other_out,
        hidden_full,
        normalized,
        proj_full,
        output_full,
        query,
        key,
        value,
        mixed_low,
        jnp.swapaxes(logsum, 1, 2),
        middle,
        block_input.reshape(rows, width),
        cosine_pair,
        sine_pair,
        gains_low,
        count,
    )[:6]
    block_output = block_output.astype(WIDE)
    input_grad = input_grad.astype(WIDE)
    gains_reduced = lax.dynamic_slice_in_dim(gains_sum[:2], me * depth, depth, 1)
    output_reduced = jnp.sum(output_terms.astype(WIDE), axis=0)
    proj_reduced = jnp.sum(proj_terms.astype(WIDE), axis=0)
    query_reduced = proj_reduced[:, :query_width]
    keyval_reduced = proj_reduced[:, query_width:].reshape(depth, 2, key_width)
    mine = jnp.sum(hidden_terms[:, 0::2].astype(WIDE), axis=1)
    other = jnp.sum(hidden_terms[:, 1::2].astype(WIDE), axis=1)

    def hidden_columns(index):
        columns = slice(index * chunk_width, (index + 1) * chunk_width)
        return join(
            jnp.concatenate([mine[c, :, columns] for c in range(CHUNKS)], axis=1),
            jnp.concatenate([other[c, :, columns] for c in range(CHUNKS)], axis=1),
            pair_bit,
            1,
        )

    gateup_reduced = jnp.stack([hidden_columns(0), hidden_columns(1)], axis=1)
    down_reduced = hidden_columns(2)
    query_mean, query_square, query_next = adamw(
        query_weight, query_reduced, query_first, query_second, MATRIX_RATE, WEIGHT_DECAY
    )
    keyval_mean, keyval_square, keyval_next = adamw(
        keyval_weight, keyval_reduced, keyval_first, keyval_second, MATRIX_RATE, WEIGHT_DECAY
    )
    output_mean, output_square, output_next = adamw(
        output_weight, output_reduced, output_first, output_second, MATRIX_RATE, WEIGHT_DECAY
    )
    gateup_mean, gateup_square, gateup_next = adamw(
        gateup_weight, gateup_reduced, gateup_first, gateup_second, MATRIX_RATE, WEIGHT_DECAY
    )
    down_mean, down_square, down_next = adamw(
        down_weight, down_reduced, down_first, down_second, MATRIX_RATE, WEIGHT_DECAY
    )
    gains_mean, gains_square, gains_next = adamw(
        norm_gains, gains_reduced, gains_first, gains_second, GAIN_RATE, 0.0
    )
    return (
        block_output.reshape(count, length, width),
        input_grad.reshape(count, length, width),
        query_reduced,
        keyval_reduced,
        output_reduced,
        gateup_reduced,
        down_reduced,
        gains_reduced,
        query_mean,
        keyval_mean,
        output_mean,
        gateup_mean,
        down_mean,
        gains_mean,
        query_square,
        keyval_square,
        output_square,
        gateup_square,
        down_square,
        gains_square,
        query_next,
        keyval_next,
        output_next,
        gateup_next,
        down_next,
        gains_next,
    )


def solution(mesh):
    in_specs = (
        P("dp", None, None),
        P("dp", None, None),
        P("dp", None),
        P("dp", "tensor"),
        P("dp", None, "tensor"),
        P("dp", "tensor"),
        P("dp", None, "tensor"),
        P("dp", "tensor"),
        P(None, "dp"),
        P("dp", "tensor"),
        P("dp", None, "tensor"),
        P("dp", "tensor"),
        P("dp", None, "tensor"),
        P("dp", "tensor"),
        P(None, "dp"),
        P("dp", "tensor"),
        P("dp", None, "tensor"),
        P("dp", "tensor"),
        P("dp", None, "tensor"),
        P("dp", "tensor"),
        P(None, "dp"),
    )
    out_specs = (
        P("dp", None, None),
        P("dp", None, None),
        P("dp", "tensor"),
        P("dp", None, "tensor"),
        P("dp", "tensor"),
        P("dp", None, "tensor"),
        P("dp", "tensor"),
        P(None, "dp"),
        P("dp", "tensor"),
        P("dp", None, "tensor"),
        P("dp", "tensor"),
        P("dp", None, "tensor"),
        P("dp", "tensor"),
        P(None, "dp"),
        P("dp", "tensor"),
        P("dp", None, "tensor"),
        P("dp", "tensor"),
        P("dp", None, "tensor"),
        P("dp", "tensor"),
        P(None, "dp"),
        P("dp", "tensor"),
        P("dp", None, "tensor"),
        P("dp", "tensor"),
        P("dp", None, "tensor"),
        P("dp", "tensor"),
        P(None, "dp"),
    )
    return jax.shard_map(body, mesh=mesh, in_specs=in_specs, out_specs=out_specs, check_vma=False)
```

```python
import functools
import math

import jax
import jax.numpy as jnp
from jax import lax
from jax.experimental import pallas as pl
from jax.experimental.pallas import tpu as pltpu
from jax.sharding import PartitionSpec as P

HD = 64
STEP = 10

NORM_EPS = 1e-05
ROPE_BASE = 500000.0
BETA_ONE = 0.9
BETA_TWO = 0.95
ADAM_EPS = 1e-08
MATRIX_RATE = 0.05
GAIN_RATE = 0.6
WEIGHT_DECAY = 0.1
MASKED = -1e30

PAIR = 2
CHUNKS = 4

LOW = jnp.bfloat16
WIDE = jnp.float32
ROWS_BY_ROWS = (((1,), (1,)), ((), ()))
COLUMNS_BY_COLUMNS = (((0,), (0,)), ((), ()))


def dot(left, right, dims=(((1,), (0,)), ((), ()))):
    return lax.dot_general(left, right, dims, preferred_element_type=WIDE)


def swap(values, axis, mask):
    pairs = [(k, k ^ mask) for k in range(lax.axis_size(axis))]
    return lax.ppermute(values, axis, pairs)


def part(values, index, parts, dim):
    size = values.shape[dim] // parts
    return lax.dynamic_slice_in_dim(values, index * size, size, dim)


def join(mine, other, bit, dim):
    first = jnp.concatenate([mine, other], axis=dim)
    second = jnp.concatenate([other, mine], axis=dim)
    return jnp.where(bit == 0, first, second)


def angle_tables(positions):
    half_steps = jnp.arange(HD // 2, dtype=WIDE)
    frequency = jnp.exp(half_steps * (-2.0 / HD) * math.log(ROPE_BASE))
    angles = positions.astype(WIDE)[..., None] * frequency
    cosine = jnp.cos(angles)
    sine = jnp.sin(angles)
    return (
        jnp.concatenate([cosine, cosine], axis=-1)[..., None, :],
        jnp.concatenate([sine, sine], axis=-1)[..., None, :],
    )


def rotate(values, cosine, sine):
    middle_index = values.shape[-1] // 2
    turned = jnp.concatenate([-values[..., middle_index:], values[..., :middle_index]], axis=-1)
    return values * cosine + turned * sine


def rms_factor(values):
    return lax.rsqrt(jnp.mean(values * values, axis=-1, keepdims=True) + NORM_EPS)


def rms_backward(values, gain, grad):
    factor = rms_factor(values)
    scaled = grad * gain
    inner = jnp.mean(scaled * values, axis=-1, keepdims=True)
    grad_values = factor * scaled - values * (factor * factor * factor * inner)
    grad_gain = jnp.sum(grad * values * factor, axis=0)
    return grad_values, grad_gain


def attend_group(j, group, block, count, length, query_ref, key_ref, value_ref, mixed_ref, logsum_ref):
    row_index = lax.broadcasted_iota(jnp.int32, (block, block), 0)
    column_index = lax.broadcasted_iota(jnp.int32, (block, block), 1)
    allowed = column_index <= row_index
    for sequence in range(count):
        base = sequence * length
        for head in range(group):
            columns = slice((j * group + head) * HD, (j * group + head + 1) * HD)
            for start in range(base, base + length, block):
                rows = slice(start, start + block)
                before = slice(base, start)
                query = query_ref[rows, columns] * HD ** (-0.5)
                last = jnp.where(allowed, dot(query, key_ref[j, rows], ROWS_BY_ROWS), MASKED)
                highest = jnp.max(last, axis=-1, keepdims=True)
                if start > base:
                    early = dot(query, key_ref[j, before], ROWS_BY_ROWS)
                    highest = jnp.maximum(highest, jnp.max(early, axis=-1, keepdims=True))
                    early = jnp.exp(early - highest)
                last = jnp.exp(last - highest)
                total = jnp.sum(last, axis=-1, keepdims=True)
                if start > base:
                    total = total + jnp.sum(early, axis=-1, keepdims=True)
                share = 1.0 / total
                mixed = dot((last * share).astype(LOW), value_ref[j, rows])
                if start > base:
                    mixed = mixed + dot((early * share).astype(LOW), value_ref[j, before])
                mixed_ref[rows, columns] = mixed.astype(LOW)
                logsum_ref[j, rows, head : head + 1] = highest + jnp.log(total)


MESH = pl.DeviceIdType.MESH
MEGABYTE = 1 << 20


def flip(index, mask):
    bit = 1
    while bit <= mask:
        if mask & bit:
            index = index + bit - 2 * bit * lax.rem(lax.div(index, bit), 2)
        bit *= 2
    return index


def remote(source, target, sems, axis, mask):
    return pltpu.make_async_remote_copy(
        src_ref=source,
        dst_ref=target,
        send_sem=sems[0],
        recv_sem=sems[1],
        device_id={axis: flip(lax.axis_index(axis), mask)},
        device_id_type=MESH,
    )


def greet(partners):
    barrier = pltpu.get_barrier_semaphore()
    for axis, mask in partners:
        pl.semaphore_signal(
            barrier,
            inc=1,
            device_id={axis: flip(lax.axis_index(axis), mask)},
            device_id_type=MESH,
        )
    pl.semaphore_wait(barrier, len(partners))


class Gather:
    def __init__(self, masks, source, place, sems):
        self.masks, self.source, self.place, self.sems = masks, source, place, sems
        self.me = lax.axis_index("dp")

    def sem(self, phase, mask):
        send, recv = self.sems
        return send.at[phase, mask // 2], recv.at[phase, mask // 2]

    def far_copy(self, mask):
        return remote(self.source(mask), self.place(self.me), self.sem(0, mask), "dp", mask)

    def near_copy(self, mask):
        here = self.place(flip(self.me, mask))
        return remote(here if mask else self.source(0), here, self.sem(1, mask), "dp", 1)

    def start(self):
        for mask in self.masks[1:]:
            self.far_copy(mask).start()

    def start_own(self):
        self.near_copy(0).start()

    def forward(self, mask):
        here = self.place(flip(self.me, mask))
        remote(here, here, self.sem(0, mask), "dp", mask).wait_recv()
        self.near_copy(mask).start()

    def arrive(self):
        for mask in self.masks:
            here = self.place(flip(self.me, mask ^ 1))
            remote(here, here, self.sem(1, mask), "dp", 1).wait_recv()

    def drain(self):
        for mask in self.masks[1:]:
            self.far_copy(mask).wait_send()
        for mask in self.masks:
            self.near_copy(mask).wait_send()


def rotated(values, cosine, sine, first):
    width = values.shape[1]
    turned = jnp.where(
        first, pltpu.roll(values, width - HD // 2, 1), pltpu.roll(values, HD // 2, 1)
    )
    return values * cosine + turned * sine


SLOTS = 2


class Scatter:
    def __init__(self, masks, product, landing, terms, stage, sems):
        self.masks, self.product, self.landing, self.terms = masks, product, landing, terms
        self.stage, self.sems = stage, sems
        self.me = lax.axis_index("dp")
        self.depth = product.shape[0] // lax.axis_size("dp")

    def rows(self, owner):
        return pl.ds(pl.multiple_of(owner * self.depth, self.depth), self.depth)

    def copy(self, phase, mask, source, target):
        send, recv, _ = self.sems
        at = mask // 2
        axis_mask = 1 if phase == 0 else mask
        return remote(source, target, (send.at[phase, at], recv.at[phase, at]), "dp", axis_mask)

    def start(self):
        for mask in self.masks[1:] + [0]:
            self.near_copy(mask).start()

    def near_copy(self, mask):
        source = self.product.at[self.rows(flip(self.me, mask ^ 1))]
        return self.copy(0, mask, source, self.landing.at[mask // 2])

    def load_copy(self, index, mask):
        return pltpu.make_async_copy(
            self.landing.at[mask // 2], self.stage.at[index % 2], self.sems[2].at[index % 2]
        )

    def store_copy(self, index, mask):
        target = self.landing.at[mask // 2] if mask else self.terms.at[0]
        return pltpu.make_async_copy(
            self.stage.at[index % 2], target, self.sems[2].at[2 + index % 2]
        )

    def far_copy(self, mask):
        return self.copy(1, mask, self.landing.at[mask // 2], self.terms.at[mask // 2])

    def steps(self):
        order = self.masks[1:] + [0]
        for step in range(len(order) + 2):
            if step >= 2:
                mask = order[step - 2]
                self.store_copy(step - 2, mask).wait()
                if mask:
                    self.far_copy(mask).start()
            if step < len(order):
                mask = order[step]
                landed = self.landing.at[mask // 2]
                self.copy(0, mask, landed, landed).wait_recv()
                self.load_copy(step, mask).start()
            if 1 <= step <= len(order):
                mask = order[step - 1]
                slot = (step - 1) % 2
                self.load_copy(step - 1, mask).wait()
                at = self.rows(flip(self.me, mask))
                total = self.product[at].astype(WIDE) + self.stage[slot].astype(WIDE)
                self.stage[slot] = total.astype(LOW)
                self.store_copy(step - 1, mask).start()
            yield

    def pump(self):
        for _ in self.steps():
            pass

    def free(self):
        for mask in self.masks:
            self.near_copy(mask).wait_send()

    def release(self):
        for mask in self.masks[1:]:
            self.far_copy(mask).wait_send()

    def arrive(self):
        for mask in self.masks[1:]:
            landed = self.terms.at[mask // 2]
            self.copy(1, mask, landed, landed).wait_recv()


def attend_back_group(
    j,
    group,
    block,
    count,
    length,
    query_ref,
    key_ref,
    value_ref,
    logsum_ref,
    grad_ref,
    query_grad_ref,
    key_grad_ref,
    value_grad_ref,
):
    key_index = lax.broadcasted_iota(jnp.int32, (block, block), 0)
    query_index = lax.broadcasted_iota(jnp.int32, (block, block), 1)
    allowed = key_index <= query_index
    scale = HD ** (-0.5)
    for sequence in range(count):
        base = sequence * length
        for head in range(group):
            columns = slice((j * group + head) * HD, (j * group + head + 1) * HD)
            for start in range(base, base + length, block):
                rows = slice(start, start + block)
                query = query_ref[rows, columns] * scale
                grad = grad_ref[rows, columns]
                logsum = logsum_ref[j, head : head + 1, rows]
                spans = [(rows, True)]
                if start > base:
                    spans.append((slice(base, start), False))
                probs, grad_probs = [], []
                for span, masked in spans:
                    scores = dot(key_ref[j, span], query, ROWS_BY_ROWS)
                    if masked:
                        scores = jnp.where(allowed, scores, MASKED)
                    probs.append(jnp.exp(scores - logsum))
                    grad_probs.append(dot(value_ref[j, span], grad, ROWS_BY_ROWS))
                inner = sum(
                    jnp.sum(one * two, axis=0, keepdims=True)
                    for one, two in zip(probs, grad_probs)
                )
                query_grad = None
                for (span, _), one, two in zip(spans, probs, grad_probs):
                    grad_scores = (one * (two - inner)).astype(LOW)
                    term = dot(grad_scores, key_ref[j, span], COLUMNS_BY_COLUMNS)
                    query_grad = term if query_grad is None else query_grad + term
                    key_grad_ref[j, span] += dot(grad_scores, query)
                    value_grad_ref[j, span] += dot(one.astype(LOW), grad)
                query_grad_ref[rows, columns] = query_grad * scale


def whole_kernel(
    sizes,
    x_ref,
    cot_ref,
    proj_ref,
    out_ref,
    hidden_ref,
    gains_ref,
    cosine_ref,
    sine_ref,
    hidden_terms,
    out_terms,
    proj_terms,
    output_ref,
    input_grad_ref,
    gains_sum,
    hidden_full,
    proj_full,
    out_full,
    other_cot,
    both_ref,
    hidden_land,
    out_land,
    proj_land,
    middle_low,
    line_land,
    saved_normalized,
    saved_query,
    saved_key,
    saved_value,
    saved_mixed,
    saved_middle,
    product,
    stage,
    core_out,
    core_in,
    held,
    keep,
    line_out,
    line_in,
    last_in,
    pair_in,
    flat,
    middle,
    low_out,
    logsums,
    gains_slots,
    gains_full,
    gain_rows,
    gain_blocks,
    gain_land,
    gain_part,
    tensor_land,
    gather_send,
    gather_recv,
    weight_send,
    weight_recv,
    token_send,
    token_recv,
    scatter_send,
    scatter_recv,
    scatter_local,
    core_send,
    core_recv,
    line_send,
    line_recv,
    pair_send,
    pair_recv,
    spread_send,
    spread_recv,
    gain_send,
    gain_recv,
    tensor_send,
    tensor_recv,
    own_sem,
    load_sem,
    save_sem,
    strip_sem,
    local_sem,
    credit,
):
    count, length = sizes
    rows, width = cot_ref.shape
    devices = lax.axis_size("dp")
    masks = list(range(0, devices, 2))
    me = lax.axis_index("dp")
    tensor = lax.axis_index("tensor")
    core, line = lax.rem(tensor, 2), lax.div(tensor, 2)
    pair_bit = lax.rem(lax.div(me, PAIR), 2)
    depth = proj_ref.shape[0]
    chunks = hidden_full.shape[0]
    unit = hidden_full.shape[2] // 3
    half, piece = rows // 2, rows // 4
    strips, strip = keep.shape[0], keep.shape[2]
    query_width = saved_query.shape[1]
    kv = saved_key.shape[0]
    group = query_width // (kv * HD)
    block = min(256, length)
    greet(
        [("dp", mask) for mask in range(1, devices)] + [("tensor", mask) for mask in range(1, 4)]
    )

    def block_rows(ref):
        return lambda owner: ref.at[pl.ds(pl.multiple_of(owner * depth, depth), depth)]

    def pair_half(mask):
        return pair_bit if not mask & PAIR else 1 - pair_bit

    def gather(index, ref, place_of):
        sems = gather_send.at[index], gather_recv.at[index]
        return Gather(masks, lambda mask: ref, place_of, sems)

    gains = gather(0, gains_ref, lambda owner: gains_slots.at[owner])
    proj_in = gather(1, proj_ref, block_rows(proj_full))
    out_in = gather(2, out_ref, block_rows(out_full))
    hidden_in = [
        Gather(
            masks,
            lambda mask, c=c: hidden_ref.at[pair_half(mask), c],
            block_rows(hidden_full.at[c]),
            (weight_send.at[c], weight_recv.at[c]),
        )
        for c in range(chunks)
    ]

    def own_copy(index):
        one = ([gains, proj_in, out_in] + hidden_in)[index]
        return pltpu.make_async_copy(one.source(0), one.place(me), own_sem.at[index])

    def pump(c):
        for mask in masks[1:]:
            hidden_in[c].forward(mask)

    quarter = pl.ds(pl.multiple_of(core * half + line * piece, piece), piece)
    near_half = pl.multiple_of(core * half, half)
    far_half = pl.multiple_of((1 - core) * half, half)
    near_line = pl.ds(pl.multiple_of(line * piece, piece), piece)
    far_line = pl.ds(pl.multiple_of((1 - line) * piece, piece), piece)

    def place(ref, core_at, line_at):
        return ref.at[pl.ds(pl.multiple_of(core_at * half + line_at * piece, piece), piece)]

    near_ref, far_ref = both_ref.at[0], both_ref.at[1]

    def token_ends(index):
        cot_near, cot_there = place(other_cot, core, line), place(other_cot, core, 1 - line)
        near, near_there = place(near_ref, core, line), place(near_ref, core, 1 - line)
        far, far_there = place(far_ref, core, line), place(far_ref, core, 1 - line)
        return [
            lambda: (place(cot_ref, core, line), cot_near, "dp", PAIR, cot_near),
            lambda: (cot_near, cot_near, "tensor", 2, cot_there),
            lambda: (cot_near, cot_near, "tensor", 1, place(other_cot, 1 - core, line)),
            lambda: (cot_there, cot_there, "tensor", 1, place(other_cot, 1 - core, 1 - line)),
            lambda: (low_out, far, "dp", PAIR, far),
            lambda: (low_out, near, "tensor", 2, near_there),
            lambda: (low_out, near, "tensor", 1, place(near_ref, 1 - core, line)),
            lambda: (near_there, near_there, "tensor", 1, place(near_ref, 1 - core, 1 - line)),
            lambda: (far, far, "tensor", 2, far_there),
            lambda: (far, far, "tensor", 1, place(far_ref, 1 - core, line)),
            lambda: (far_there, far_there, "tensor", 1, place(far_ref, 1 - core, 1 - line)),
        ][index]()

    def token(index):
        source, target, axis, mask, _ = token_ends(index)
        sems = token_send.at[index], token_recv.at[index]
        return remote(source, target, sems, axis, mask)

    def token_arrive(*indices):
        for index in indices:
            _, _, axis, mask, landed = token_ends(index)
            sems = token_send.at[index], token_recv.at[index]
            remote(landed, landed, sems, axis, mask).wait_recv()

    def scatter(index, product_ref, landing, terms):
        columns = landing.shape[2]
        return Scatter(
            masks,
            product_ref,
            landing,
            terms,
            stage.at[:, :, :columns] if columns < stage.shape[2] else stage,
            (scatter_send.at[index], scatter_recv.at[index], scatter_local.at[index]),
        )

    hidden = [
        scatter(c, product.at[c % SLOTS], hidden_land.at[c], hidden_terms.at[c]) for c in range(chunks)
    ]

    def core_copy(slot, parts):
        return remote(
            core_out.at[slot, pl.ds(0, parts)],
            core_in.at[slot, pl.ds(0, parts)],
            (core_send.at[slot], core_recv.at[slot]),
            "tensor",
            1,
        )

    def line_copy(turn, s, parts, landing, source=line_out):
        return remote(
            source.at[s, pl.ds(0, parts)],
            landing.at[s],
            (line_send.at[turn, s], line_recv.at[turn, s]),
            "tensor",
            2,
        )

    def pair_copy(turn, s, landing):
        return remote(
            line_out.at[s, 1],
            landing.at[s],
            (pair_send.at[turn, s], pair_recv.at[turn, s]),
            "dp",
            PAIR,
        )

    def reduce_strips(
        turn, parts, term, prepare, landing, source=line_out, kept=keep, between=()
    ):
        def finish(s, slot):
            core_copy(slot, parts).wait_recv()
            near = []
            for q in range(parts):
                source[s, q] = (
                    held[q, far_line] + core_in[slot, q, far_line].astype(WIDE)
                ).astype(LOW)
                near.append(held[q, near_line] + core_in[slot, q, near_line].astype(WIDE))
            kept[s] = near[0]
            if parts == 2:
                flat[:, pl.ds(pl.multiple_of(s * strip, strip), strip)] = near[1]
            pl.semaphore_signal(
                credit, inc=1, device_id={"tensor": flip(tensor, 1)}, device_id_type=MESH
            )
            line_copy(turn, s, parts, landing, source).start()

        def one_strip(s, carry):
            slot = lax.rem(s, 2)
            prepare(s, slot)

            @pl.when(s >= 2)
            def _():
                core_copy(slot, parts).wait_send()

            for q in range(parts):
                core_out[slot, q] = term(q, far_half, s, slot).astype(LOW)
            if turn:
                pl.semaphore_wait(credit, 1)
            else:

                @pl.when(s >= 2)
                def _():
                    pl.semaphore_wait(credit, 1)

            core_copy(slot, parts).start()

            @pl.when(s >= 1)
            def _():
                finish(s - 1, 1 - slot)

            for q in range(parts):
                held[q] = term(q, near_half, s, slot)
            return carry

        cuts = [strips * cut // (len(between) + 1) for cut in range(len(between) + 2)]
        for first, last, step in zip(cuts[:-1], cuts[1:], list(between) + [None]):
            lax.fori_loop(first, last, one_strip, 0)
            if step is not None:
                step()
        finish(strips - 1, (strips - 1) % 2)
        for slot in range(2):
            core_copy(slot, parts).wait_send()

    def strip_loads(s, slot):
        return [
            pltpu.make_async_copy(
                hidden_full.at[c, pl.ds(pl.multiple_of(s * strip, strip), strip)],
                weights.at[pl.ds(pl.multiple_of((slot * chunks + c) * strip, strip), strip)],
                strip_sem.at[slot, c],
            )
            for c in range(chunks)
        ]

    def start_strip(s, slot):
        for copy in strip_loads(s, slot):
            copy.start()

    def prepare_strip(s, slot):
        @pl.when(s + 1 < strips)
        def _():
            start_strip(s + 1, 1 - slot)

        for copy in strip_loads(s, slot):
            copy.wait()

    def hidden_term(ref, first, wide):
        def term(q, start, s, slot):
            at = pl.ds(pl.multiple_of(q * rows + start, half), half)
            total = None
            for c in range(chunks):
                block = weights[
                    pl.ds(pl.multiple_of((slot * chunks + c) * strip, strip), strip),
                    first : first + wide,
                ]
                one = dot(ref[at, c * wide : (c + 1) * wide], block, ROWS_BY_ROWS)
                total = one if total is None else total + one
            return total

        return term

    def to_pair(turn, landing):
        if landing is not line_in:
            for s in range(strips):
                line_copy(turn, s, 2, landing).wait_recv()
            copy = pltpu.make_async_copy(landing, line_in, load_sem.at[0])
            copy.start()
            copy.wait()
        for s in range(strips):
            copy = line_copy(turn, s, 2, landing)
            if landing is line_in:
                copy.wait_recv()
            copy.wait_send()
            columns = slice(s * strip, (s + 1) * strip)
            line_out[s, 1] = (flat[:, columns] + line_in[s, 1].astype(WIDE)).astype(LOW)
            pair_copy(turn - 1, s, pair_in.at[turn - 1]).start()
            flat[:, columns] = keep[s] + line_in[s, 0].astype(WIDE)

    def from_pair(turn):
        for s in range(strips):
            copy = pair_copy(turn - 1, s, pair_in.at[turn - 1])
            copy.wait_recv()
            copy.wait_send()
            flat[:, s * strip : (s + 1) * strip] += pair_in[turn - 1, s].astype(WIDE)

    tile = min(64, piece)

    def rms_back(values_of, gain, grads_of, store, gain_row):
        def one_tile(index, total):
            at = pl.ds(pl.multiple_of(index * tile, tile), tile)
            there = pl.ds(pl.multiple_of(core * half + line * piece + index * tile, tile), tile)
            values, grads = values_of(at), grads_of(at)
            grad_values, grad_gain = rms_backward(values, gain, grads)
            store(at, there, grad_values)
            return total + grad_gain[None]

        zero = jnp.zeros((1, width), WIDE)
        gain_rows[gain_row : gain_row + 1] = lax.fori_loop(0, piece // tile, one_tile, zero)

    def spread_copy(index, source, target, mask):
        return remote(
            source, target, (spread_send.at[index], spread_recv.at[index]), "tensor", mask
        )

    def spread(base, source, target):
        here = place(target, core, line)
        spread_copy(base, source, here, 2).start()
        spread_copy(base + 1, source, here, 1).start()
        pltpu.make_async_copy(source, here, local_sem.at[base]).start()

    def spread_on(base, target):
        there = place(target, core, 1 - line)
        spread_copy(base, there, there, 2).wait_recv()
        spread_copy(base + 2, there, there, 1).start()

    def spread_release(base, source, target):
        here, there = place(target, core, line), place(target, core, 1 - line)
        spread_copy(base, source, here, 2).wait_send()
        spread_copy(base + 1, source, here, 1).wait_send()
        spread_copy(base + 2, there, there, 1).wait_send()
        pltpu.make_async_copy(source, here, local_sem.at[base]).wait()

    def spread_end(base, target):
        near, far = place(target, 1 - core, line), place(target, 1 - core, 1 - line)
        spread_copy(base + 1, near, near, 1).wait_recv()
        spread_copy(base + 2, far, far, 1).wait_recv()

    def gain_copy(mask):
        return remote(
            gain_blocks.at[flip(me, mask)],
            gain_land.at[mask],
            (gain_send.at[mask], gain_recv.at[mask]),
            "dp",
            mask,
        )

    def tensor_copy(mask):
        return remote(
            gain_part,
            tensor_land.at[mask],
            (tensor_send.at[mask], tensor_recv.at[mask]),
            "tensor",
            mask,
        )

    def lanes_turned(values, cosine, sine):
        times = values.shape[1] // cosine.shape[1]
        lanes = lax.broadcasted_iota(jnp.int32, values.shape, 1)
        return rotated(
            values,
            jnp.concatenate([cosine] * times, axis=1),
            jnp.concatenate([sine] * times, axis=1),
            lax.rem(lanes, HD) < HD // 2,
        ).astype(LOW)

    tokens = min(256, rows)

    def tile_at(index, size):
        return pl.ds(pl.multiple_of(index * size, size), size)

    gains.start()
    proj_in.start()
    gains.start_own()
    proj_in.start_own()
    for index in range(3 + chunks):
        own_copy(index).start()

    def attention(
        x, normalized, proj, out, query, key, value, mixed, logsum, cosines, sines
    ):
        loads = [
            pltpu.make_async_copy(source, target, load_sem.at[index])
            for index, (source, target) in enumerate(
                [(x_ref, x), (cosine_ref, cosines), (sine_ref, sines)]
            )
        ]
        for copy in loads:
            copy.start()
        logsum[...] = jnp.zeros_like(logsum)
        for mask in masks[1:]:
            gains.forward(mask)
        proj_in.forward(masks[1])
        out_in.start()
        out_in.start_own()
        gains.arrive()
        own_copy(0).wait()
        gains_full[...] = jnp.concatenate([gains_slots[j] for j in range(devices)], axis=1)
        for copy in loads:
            copy.wait()

        def norm_tile(index, carry):
            at = tile_at(index, tokens)
            values = x[at].astype(WIDE)
            normalized[at] = (values * rms_factor(values) * gains_full[0:1]).astype(LOW)
            return carry

        lax.fori_loop(0, rows // tokens, norm_tile, 0)
        saves = [
            pltpu.make_async_copy(source, target, save_sem.at[index])
            for index, (source, target) in enumerate(
                [
                    (normalized, saved_normalized),
                    (query, saved_query),
                    (key, saved_key),
                    (value, saved_value),
                    (mixed, saved_mixed),
                    (middle, saved_middle),
                ]
            )
        ]
        saves[0].start()
        for mask in masks[2:]:
            proj_in.forward(mask)
            if mask == masks[2]:
                token(0).start()
                hidden_in[0].start()
        hidden_in[1].start()
        hidden_in[0].start_own()
        hidden_in[1].start_own()
        proj_in.arrive()
        own_copy(1).wait()
        load_proj = pltpu.make_async_copy(proj_full, proj, load_sem.at[3])
        load_proj.start()
        load_proj.wait()

        def project_tile(index, carry):
            at = tile_at(index, tokens)
            pre = dot(normalized[at], proj[...])
            cosine, sine = cosines[at], sines[at]
            query[at] = lanes_turned(pre[:, :query_width], cosine, sine)
            keys = lanes_turned(pre[:, query_width : query_width + kv * HD], cosine, sine)
            values = pre[:, query_width + kv * HD :].astype(LOW)
            for j in range(kv):
                key[j, at] = keys[:, j * HD : (j + 1) * HD]
                value[j, at] = values[:, j * HD : (j + 1) * HD]
            return carry

        lax.fori_loop(0, rows // tokens, project_tile, 0)
        for copy in saves[1:4]:
            copy.start()
        for j in range(kv):
            attend_group(j, group, block, count, length, query, key, value, mixed, logsum)
            if j == 0:
                token_arrive(0)
                token(1).start()
                token(2).start()
                for mask in masks[1:]:
                    out_in.forward(mask)
        saves[4].start()
        for j in range(kv):
            logsums[j] = logsum[j].T[: logsums.shape[1]]
        out_in.arrive()
        own_copy(2).wait()
        load_out = pltpu.make_async_copy(out_full, out, load_sem.at[4])
        load_out.start()
        load_out.wait()

        def out_term(q, start, s, slot):
            return dot(
                mixed[pl.ds(start, half)],
                out[pl.ds(pl.multiple_of(s * strip, strip), strip)],
                ROWS_BY_ROWS,
            )

        reduce_strips(0, 1, out_term, lambda s, slot: None, last_in)
        pump(0)
        for s in range(strips):
            copy = line_copy(0, s, 1, last_in)
            copy.wait_recv()
            copy.wait_send()
            columns = slice(s * strip, (s + 1) * strip)
            middle[:, columns] = (
                x[quarter, columns].astype(WIDE) + keep[s] + last_in[s, 0].astype(WIDE)
            )
        saves[5].start()
        values = middle[...]
        low_out[...] = (values * rms_factor(values) * gains_full[1:2]).astype(LOW)
        for index in (4, 5, 6):
            token(index).start()
        for c in range(2, chunks):
            hidden_in[c].start()
            hidden_in[c].start_own()
        for copy in saves:
            copy.wait()

    pl.run_scoped(
        attention,
        pltpu.VMEM((rows, width), LOW),
        pltpu.VMEM((rows, width), LOW),
        pltpu.VMEM(proj_full.shape, LOW),
        pltpu.VMEM(out_full.shape, LOW),
        pltpu.VMEM(saved_query.shape, LOW),
        pltpu.VMEM(saved_key.shape, LOW),
        pltpu.VMEM(saved_value.shape, LOW),
        pltpu.VMEM(saved_mixed.shape, LOW),
        pltpu.VMEM((kv, rows, 128), WIDE),
        pltpu.VMEM(cosine_ref.shape, WIDE),
        pltpu.VMEM(sine_ref.shape, WIDE),
    )

    weights = None

    def feed_forward(normed, grads, weights_ref, gate_ref, hidden_out):
        nonlocal weights
        weights = weights_ref
        load_cot = pltpu.make_async_copy(cot_ref, grads.at[pl.ds(0, rows)], load_sem.at[0])
        load_cot.start()
        place_own = pltpu.make_async_copy(low_out, place(near_ref, core, line), local_sem.at[1])
        place_own.start()
        pump(1)
        token_arrive(5)
        token(7).start()
        token_arrive(1)
        token(3).start()
        token_arrive(4)
        token(8).start()
        token(9).start()
        pump(2)
        place_own.wait()
        token_arrive(6, 7, 2, 3)
        loads = [
            load_cot,
            pltpu.make_async_copy(near_ref, normed.at[pl.ds(0, rows)], load_sem.at[1]),
            pltpu.make_async_copy(other_cot, grads.at[pl.ds(rows, rows)], load_sem.at[2]),
            pltpu.make_async_copy(far_ref, normed.at[pl.ds(rows, rows)], load_sem.at[3]),
        ]
        loads[1].start()
        loads[2].start()

        def load_weights(c):
            hidden_in[c].arrive()
            own_copy(3 + c).wait()
            copy = pltpu.make_async_copy(hidden_full.at[c], weights, load_sem.at[4])
            copy.start()
            return copy

        waiting = [load_weights(0)]
        token_arrive(8)
        token(10).start()
        token_arrive(9, 10)
        loads[3].start()
        for copy in loads:
            copy.wait()
        half_tokens = min(512, 2 * rows)

        def stage_one(c):
            (waiting.pop() if waiting else load_weights(c)).wait()

            def one_tile(index, carry):
                at = tile_at(index, half_tokens)
                gate_up = dot(normed[at], weights[:, : 2 * unit])
                grad_hidden = dot(grads[at], weights[:, 2 * unit :])
                gate, upward = gate_up[:, :unit], gate_up[:, unit:]
                sigma = jax.nn.sigmoid(gate)
                passed = gate * sigma
                hidden_out[at, c * unit : (c + 1) * unit] = (passed * upward).astype(LOW)
                grad_gate = grad_hidden * upward * sigma * (1.0 + gate * (1.0 - sigma))
                first = 2 * c * unit
                gate_ref[at, first : first + unit] = grad_gate.astype(LOW)
                gate_ref[at, first + unit : first + 2 * unit] = (grad_hidden * passed).astype(LOW)
                return carry

            lax.fori_loop(0, 2 * rows // half_tokens, one_tile, 0)

        columns = min(512, width)

        def stage_two(c):
            if c >= SLOTS:
                hidden[c - SLOTS].free()

            def one_tile(index, carry):
                at = pl.ds(pl.multiple_of(index * columns, columns), columns)
                gate_up = dot(
                    normed[:, at], gate_ref[:, 2 * c * unit : 2 * (c + 1) * unit], COLUMNS_BY_COLUMNS
                )
                down = dot(grads[:, at], hidden_out[:, c * unit : (c + 1) * unit], COLUMNS_BY_COLUMNS)
                product[c % SLOTS, at, : 2 * unit] = gate_up.astype(LOW)
                product[c % SLOTS, at, 2 * unit :] = down.astype(LOW)
                return carry

            lax.fori_loop(0, width // columns, one_tile, 0)
            hidden[c].start()

        gain_rows[...] = jnp.zeros_like(gain_rows)
        stage_one(0)
        waiting.append(load_weights(1))
        hidden_in[3].forward(masks[1])
        stage_one(1)
        hidden_in[3].forward(masks[2])
        stage_one(2)
        for mask in masks[3:]:
            hidden_in[3].forward(mask)
        stage_two(0)
        stage_one(3)
        start_strip(0, 0)
        early = hidden[0].steps()

        def pump_step():
            next(early)

        reduce_strips(
            1,
            2,
            hidden_term(gate_ref, 0, 2 * unit),
            prepare_strip,
            line_in,
            between=[pump_step] * 3,
        )
        for _ in early:
            pass
        stage_two(1)
        stage_two(2)
        to_pair(1, line_in)
        from_pair(1)
        for index in (4, 5, 6):
            token(index).wait_send()

        def store(at, there, grad_values):
            total = grads[there].astype(WIDE) + grad_values
            middle[at] = total
            low_out[at] = total.astype(LOW)

        rms_back(lambda at: middle[at], gains_full[1:2], lambda at: flat[at], store, 1)
        spread(0, low_out, middle_low)
        start_strip(0, 0)
        hidden[1].pump()
        stage_two(3)
        reduce_strips(2, 2, hidden_term(hidden_out, 2 * unit, unit), prepare_strip, line_land)
        spread_on(0, middle_low)

    pl.run_scoped(
        feed_forward,
        pltpu.VMEM((2 * rows, width), LOW),
        pltpu.VMEM((2 * rows, width), LOW),
        pltpu.VMEM((width, 3 * unit), LOW),
        pltpu.VMEM((2 * rows, 2 * unit * chunks), LOW),
        pltpu.VMEM((2 * rows, unit * chunks), LOW),
    )

    def second_phase(
        grads,
        out_weight,
        proj_weight,
        query,
        key,
        value,
        mixed,
        normalized,
        grad_mixed,
        query_grad,
        key_grad,
        value_grad,
        projected,
        out_product,
        proj_product,
        cosines,
        sines,
        last_out,
        last_keep,
        low_grad,
    ):
        sources = [out_full, saved_query, saved_key, saved_value, saved_mixed]
        sources += [proj_full, saved_normalized, cosine_ref, sine_ref]
        targets = [out_weight, query, key, value, mixed, proj_weight, normalized, cosines, sines]
        loads = [
            pltpu.make_async_copy(source, target, load_sem.at[index])
            for index, (source, target) in enumerate(zip(sources, targets))
        ]
        loads[0].start()
        key_grad[...] = jnp.zeros_like(key_grad)
        value_grad[...] = jnp.zeros_like(value_grad)
        spread_end(0, middle_low)
        spread_release(0, low_out, middle_low)
        hidden[2].pump()
        load_grads = pltpu.make_async_copy(middle_low, grads, load_sem.at[len(loads)])
        load_grads.start()
        for copy in loads[1:]:
            copy.start()
        loads[0].wait()
        load_grads.wait()
        def mixed_tile(index, carry):
            at = pl.ds(pl.multiple_of(index * tokens, tokens), tokens)
            grad_mixed[at] = dot(grads[at], out_weight[...]).astype(LOW)
            return carry

        lax.fori_loop(0, rows // tokens, mixed_tile, 0)
        for copy in loads[1:5]:
            copy.wait()
        columns = min(256, width)

        def out_tile(index, carry):
            at = pl.ds(pl.multiple_of(index * columns, columns), columns)
            out_product[at] = dot(grads[:, at], mixed[...], COLUMNS_BY_COLUMNS).astype(LOW)
            return carry

        lax.fori_loop(0, width // columns, out_tile, 0)
        out = scatter(chunks, out_product, out_land, out_terms)
        out.start()
        for j in range(kv):
            attend_back_group(
                j,
                group,
                block,
                count,
                length,
                query,
                key,
                value,
                logsums,
                grad_mixed,
                query_grad,
                key_grad,
                value_grad,
            )
        hidden[3].pump()
        for copy in loads[5:]:
            copy.wait()

        def turn_tile(index, carry):
            at = pl.ds(pl.multiple_of(index * tokens, tokens), tokens)
            cosine, sine = cosines[at], -sines[at]

            keys = jnp.concatenate([key_grad[j, at] for j in range(kv)], axis=1)
            values = jnp.concatenate([value_grad[j, at] for j in range(kv)], axis=1)
            projected[at, :query_width] = lanes_turned(query_grad[at], cosine, sine)
            projected[at, query_width : query_width + kv * HD] = lanes_turned(keys, cosine, sine)
            projected[at, query_width + kv * HD :] = values.astype(LOW)
            return carry

        lax.fori_loop(0, rows // tokens, turn_tile, 0)

        def proj_term(q, start, s, slot):
            return dot(
                projected[pl.ds(start, half)],
                proj_weight[pl.ds(pl.multiple_of(s * strip, strip), strip)],
                ROWS_BY_ROWS,
            )

        def proj_tile(index, carry):
            at = pl.ds(pl.multiple_of(index * columns, columns), columns)
            proj_product[at] = dot(normalized[:, at], projected[...], COLUMNS_BY_COLUMNS).astype(LOW)
            return carry

        lax.fori_loop(0, width // columns, proj_tile, 0)
        proj = scatter(chunks + 1, proj_product, proj_land, proj_terms)
        proj.start()
        reduce_strips(3, 1, proj_term, lambda s, slot: None, last_in, last_out, last_keep)
        to_pair(2, line_land)
        out.pump()
        load_x = pltpu.make_async_copy(x_ref.at[quarter], low_grad, load_sem.at[1])
        load_x.start()
        for s in range(strips):
            copy = line_copy(3, s, 1, last_in, last_out)
            copy.wait_recv()
            copy.wait_send()
        load_x.wait()

        def grads_of(at):
            return jnp.concatenate(
                [last_keep[s, at] + last_in[s, 0, at].astype(WIDE) for s in range(strips)], axis=1
            )

        def store(at, there, grad_values):
            low_out[at] = (middle[at] + grad_values).astype(LOW)

        rms_back(lambda at: low_grad[at].astype(WIDE), gains_full[0:1], grads_of, store, 0)
        spread(3, low_out, input_grad_ref)
        for owner in range(devices):
            gain_blocks[owner] = gain_rows[:, owner * depth : (owner + 1) * depth]
        for mask in range(1, devices):
            gain_copy(mask).start()

        again = [
            pltpu.make_async_copy(
                saved_middle.at[:, pl.ds(s * strip, strip)], last_keep.at[s], strip_sem.at[s % 2, s // 2]
            )
            for s in range(strips)
        ]
        for copy in again:
            copy.start()
        proj.pump()
        from_pair(2)
        for s, copy in enumerate(again):
            columns = slice(s * strip, (s + 1) * strip)
            copy.wait()
            low_grad[:, columns] = (last_keep[s] + flat[:, columns]).astype(LOW)
        spread(6, low_grad, output_ref)
        for mask in range(1, devices):
            gain_copy(mask).wait_recv()
        total = gain_blocks[me]
        for mask in range(1, devices):
            total = total + gain_land[mask]
        gain_part[...] = total
        for mask in range(1, 4):
            tensor_copy(mask).start()
        spread_on(3, input_grad_ref)
        for mask in range(1, 4):
            tensor_copy(mask).wait_recv()
        gains_sum[...] = gain_part[...] + tensor_land[1] + tensor_land[2] + tensor_land[3]
        spread_on(6, output_ref)
        for gather in hidden + [out, proj]:
            gather.arrive()
        for gather in hidden[chunks - SLOTS :] + [out, proj]:
            gather.free()
        for gather in hidden + [out, proj]:
            gather.release()
        for base, source, target in ((3, low_out, input_grad_ref), (6, low_grad, output_ref)):
            spread_end(base, target)
            spread_release(base, source, target)
        for mask in range(1, devices):
            gain_copy(mask).wait_send()
        for mask in range(1, 4):
            tensor_copy(mask).wait_send()
        for index in (0, 1, 2, 3, 7, 8, 9, 10):
            token(index).wait_send()
        for one in [gains, proj_in, out_in] + hidden_in:
            one.drain()
        pl.semaphore_wait(credit, 2)

    pl.run_scoped(
        second_phase,
        pltpu.VMEM((rows, width), LOW),
        pltpu.VMEM(out_full.shape, LOW),
        pltpu.VMEM(proj_full.shape, LOW),
        pltpu.VMEM(saved_query.shape, LOW),
        pltpu.VMEM(saved_key.shape, LOW),
        pltpu.VMEM(saved_value.shape, LOW),
        pltpu.VMEM(saved_mixed.shape, LOW),
        pltpu.VMEM((rows, width), LOW),
        pltpu.VMEM(saved_query.shape, LOW),
        pltpu.VMEM(saved_query.shape, WIDE),
        pltpu.VMEM(saved_key.shape, WIDE),
        pltpu.VMEM(saved_key.shape, WIDE),
        pltpu.VMEM((rows, proj_full.shape[1]), LOW),
        pltpu.VMEM(out_full.shape, LOW),
        pltpu.VMEM(proj_full.shape, LOW),
        pltpu.VMEM(cosine_ref.shape, WIDE),
        pltpu.VMEM(sine_ref.shape, WIDE),
        pltpu.VMEM((strips, 1, piece, strip), LOW),
        pltpu.VMEM((strips, piece, strip), WIDE),
        pltpu.VMEM((piece, width), LOW),
    )


def whole_layer(x, cot, proj, out, hidden, gains, cosine, sine, kv, count):
    rows, width = cot.shape
    devices = lax.axis_size("dp")
    spans = devices // 2
    depth = proj.shape[0]
    chunks = hidden.shape[1]
    assert chunks == 4
    columns = hidden.shape[3]
    query_width, proj_width = out.shape[1], proj.shape[1]
    half, piece = rows // 2, rows // 4
    strip = width // (2 * chunks)
    strips = width // strip
    vmem = pl.BlockSpec(memory_space=pltpu.VMEM)
    anywhere = pl.BlockSpec(memory_space=pl.ANY)
    shape = jax.ShapeDtypeStruct
    dma = pltpu.SemaphoreType.DMA
    low, wide = (lambda *sizes: pltpu.VMEM(sizes, LOW)), (lambda *sizes: pltpu.VMEM(sizes, WIDE))
    return pl.pallas_call(
        functools.partial(whole_kernel, (count, rows // count)),
        in_specs=[anywhere] * 5 + [vmem] + [anywhere] * 2,
        out_specs=[anywhere] * 5 + [vmem] + [anywhere] * 16,
        out_shape=[
            shape((chunks, spans, depth, columns), LOW),
            shape((spans, depth, query_width), LOW),
            shape((spans, depth, proj_width), LOW),
            shape((rows, width), LOW),
            shape((rows, width), LOW),
            shape((gains.shape[0], depth), WIDE),
            shape((chunks, width, columns), LOW),
            shape((width, proj_width), LOW),
            shape((width, query_width), LOW),
            shape((rows, width), LOW),
            shape((2, rows, width), LOW),
            shape((chunks, spans, depth, columns), LOW),
            shape((spans, depth, query_width), LOW),
            shape((spans, depth, proj_width), LOW),
            shape((rows, width), LOW),
            shape((strips, 2, piece, strip), LOW),
            shape((rows, width), LOW),
            shape((rows, query_width), LOW),
            shape((kv, rows, HD), LOW),
            shape((kv, rows, HD), LOW),
            shape((rows, query_width), LOW),
            shape((piece, width), WIDE),
        ],
        scratch_shapes=[
            low(SLOTS, width, columns),
            low(2, depth, columns),
            low(2, 2, half, strip),
            low(2, 2, half, strip),
            wide(2, half, strip),
            wide(strips, piece, strip),
            low(strips, 2, piece, strip),
            low(strips, 2, piece, strip),
            low(strips, 1, piece, strip),
            low(2, strips, piece, strip),
            wide(piece, width),
            wide(piece, width),
            low(piece, width),
            wide(kv, 8, rows),
            wide(devices, gains.shape[0], depth),
            wide(gains.shape[0], width),
            wide(gains.shape[0], width),
            wide(devices, gains.shape[0], depth),
            wide(devices, gains.shape[0], depth),
            wide(gains.shape[0], depth),
            wide(4, gains.shape[0], depth),
            dma((3, 2, spans)),
            dma((3, 2, spans)),
            dma((chunks, 2, spans)),
            dma((chunks, 2, spans)),
            dma((11,)),
            dma((11,)),
            dma((chunks + 2, 2, spans)),
            dma((chunks + 2, 2, spans)),
            dma((chunks + 2, 4)),
            dma((2,)),
            dma((2,)),
            dma((4, strips)),
            dma((4, strips)),
            dma((2, strips)),
            dma((2, strips)),
            dma((9,)),
            dma((9,)),
            dma((devices,)),
            dma((devices,)),
            dma((4,)),
            dma((4,)),
            dma((3 + chunks,)),
            dma((10,)),
            dma((6,)),
            dma((2, chunks)),
            dma((9,)),
            pltpu.SemaphoreType.REGULAR,
        ],
        compiler_params=pltpu.CompilerParams(
            collective_id=0, has_side_effects=True, vmem_limit_bytes=63 * MEGABYTE
        ),
        name="whole_layer",
    )(x, cot, proj, out, hidden, gains, cosine, sine)


def adamw(weight, grad, first, second, rate, decay):
    first = BETA_ONE * first + (1.0 - BETA_ONE) * grad
    second = BETA_TWO * second + (1.0 - BETA_TWO) * grad * grad
    fixed_first = first / (1.0 - BETA_ONE**STEP)
    fixed_second = second / (1.0 - BETA_TWO**STEP)
    weight = weight - rate * (fixed_first / (jnp.sqrt(fixed_second) + ADAM_EPS) + decay * weight)
    return (first, second, weight)


def body(
    block_input,
    cotangent,
    positions,
    query_weight,
    keyval_weight,
    output_weight,
    gateup_weight,
    down_weight,
    norm_gains,
    query_first,
    keyval_first,
    output_first,
    gateup_first,
    down_first,
    gains_first,
    query_second,
    keyval_second,
    output_second,
    gateup_second,
    down_second,
    gains_second,
):
    count, length, width = block_input.shape
    rows = count * length
    depth = query_weight.shape[0]
    query_width = query_weight.shape[1]
    key_width = keyval_weight.shape[2]
    me = lax.axis_index("dp")
    pair_bit = (me // PAIR) % 2

    proj_block = jnp.concatenate(
        [query_weight.astype(LOW), keyval_weight.reshape(depth, 2 * key_width).astype(LOW)], axis=1
    )
    half_width = down_weight.shape[1] // 2
    chunk_width = half_width // CHUNKS
    hidden_block = jnp.concatenate(
        [
            part[:, None].reshape(depth, 2, CHUNKS, chunk_width)
            for part in (gateup_weight[:, 0], gateup_weight[:, 1], down_weight)
        ],
        axis=3,
    )
    hidden_block = hidden_block.astype(LOW).transpose(1, 2, 0, 3)
    gains_block = jnp.pad(norm_gains.astype(LOW).astype(WIDE), ((0, 6), (0, 0)))
    grad_out = cotangent.reshape(rows, width)
    heads, kv = query_width // HD, key_width // HD
    cosine, sine = angle_tables(positions.reshape(rows))
    signs = jnp.where(jnp.arange(HD) < HD // 2, -1.0, 1.0).astype(WIDE)
    cosine_pair = jnp.tile(cosine[:, 0], (1, 2))
    sine_pair = jnp.tile(sine[:, 0] * signs, (1, 2))
    hidden_terms, output_terms, proj_terms, block_output, input_grad, gains_sum = whole_layer(
        block_input.reshape(rows, width),
        grad_out,
        proj_block,
        output_weight.astype(LOW),
        hidden_block,
        gains_block,
        cosine_pair,
        sine_pair,
        kv,
        count,
    )[:6]
    block_output = block_output.astype(WIDE)
    input_grad = input_grad.astype(WIDE)
    gains_reduced = gains_sum[:2]
    output_reduced = jnp.sum(output_terms.astype(WIDE), axis=0)
    proj_reduced = jnp.sum(proj_terms.astype(WIDE), axis=0)
    query_reduced = proj_reduced[:, :query_width]
    keyval_reduced = proj_reduced[:, query_width:].reshape(depth, 2, key_width)
    mine = jnp.sum(hidden_terms[:, 0::2].astype(WIDE), axis=1)
    other = jnp.sum(hidden_terms[:, 1::2].astype(WIDE), axis=1)

    def hidden_columns(index):
        columns = slice(index * chunk_width, (index + 1) * chunk_width)
        return join(
            jnp.concatenate([mine[c, :, columns] for c in range(CHUNKS)], axis=1),
            jnp.concatenate([other[c, :, columns] for c in range(CHUNKS)], axis=1),
            pair_bit,
            1,
        )

    gateup_reduced = jnp.stack([hidden_columns(0), hidden_columns(1)], axis=1)
    down_reduced = hidden_columns(2)
    query_mean, query_square, query_next = adamw(
        query_weight, query_reduced, query_first, query_second, MATRIX_RATE, WEIGHT_DECAY
    )
    keyval_mean, keyval_square, keyval_next = adamw(
        keyval_weight, keyval_reduced, keyval_first, keyval_second, MATRIX_RATE, WEIGHT_DECAY
    )
    output_mean, output_square, output_next = adamw(
        output_weight, output_reduced, output_first, output_second, MATRIX_RATE, WEIGHT_DECAY
    )
    gateup_mean, gateup_square, gateup_next = adamw(
        gateup_weight, gateup_reduced, gateup_first, gateup_second, MATRIX_RATE, WEIGHT_DECAY
    )
    down_mean, down_square, down_next = adamw(
        down_weight, down_reduced, down_first, down_second, MATRIX_RATE, WEIGHT_DECAY
    )
    gains_mean, gains_square, gains_next = adamw(
        norm_gains, gains_reduced, gains_first, gains_second, GAIN_RATE, 0.0
    )
    return (
        block_output.reshape(count, length, width),
        input_grad.reshape(count, length, width),
        query_reduced,
        keyval_reduced,
        output_reduced,
        gateup_reduced,
        down_reduced,
        gains_reduced,
        query_mean,
        keyval_mean,
        output_mean,
        gateup_mean,
        down_mean,
        gains_mean,
        query_square,
        keyval_square,
        output_square,
        gateup_square,
        down_square,
        gains_square,
        query_next,
        keyval_next,
        output_next,
        gateup_next,
        down_next,
        gains_next,
    )


def solution(mesh):
    in_specs = (
        P("dp", None, None),
        P("dp", None, None),
        P("dp", None),
        P("dp", "tensor"),
        P("dp", None, "tensor"),
        P("dp", "tensor"),
        P("dp", None, "tensor"),
        P("dp", "tensor"),
        P(None, "dp"),
        P("dp", "tensor"),
        P("dp", None, "tensor"),
        P("dp", "tensor"),
        P("dp", None, "tensor"),
        P("dp", "tensor"),
        P(None, "dp"),
        P("dp", "tensor"),
        P("dp", None, "tensor"),
        P("dp", "tensor"),
        P("dp", None, "tensor"),
        P("dp", "tensor"),
        P(None, "dp"),
    )
    out_specs = (
        P("dp", None, None),
        P("dp", None, None),
        P("dp", "tensor"),
        P("dp", None, "tensor"),
        P("dp", "tensor"),
        P("dp", None, "tensor"),
        P("dp", "tensor"),
        P(None, "dp"),
        P("dp", "tensor"),
        P("dp", None, "tensor"),
        P("dp", "tensor"),
        P("dp", None, "tensor"),
        P("dp", "tensor"),
        P(None, "dp"),
        P("dp", "tensor"),
        P("dp", None, "tensor"),
        P("dp", "tensor"),
        P("dp", None, "tensor"),
        P("dp", "tensor"),
        P(None, "dp"),
        P("dp", "tensor"),
        P("dp", None, "tensor"),
        P("dp", "tensor"),
        P("dp", None, "tensor"),
        P("dp", "tensor"),
        P(None, "dp"),
    )
    return jax.shard_map(body, mesh=mesh, in_specs=in_specs, out_specs=out_specs, check_vma=False)
```

```python
import functools
import math

import jax
import jax.numpy as jnp
from jax import lax
from jax.experimental import pallas as pl
from jax.experimental.pallas import tpu as pltpu
from jax.sharding import PartitionSpec as P

HD = 64
STEP = 10

NORM_EPS = 1e-05
ROPE_BASE = 500000.0
BETA_ONE = 0.9
BETA_TWO = 0.95
ADAM_EPS = 1e-08
MATRIX_RATE = 0.05
GAIN_RATE = 0.6
WEIGHT_DECAY = 0.1
MASKED = -1e30

PAIR = 2
CHUNKS = 4

LANES = 128

LOW = jnp.bfloat16
WIDE = jnp.float32
ROWS_BY_ROWS = (((1,), (1,)), ((), ()))
COLUMNS_BY_COLUMNS = (((0,), (0,)), ((), ()))


def dot(left, right, dims=(((1,), (0,)), ((), ()))):
    return lax.dot_general(left, right, dims, preferred_element_type=WIDE)


def swap(values, axis, mask):
    pairs = [(k, k ^ mask) for k in range(lax.axis_size(axis))]
    return lax.ppermute(values, axis, pairs)


def part(values, index, parts, dim):
    size = values.shape[dim] // parts
    return lax.dynamic_slice_in_dim(values, index * size, size, dim)


def join(mine, other, bit, dim):
    first = jnp.concatenate([mine, other], axis=dim)
    second = jnp.concatenate([other, mine], axis=dim)
    return jnp.where(bit == 0, first, second)


def angle_tables(positions):
    lanes = jnp.arange(2 * HD, dtype=jnp.int32) % HD
    half_steps = (lanes % (HD // 2)).astype(WIDE)
    frequency = jnp.exp(half_steps * (-2.0 / HD) * math.log(ROPE_BASE))
    angles = positions.astype(WIDE)[:, None] * frequency
    signs = jnp.where(lanes < HD // 2, -1.0, 1.0).astype(WIDE)
    return jnp.cos(angles), jnp.sin(angles) * signs


def rms_factor(values):
    return lax.rsqrt(jnp.mean(values * values, axis=-1, keepdims=True) + NORM_EPS)


def rms_backward(values, gain, grad):
    factor = rms_factor(values)
    scaled = grad * gain
    inner = jnp.mean(scaled * values, axis=-1, keepdims=True)
    grad_values = factor * scaled - values * (factor * factor * factor * inner)
    grad_gain = jnp.sum(grad * values * factor, axis=0)
    return grad_values, grad_gain


def attend_group(j, group, block, count, length, query_ref, key_ref, value_ref, mixed_ref, logsum_ref):
    row_index = lax.broadcasted_iota(jnp.int32, (block, block), 0)
    column_index = lax.broadcasted_iota(jnp.int32, (block, block), 1)
    allowed = column_index <= row_index
    for sequence in range(count):
        base = sequence * length
        for head in range(group):
            columns = slice((j * group + head) * HD, (j * group + head + 1) * HD)
            for start in range(base, base + length, block):
                rows = slice(start, start + block)
                before = slice(base, start)
                query = query_ref[rows, columns] * HD ** (-0.5)
                last = jnp.where(allowed, dot(query, key_ref[j, rows], ROWS_BY_ROWS), MASKED)
                highest = jnp.max(last, axis=-1, keepdims=True)
                if start > base:
                    early = dot(query, key_ref[j, before], ROWS_BY_ROWS)
                    highest = jnp.maximum(highest, jnp.max(early, axis=-1, keepdims=True))
                    early = jnp.exp(early - highest)
                last = jnp.exp(last - highest)
                total = jnp.sum(last, axis=-1, keepdims=True)
                if start > base:
                    total = total + jnp.sum(early, axis=-1, keepdims=True)
                share = 1.0 / total
                mixed = dot((last * share).astype(LOW), value_ref[j, rows])
                if start > base:
                    mixed = mixed + dot((early * share).astype(LOW), value_ref[j, before])
                mixed_ref[rows, columns] = mixed.astype(LOW)
                logsum_ref[j, rows, head : head + 1] = highest + jnp.log(total)


MESH = pl.DeviceIdType.MESH
MEGABYTE = 1 << 20


def flip(index, mask):
    bit = 1
    while bit <= mask:
        if mask & bit:
            index = index + bit - 2 * bit * lax.rem(lax.div(index, bit), 2)
        bit *= 2
    return index


def remote(source, target, sems, axis, mask):
    return pltpu.make_async_remote_copy(
        src_ref=source,
        dst_ref=target,
        send_sem=sems[0],
        recv_sem=sems[1],
        device_id={axis: flip(lax.axis_index(axis), mask)},
        device_id_type=MESH,
    )


def greet(partners):
    barrier = pltpu.get_barrier_semaphore()
    for axis, mask in partners:
        pl.semaphore_signal(
            barrier,
            inc=1,
            device_id={axis: flip(lax.axis_index(axis), mask)},
            device_id_type=MESH,
        )
    pl.semaphore_wait(barrier, len(partners))


class Gather:
    def __init__(self, masks, source, place, sems):
        self.masks, self.source, self.place, self.sems = masks, source, place, sems
        self.me = lax.axis_index("dp")

    def sem(self, phase, mask):
        send, recv = self.sems
        return send.at[phase, mask // 2], recv.at[phase, mask // 2]

    def far_copy(self, mask):
        return remote(self.source(mask), self.place(self.me), self.sem(0, mask), "dp", mask)

    def near_copy(self, mask):
        here = self.place(flip(self.me, mask))
        return remote(here if mask else self.source(0), here, self.sem(1, mask), "dp", 1)

    def start(self):
        for mask in self.masks[1:]:
            self.far_copy(mask).start()

    def start_own(self):
        self.near_copy(0).start()

    def forward(self, mask):
        here = self.place(flip(self.me, mask))
        remote(here, here, self.sem(0, mask), "dp", mask).wait_recv()
        self.near_copy(mask).start()

    def arrive(self):
        for mask in self.masks:
            here = self.place(flip(self.me, mask ^ 1))
            remote(here, here, self.sem(1, mask), "dp", 1).wait_recv()

    def drain(self):
        for mask in self.masks[1:]:
            self.far_copy(mask).wait_send()
        for mask in self.masks:
            self.near_copy(mask).wait_send()


def rotated(values, cosine, sine, first):
    width = values.shape[1]
    turned = jnp.where(
        first, pltpu.roll(values, width - HD // 2, 1), pltpu.roll(values, HD // 2, 1)
    )
    return values * cosine + turned * sine


SLOTS = 2


class Scatter:
    def __init__(self, masks, product, landing, target, landed, stage, sems):
        self.masks, self.product, self.landing = masks, product, landing
        self.target, self.landed, self.stage, self.sems = target, landed, stage, sems
        self.me = lax.axis_index("dp")
        self.depth = product.shape[0] // lax.axis_size("dp")

    def rows(self, owner):
        return pl.ds(pl.multiple_of(owner * self.depth, self.depth), self.depth)

    def copy(self, phase, mask, source, target):
        send, recv, _ = self.sems
        at = mask // 2
        axis_mask = 1 if phase == 0 else mask
        return remote(source, target, (send.at[phase, at], recv.at[phase, at]), "dp", axis_mask)

    def start(self):
        for mask in self.masks[1:] + [0]:
            self.near_copy(mask).start()

    def near_copy(self, mask):
        source = self.product.at[self.rows(flip(self.me, mask ^ 1))]
        return self.copy(0, mask, source, self.landing.at[mask // 2])

    def load_copy(self, index, mask):
        return pltpu.make_async_copy(
            self.landing.at[mask // 2], self.stage.at[index % 2], self.sems[2].at[index % 2]
        )

    def store_copy(self, index, mask):
        target = self.landing.at[mask // 2] if mask else self.target(0)
        return pltpu.make_async_copy(
            self.stage.at[index % 2], target, self.sems[2].at[2 + index % 2]
        )

    def far_copy(self, mask):
        return self.copy(1, mask, self.landing.at[mask // 2], self.target(mask))

    def steps(self):
        order = self.masks[1:] + [0]
        for step in range(len(order) + 2):
            if step >= 2:
                mask = order[step - 2]
                self.store_copy(step - 2, mask).wait()
                if mask:
                    self.far_copy(mask).start()
            if step < len(order):
                mask = order[step]
                landed = self.landing.at[mask // 2]
                self.copy(0, mask, landed, landed).wait_recv()
                self.load_copy(step, mask).start()
            if 1 <= step <= len(order):
                mask = order[step - 1]
                slot = (step - 1) % 2
                self.load_copy(step - 1, mask).wait()
                at = self.rows(flip(self.me, mask))
                total = self.product[at].astype(WIDE) + self.stage[slot].astype(WIDE)
                self.stage[slot] = total.astype(LOW)
                self.store_copy(step - 1, mask).start()
            yield

    def pump(self):
        for _ in self.steps():
            pass

    def free(self):
        for mask in self.masks:
            self.near_copy(mask).wait_send()

    def release(self):
        for mask in self.masks[1:]:
            self.far_copy(mask).wait_send()

    def arrive(self):
        for mask in self.masks[1:]:
            landed = self.landed(mask)
            self.copy(1, mask, landed, landed).wait_recv()


def attend_back_group(
    j,
    group,
    block,
    count,
    length,
    query_ref,
    key_ref,
    value_ref,
    logsum_ref,
    grad_ref,
    query_grad_ref,
    key_grad_ref,
    value_grad_ref,
):
    key_index = lax.broadcasted_iota(jnp.int32, (block, block), 0)
    query_index = lax.broadcasted_iota(jnp.int32, (block, block), 1)
    allowed = key_index <= query_index
    scale = HD ** (-0.5)
    for sequence in range(count):
        base = sequence * length
        for head in range(group):
            columns = slice((j * group + head) * HD, (j * group + head + 1) * HD)
            for start in range(base, base + length, block):
                rows = slice(start, start + block)
                query = query_ref[rows, columns] * scale
                grad = grad_ref[rows, columns]
                logsum = logsum_ref[j, head : head + 1, rows]
                spans = [(rows, True)]
                if start > base:
                    spans.append((slice(base, start), False))
                probs, grad_probs = [], []
                for span, masked in spans:
                    scores = dot(key_ref[j, span], query, ROWS_BY_ROWS)
                    if masked:
                        scores = jnp.where(allowed, scores, MASKED)
                    probs.append(jnp.exp(scores - logsum))
                    grad_probs.append(dot(value_ref[j, span], grad, ROWS_BY_ROWS))
                inner = sum(
                    jnp.sum(one * two, axis=0, keepdims=True)
                    for one, two in zip(probs, grad_probs)
                )
                query_grad = None
                for (span, _), one, two in zip(spans, probs, grad_probs):
                    grad_scores = (one * (two - inner)).astype(LOW)
                    term = dot(grad_scores, key_ref[j, span], COLUMNS_BY_COLUMNS)
                    query_grad = term if query_grad is None else query_grad + term
                    key_grad_ref[j, span] += dot(grad_scores, query)
                    value_grad_ref[j, span] += dot(one.astype(LOW), grad)
                query_grad_ref[rows, columns] = query_grad * scale


def whole_kernel(
    sizes,
    x_ref,
    cot_ref,
    proj_ref,
    out_ref,
    gateup_ref,
    down_ref,
    gains_ref,
    cosine_ref,
    sine_ref,
    hidden_terms,
    out_terms,
    proj_terms,
    output_ref,
    input_grad_ref,
    gains_sum,
    gateup_sum,
    down_sum,
    hidden_ref,
    hidden_full,
    proj_full,
    out_full,
    other_cot,
    both_ref,
    hidden_land,
    out_land,
    proj_land,
    middle_low,
    line_land,
    saved_normalized,
    saved_query,
    saved_key,
    saved_value,
    saved_mixed,
    saved_middle,
    product,
    stage,
    core_out,
    core_in,
    held,
    keep,
    line_out,
    line_in,
    last_in,
    pair_in,
    flat,
    middle,
    low_out,
    logsums,
    gains_slots,
    gains_full,
    gain_rows,
    gain_blocks,
    gain_land,
    gain_part,
    tensor_land,
    gather_send,
    gather_recv,
    weight_send,
    weight_recv,
    token_send,
    token_recv,
    scatter_send,
    scatter_recv,
    scatter_local,
    core_send,
    core_recv,
    line_send,
    line_recv,
    pair_send,
    pair_recv,
    spread_send,
    spread_recv,
    gain_send,
    gain_recv,
    tensor_send,
    tensor_recv,
    own_sem,
    load_sem,
    save_sem,
    strip_sem,
    local_sem,
    final_sem,
    final_out_sem,
    credit,
):
    count, length = sizes
    rows, width = cot_ref.shape
    devices = lax.axis_size("dp")
    masks = list(range(0, devices, 2))
    me = lax.axis_index("dp")
    tensor = lax.axis_index("tensor")
    core, line = lax.rem(tensor, 2), lax.div(tensor, 2)
    pair_bit = lax.rem(lax.div(me, PAIR), 2)
    depth = proj_ref.shape[0]
    chunks = hidden_full.shape[0]
    unit = hidden_full.shape[2] // 3
    half, piece = rows // 2, rows // 4
    strips, strip = keep.shape[0], keep.shape[2]
    query_width = saved_query.shape[1]
    kv = saved_key.shape[0]
    group = query_width // (kv * HD)
    block = min(256, length)
    greet(
        [("dp", mask) for mask in range(1, devices)] + [("tensor", mask) for mask in range(1, 4)]
    )

    def block_rows(ref):
        return lambda owner: ref.at[pl.ds(pl.multiple_of(owner * depth, depth), depth)]

    def pair_half(mask):
        return pair_bit if not mask & PAIR else 1 - pair_bit

    def gather(index, ref, place_of):
        sems = gather_send.at[index], gather_recv.at[index]
        return Gather(masks, lambda mask: ref, place_of, sems)

    gains = gather(0, gains_ref, lambda owner: gains_slots.at[owner])
    proj_in = gather(1, proj_ref, block_rows(proj_full))
    out_in = gather(2, out_ref, block_rows(out_full))
    hidden_in = [
        Gather(
            masks,
            lambda mask, c=c: hidden_ref.at[pair_half(mask), c],
            block_rows(hidden_full.at[c]),
            (weight_send.at[c], weight_recv.at[c]),
        )
        for c in range(chunks)
    ]

    def own_copy(index):
        one = ([gains, proj_in, out_in] + hidden_in)[index]
        return pltpu.make_async_copy(one.source(0), one.place(me), own_sem.at[index])

    def pump(c):
        for mask in masks[1:]:
            hidden_in[c].forward(mask)

    quarter = pl.ds(pl.multiple_of(core * half + line * piece, piece), piece)
    near_half = pl.multiple_of(core * half, half)
    far_half = pl.multiple_of((1 - core) * half, half)
    near_line = pl.ds(pl.multiple_of(line * piece, piece), piece)
    far_line = pl.ds(pl.multiple_of((1 - line) * piece, piece), piece)

    def place(ref, core_at, line_at):
        return ref.at[pl.ds(pl.multiple_of(core_at * half + line_at * piece, piece), piece)]

    near_ref, far_ref = both_ref.at[0], both_ref.at[1]

    def token_ends(index):
        cot_near, cot_there = place(other_cot, core, line), place(other_cot, core, 1 - line)
        near, near_there = place(near_ref, core, line), place(near_ref, core, 1 - line)
        far, far_there = place(far_ref, core, line), place(far_ref, core, 1 - line)
        return [
            lambda: (place(cot_ref, core, line), cot_near, "dp", PAIR, cot_near),
            lambda: (cot_near, cot_near, "tensor", 2, cot_there),
            lambda: (cot_near, cot_near, "tensor", 1, place(other_cot, 1 - core, line)),
            lambda: (cot_there, cot_there, "tensor", 1, place(other_cot, 1 - core, 1 - line)),
            lambda: (low_out, far, "dp", PAIR, far),
            lambda: (low_out, near, "tensor", 2, near_there),
            lambda: (low_out, near, "tensor", 1, place(near_ref, 1 - core, line)),
            lambda: (near_there, near_there, "tensor", 1, place(near_ref, 1 - core, 1 - line)),
            lambda: (far, far, "tensor", 2, far_there),
            lambda: (far, far, "tensor", 1, place(far_ref, 1 - core, line)),
            lambda: (far_there, far_there, "tensor", 1, place(far_ref, 1 - core, 1 - line)),
        ][index]()

    def token(index):
        source, target, axis, mask, _ = token_ends(index)
        sems = token_send.at[index], token_recv.at[index]
        return remote(source, target, sems, axis, mask)

    def token_arrive(*indices):
        for index in indices:
            _, _, axis, mask, landed = token_ends(index)
            sems = token_send.at[index], token_recv.at[index]
            remote(landed, landed, sems, axis, mask).wait_recv()

    def scatter(index, product_ref, landing, target, landed):
        columns = landing.shape[2]
        return Scatter(
            masks,
            product_ref,
            landing,
            target,
            landed,
            stage.at[:, :, :columns] if columns < stage.shape[2] else stage,
            (scatter_send.at[index], scatter_recv.at[index], scatter_local.at[index]),
        )

    hidden = [
        scatter(
            c,
            product.at[c % SLOTS],
            hidden_land.at[c],
            lambda mask, c=c: hidden_terms.at[pair_bit, c, mask // 4],
            lambda mask, c=c: hidden_terms.at[pair_half(mask), c, mask // 4],
        )
        for c in range(chunks)
    ]

    def core_copy(slot, parts):
        return remote(
            core_out.at[slot, pl.ds(0, parts)],
            core_in.at[slot, pl.ds(0, parts)],
            (core_send.at[slot], core_recv.at[slot]),
            "tensor",
            1,
        )

    def line_copy(turn, s, parts, landing, source=line_out):
        return remote(
            source.at[s, pl.ds(0, parts)],
            landing.at[s],
            (line_send.at[turn, s], line_recv.at[turn, s]),
            "tensor",
            2,
        )

    def pair_copy(turn, s, landing):
        return remote(
            line_out.at[s, 1],
            landing.at[s],
            (pair_send.at[turn, s], pair_recv.at[turn, s]),
            "dp",
            PAIR,
        )

    def reduce_strips(
        turn, parts, term, prepare, landing, source=line_out, kept=keep, between=()
    ):
        def finish(s, slot):
            core_copy(slot, parts).wait_recv()
            near = []
            for q in range(parts):
                source[s, q] = (
                    held[q, far_line] + core_in[slot, q, far_line].astype(WIDE)
                ).astype(LOW)
                near.append(held[q, near_line] + core_in[slot, q, near_line].astype(WIDE))
            kept[s] = near[0]
            if parts == 2:
                flat[:, pl.ds(pl.multiple_of(s * strip, strip), strip)] = near[1]
            pl.semaphore_signal(
                credit, inc=1, device_id={"tensor": flip(tensor, 1)}, device_id_type=MESH
            )
            line_copy(turn, s, parts, landing, source).start()

        def one_strip(s, carry):
            slot = lax.rem(s, 2)
            prepare(s, slot)

            @pl.when(s >= 2)
            def _():
                core_copy(slot, parts).wait_send()

            for q in range(parts):
                core_out[slot, q] = term(q, far_half, s, slot).astype(LOW)
            if turn:
                pl.semaphore_wait(credit, 1)
            else:

                @pl.when(s >= 2)
                def _():
                    pl.semaphore_wait(credit, 1)

            core_copy(slot, parts).start()

            @pl.when(s >= 1)
            def _():
                finish(s - 1, 1 - slot)

            for q in range(parts):
                held[q] = term(q, near_half, s, slot)
            return carry

        cuts = [strips * cut // (len(between) + 1) for cut in range(len(between) + 2)]
        for first, last, step in zip(cuts[:-1], cuts[1:], list(between) + [None]):
            lax.fori_loop(first, last, one_strip, 0)
            if step is not None:
                step()
        finish(strips - 1, (strips - 1) % 2)
        for slot in range(2):
            core_copy(slot, parts).wait_send()

    def strip_loads(s, slot):
        return [
            pltpu.make_async_copy(
                hidden_full.at[c, pl.ds(pl.multiple_of(s * strip, strip), strip)],
                weights.at[pl.ds(pl.multiple_of((slot * chunks + c) * strip, strip), strip)],
                strip_sem.at[slot, c],
            )
            for c in range(chunks)
        ]

    def start_strip(s, slot):
        for copy in strip_loads(s, slot):
            copy.start()

    def prepare_strip(s, slot):
        @pl.when(s + 1 < strips)
        def _():
            start_strip(s + 1, 1 - slot)

        for copy in strip_loads(s, slot):
            copy.wait()

    def hidden_term(ref, first, wide):
        def term(q, start, s, slot):
            at = pl.ds(pl.multiple_of(q * rows + start, half), half)
            total = None
            for c in range(chunks):
                block = weights[
                    pl.ds(pl.multiple_of((slot * chunks + c) * strip, strip), strip),
                    first : first + wide,
                ]
                one = dot(ref[at, c * wide : (c + 1) * wide], block, ROWS_BY_ROWS)
                total = one if total is None else total + one
            return total

        return term

    def to_pair(turn, landing):
        if landing is not line_in:
            for s in range(strips):
                line_copy(turn, s, 2, landing).wait_recv()
            copy = pltpu.make_async_copy(landing, line_in, load_sem.at[0])
            copy.start()
            copy.wait()
        for s in range(strips):
            copy = line_copy(turn, s, 2, landing)
            if landing is line_in:
                copy.wait_recv()
            copy.wait_send()
            columns = slice(s * strip, (s + 1) * strip)
            line_out[s, 1] = (flat[:, columns] + line_in[s, 1].astype(WIDE)).astype(LOW)
            pair_copy(turn - 1, s, pair_in.at[turn - 1]).start()
            flat[:, columns] = keep[s] + line_in[s, 0].astype(WIDE)

    def from_pair(turn):
        for s in range(strips):
            copy = pair_copy(turn - 1, s, pair_in.at[turn - 1])
            copy.wait_recv()
            copy.wait_send()
            flat[:, s * strip : (s + 1) * strip] += pair_in[turn - 1, s].astype(WIDE)

    tile = min(64, piece)

    def rms_back(values_of, gain, grads_of, store, gain_row):
        def one_tile(index, total):
            at = pl.ds(pl.multiple_of(index * tile, tile), tile)
            there = pl.ds(pl.multiple_of(core * half + line * piece + index * tile, tile), tile)
            values, grads = values_of(at), grads_of(at)
            grad_values, grad_gain = rms_backward(values, gain, grads)
            store(at, there, grad_values)
            return total + grad_gain[None]

        zero = jnp.zeros((1, width), WIDE)
        gain_rows[gain_row : gain_row + 1] = lax.fori_loop(0, piece // tile, one_tile, zero)

    def spread_copy(index, source, target, mask):
        return remote(
            source, target, (spread_send.at[index], spread_recv.at[index]), "tensor", mask
        )

    def spread(base, source, target):
        here = place(target, core, line)
        spread_copy(base, source, here, 2).start()
        spread_copy(base + 1, source, here, 1).start()
        pltpu.make_async_copy(source, here, local_sem.at[base]).start()

    def spread_on(base, target):
        there = place(target, core, 1 - line)
        spread_copy(base, there, there, 2).wait_recv()
        spread_copy(base + 2, there, there, 1).start()

    def spread_release(base, source, target):
        here, there = place(target, core, line), place(target, core, 1 - line)
        spread_copy(base, source, here, 2).wait_send()
        spread_copy(base + 1, source, here, 1).wait_send()
        spread_copy(base + 2, there, there, 1).wait_send()
        pltpu.make_async_copy(source, here, local_sem.at[base]).wait()

    def spread_end(base, target):
        near, far = place(target, 1 - core, line), place(target, 1 - core, 1 - line)
        spread_copy(base + 1, near, near, 1).wait_recv()
        spread_copy(base + 2, far, far, 1).wait_recv()

    def gain_copy(mask):
        return remote(
            gain_blocks.at[flip(me, mask)],
            gain_land.at[mask],
            (gain_send.at[mask], gain_recv.at[mask]),
            "dp",
            mask,
        )

    def tensor_copy(mask):
        return remote(
            gain_part,
            tensor_land.at[mask],
            (tensor_send.at[mask], tensor_recv.at[mask]),
            "tensor",
            mask,
        )

    def lanes_turned(values, cosine, sine):
        times = values.shape[1] // cosine.shape[1]
        lanes = lax.broadcasted_iota(jnp.int32, values.shape, 1)
        return rotated(
            values,
            jnp.concatenate([cosine] * times, axis=1),
            jnp.concatenate([sine] * times, axis=1),
            lax.rem(lanes, HD) < HD // 2,
        ).astype(LOW)

    tokens = min(256, rows)

    def tile_at(index, size):
        return pl.ds(pl.multiple_of(index * size, size), size)

    gains.start()
    proj_in.start()
    gains.start_own()
    proj_in.start_own()
    for index in range(3):
        own_copy(index).start()

    def attention(
        x,
        normalized,
        proj,
        out,
        query,
        key,
        value,
        mixed,
        logsum,
        cosines,
        sines,
        gateup,
        down,
        blocks,
    ):
        loads = [
            pltpu.make_async_copy(source, target, load_sem.at[index])
            for index, (source, target) in enumerate(
                [
                    (x_ref, x),
                    (cosine_ref, cosines),
                    (sine_ref, sines),
                    (gateup_ref.at[:, 0], gateup.at[0]),
                    (gateup_ref.at[:, 1], gateup.at[1]),
                    (down_ref, down),
                ]
            )
        ]
        for copy in loads:
            copy.start()
        logsum[...] = jnp.zeros_like(logsum)
        for mask in masks[1:]:
            gains.forward(mask)
        proj_in.forward(masks[1])
        out_in.start()
        out_in.start_own()
        gains.arrive()
        own_copy(0).wait()
        gains_full[...] = jnp.concatenate([gains_slots[j] for j in range(devices)], axis=1)
        for copy in loads:
            copy.wait()

        def norm_tile(index, carry):
            at = tile_at(index, tokens)
            values = x[at].astype(WIDE)
            normalized[at] = (values * rms_factor(values) * gains_full[0:1]).astype(LOW)
            return carry

        lax.fori_loop(0, rows // tokens, norm_tile, 0)
        saves = [
            pltpu.make_async_copy(source, target, save_sem.at[index])
            for index, (source, target) in enumerate(
                [
                    (normalized, saved_normalized),
                    (query, saved_query),
                    (key, saved_key),
                    (value, saved_value),
                    (mixed, saved_mixed),
                    (middle, saved_middle),
                ]
            )
        ]
        saves[0].start()
        tiles = 2 * unit // LANES
        stores = []
        for index in range(2 * chunks):
            h, c = index // chunks, index % chunks
            for j in range(tiles):
                first = index * unit + (j // 2) * LANES
                lanes = gateup[j % 2, :, first : first + LANES]
                blocks[h, c, :, j * LANES : (j + 1) * LANES] = lanes.astype(LOW)
            blocks[h, c, :, 2 * unit :] = down[:, index * unit : (index + 1) * unit].astype(LOW)
            copy = pltpu.make_async_copy(
                blocks.at[h, c], hidden_ref.at[h, c], final_sem.at[index]
            )
            copy.start()
            stores.append(copy)
        for copy in stores:
            copy.wait()
        for index in range(chunks):
            own_copy(3 + index).start()
        for mask in masks[2:]:
            proj_in.forward(mask)
            if mask == masks[2]:
                token(0).start()
                hidden_in[0].start()
        hidden_in[1].start()
        hidden_in[0].start_own()
        hidden_in[1].start_own()
        proj_in.arrive()
        own_copy(1).wait()
        load_proj = pltpu.make_async_copy(proj_full, proj, load_sem.at[6])
        load_proj.start()
        load_proj.wait()

        def project_tile(index, carry):
            at = tile_at(index, tokens)
            pre = dot(normalized[at], proj[...])
            cosine, sine = cosines[at], sines[at]
            query[at] = lanes_turned(pre[:, :query_width], cosine, sine)
            keys = lanes_turned(pre[:, query_width : query_width + kv * HD], cosine, sine)
            values = pre[:, query_width + kv * HD :].astype(LOW)
            for j in range(kv):
                key[j, at] = keys[:, j * HD : (j + 1) * HD]
                value[j, at] = values[:, j * HD : (j + 1) * HD]
            return carry

        lax.fori_loop(0, rows // tokens, project_tile, 0)
        for copy in saves[1:4]:
            copy.start()
        for j in range(kv):
            attend_group(j, group, block, count, length, query, key, value, mixed, logsum)
            if j == 0:
                token_arrive(0)
                token(1).start()
                token(2).start()
                for mask in masks[1:]:
                    out_in.forward(mask)
        saves[4].start()
        for j in range(kv):
            logsums[j] = logsum[j].T[: logsums.shape[1]]
        out_in.arrive()
        own_copy(2).wait()
        load_out = pltpu.make_async_copy(out_full, out, load_sem.at[7])
        load_out.start()
        load_out.wait()

        def out_term(q, start, s, slot):
            return dot(
                mixed[pl.ds(start, half)],
                out[pl.ds(pl.multiple_of(s * strip, strip), strip)],
                ROWS_BY_ROWS,
            )

        reduce_strips(0, 1, out_term, lambda s, slot: None, last_in)
        pump(0)
        for s in range(strips):
            copy = line_copy(0, s, 1, last_in)
            copy.wait_recv()
            copy.wait_send()
            columns = slice(s * strip, (s + 1) * strip)
            middle[:, columns] = (
                x[quarter, columns].astype(WIDE) + keep[s] + last_in[s, 0].astype(WIDE)
            )
        saves[5].start()
        values = middle[...]
        low_out[...] = (values * rms_factor(values) * gains_full[1:2]).astype(LOW)
        for index in (4, 5, 6):
            token(index).start()
        for c in range(2, chunks):
            hidden_in[c].start()
            hidden_in[c].start_own()
        for copy in saves:
            copy.wait()

    pl.run_scoped(
        attention,
        pltpu.VMEM((rows, width), LOW),
        pltpu.VMEM((rows, width), LOW),
        pltpu.VMEM(proj_full.shape, LOW),
        pltpu.VMEM(out_full.shape, LOW),
        pltpu.VMEM(saved_query.shape, LOW),
        pltpu.VMEM(saved_key.shape, LOW),
        pltpu.VMEM(saved_value.shape, LOW),
        pltpu.VMEM(saved_mixed.shape, LOW),
        pltpu.VMEM((kv, rows, 128), WIDE),
        pltpu.VMEM(cosine_ref.shape, WIDE),
        pltpu.VMEM(sine_ref.shape, WIDE),
        pltpu.VMEM((2,) + down_ref.shape, WIDE),
        pltpu.VMEM(down_ref.shape, WIDE),
        pltpu.VMEM(hidden_ref.shape, LOW),
    )

    weights = None

    def feed_forward(normed, grads, weights_ref, gate_ref, hidden_out):
        nonlocal weights
        weights = weights_ref
        load_cot = pltpu.make_async_copy(cot_ref, grads.at[pl.ds(0, rows)], load_sem.at[0])
        load_cot.start()
        place_own = pltpu.make_async_copy(low_out, place(near_ref, core, line), local_sem.at[1])
        place_own.start()
        pump(1)
        token_arrive(5)
        token(7).start()
        token_arrive(1)
        token(3).start()
        token_arrive(4)
        token(8).start()
        token(9).start()
        pump(2)
        place_own.wait()
        token_arrive(6, 7, 2, 3)
        loads = [
            load_cot,
            pltpu.make_async_copy(near_ref, normed.at[pl.ds(0, rows)], load_sem.at[1]),
            pltpu.make_async_copy(other_cot, grads.at[pl.ds(rows, rows)], load_sem.at[2]),
            pltpu.make_async_copy(far_ref, normed.at[pl.ds(rows, rows)], load_sem.at[3]),
        ]
        loads[1].start()
        loads[2].start()

        def load_weights(c):
            hidden_in[c].arrive()
            own_copy(3 + c).wait()
            copy = pltpu.make_async_copy(hidden_full.at[c], weights, load_sem.at[4])
            copy.start()
            return copy

        waiting = [load_weights(0)]
        token_arrive(8)
        token(10).start()
        token_arrive(9, 10)
        loads[3].start()
        for copy in loads:
            copy.wait()
        half_tokens = min(512, 2 * rows)

        def stage_one(c):
            (waiting.pop() if waiting else load_weights(c)).wait()

            def one_tile(index, carry):
                at = tile_at(index, half_tokens)
                gate_up = dot(normed[at], weights[:, : 2 * unit])
                grad_hidden = dot(grads[at], weights[:, 2 * unit :])
                spans = range(0, 2 * unit, 2 * LANES)
                gate = jnp.concatenate([gate_up[:, one : one + LANES] for one in spans], axis=1)
                upward = jnp.concatenate(
                    [gate_up[:, one + LANES : one + 2 * LANES] for one in spans], axis=1
                )
                sigma = jax.nn.sigmoid(gate)
                passed = gate * sigma
                hidden_out[at, c * unit : (c + 1) * unit] = (passed * upward).astype(LOW)
                grad_gate = grad_hidden * upward * sigma * (1.0 + gate * (1.0 - sigma))
                first = 2 * c * unit
                grad_gate = grad_gate.astype(LOW)
                grad_up = (grad_hidden * passed).astype(LOW)
                for one in range(0, unit, LANES):
                    to = first + 2 * one
                    gate_ref[at, to : to + LANES] = grad_gate[:, one : one + LANES]
                    gate_ref[at, to + LANES : to + 2 * LANES] = grad_up[:, one : one + LANES]
                return carry

            lax.fori_loop(0, 2 * rows // half_tokens, one_tile, 0)

        columns = min(512, width)

        def stage_two(c):
            if c >= SLOTS:
                hidden[c - SLOTS].free()

            def one_tile(index, carry):
                at = pl.ds(pl.multiple_of(index * columns, columns), columns)
                gate_up = dot(
                    normed[:, at], gate_ref[:, 2 * c * unit : 2 * (c + 1) * unit], COLUMNS_BY_COLUMNS
                )
                down = dot(grads[:, at], hidden_out[:, c * unit : (c + 1) * unit], COLUMNS_BY_COLUMNS)
                product[c % SLOTS, at, : 2 * unit] = gate_up.astype(LOW)
                product[c % SLOTS, at, 2 * unit :] = down.astype(LOW)
                return carry

            lax.fori_loop(0, width // columns, one_tile, 0)
            hidden[c].start()

        gain_rows[...] = jnp.zeros_like(gain_rows)
        stage_one(0)
        waiting.append(load_weights(1))
        hidden_in[3].forward(masks[1])
        stage_one(1)
        hidden_in[3].forward(masks[2])
        stage_one(2)
        for mask in masks[3:]:
            hidden_in[3].forward(mask)
        stage_two(0)
        stage_one(3)
        start_strip(0, 0)
        early = hidden[0].steps()

        def pump_step():
            next(early)

        reduce_strips(
            1,
            2,
            hidden_term(gate_ref, 0, 2 * unit),
            prepare_strip,
            line_in,
            between=[pump_step] * 3,
        )
        for _ in early:
            pass
        stage_two(1)
        stage_two(2)
        to_pair(1, line_in)
        from_pair(1)
        for index in (4, 5, 6):
            token(index).wait_send()

        def store(at, there, grad_values):
            total = grads[there].astype(WIDE) + grad_values
            middle[at] = total
            low_out[at] = total.astype(LOW)

        rms_back(lambda at: middle[at], gains_full[1:2], lambda at: flat[at], store, 1)
        spread(0, low_out, middle_low)
        start_strip(0, 0)
        hidden[1].pump()
        stage_two(3)
        reduce_strips(2, 2, hidden_term(hidden_out, 2 * unit, unit), prepare_strip, line_land)
        spread_on(0, middle_low)

    pl.run_scoped(
        feed_forward,
        pltpu.VMEM((2 * rows, width), LOW),
        pltpu.VMEM((2 * rows, width), LOW),
        pltpu.VMEM((width, 3 * unit), LOW),
        pltpu.VMEM((2 * rows, 2 * unit * chunks), LOW),
        pltpu.VMEM((2 * rows, unit * chunks), LOW),
    )

    def second_phase(
        grads,
        out_weight,
        proj_weight,
        query,
        key,
        value,
        mixed,
        normalized,
        grad_mixed,
        query_grad,
        key_grad,
        value_grad,
        projected,
        out_product,
        proj_product,
        cosines,
        sines,
        low_grad,
        final_out,
        final_down,
    ):
        sources = [out_full, saved_query, saved_key, saved_value, saved_mixed]
        sources += [proj_full, saved_normalized, cosine_ref, sine_ref]
        targets = [out_weight, query, key, value, mixed, proj_weight, normalized, cosines, sines]
        loads = [
            pltpu.make_async_copy(source, target, load_sem.at[index])
            for index, (source, target) in enumerate(zip(sources, targets))
        ]
        loads[0].start()
        key_grad[...] = jnp.zeros_like(key_grad)
        value_grad[...] = jnp.zeros_like(value_grad)
        spread_end(0, middle_low)
        spread_release(0, low_out, middle_low)
        hidden[2].pump()
        load_grads = pltpu.make_async_copy(middle_low, grads, load_sem.at[len(loads)])
        load_grads.start()
        for copy in loads[1:]:
            copy.start()
        loads[0].wait()
        load_grads.wait()
        def mixed_tile(index, carry):
            at = pl.ds(pl.multiple_of(index * tokens, tokens), tokens)
            grad_mixed[at] = dot(grads[at], out_weight[...]).astype(LOW)
            return carry

        lax.fori_loop(0, rows // tokens, mixed_tile, 0)
        for copy in loads[1:5]:
            copy.wait()
        columns = min(256, width)

        def out_tile(index, carry):
            at = pl.ds(pl.multiple_of(index * columns, columns), columns)
            out_product[at] = dot(grads[:, at], mixed[...], COLUMNS_BY_COLUMNS).astype(LOW)
            return carry

        lax.fori_loop(0, width // columns, out_tile, 0)
        out_place = lambda mask: out_terms.at[mask // 2]
        out = scatter(chunks, out_product, out_land, out_place, out_place)
        out.start()
        for j in range(kv):
            attend_back_group(
                j,
                group,
                block,
                count,
                length,
                query,
                key,
                value,
                logsums,
                grad_mixed,
                query_grad,
                key_grad,
                value_grad,
            )
        hidden[3].pump()
        for copy in loads[5:]:
            copy.wait()

        def turn_tile(index, carry):
            at = pl.ds(pl.multiple_of(index * tokens, tokens), tokens)
            cosine, sine = cosines[at], -sines[at]

            keys = jnp.concatenate([key_grad[j, at] for j in range(kv)], axis=1)
            values = jnp.concatenate([value_grad[j, at] for j in range(kv)], axis=1)
            projected[at, :query_width] = lanes_turned(query_grad[at], cosine, sine)
            projected[at, query_width : query_width + kv * HD] = lanes_turned(keys, cosine, sine)
            projected[at, query_width + kv * HD :] = values.astype(LOW)
            return carry

        lax.fori_loop(0, rows // tokens, turn_tile, 0)

        def proj_term(q, start, s, slot):
            return dot(
                projected[pl.ds(start, half)],
                proj_weight[pl.ds(pl.multiple_of(s * strip, strip), strip)],
                ROWS_BY_ROWS,
            )

        def proj_tile(index, carry):
            at = pl.ds(pl.multiple_of(index * columns, columns), columns)
            proj_product[at] = dot(normalized[:, at], projected[...], COLUMNS_BY_COLUMNS).astype(LOW)
            return carry

        lax.fori_loop(0, width // columns, proj_tile, 0)
        proj_place = lambda mask: proj_terms.at[mask // 2]
        proj = scatter(chunks + 1, proj_product, proj_land, proj_place, proj_place)
        proj.start()
        to_pair(2, line_land)
        reduce_strips(3, 1, proj_term, lambda s, slot: None, last_in)
        out.pump()
        hidden[chunks - 2].free()
        terms = hidden_terms.shape[2]

        def final_load(h, c, k):
            return pltpu.make_async_copy(
                hidden_terms.at[h, c, k],
                product.at[0, pl.ds(((2 * h + c % 2) * terms + k) * depth, depth)],
                final_sem.at[(2 * h + c % 2) * terms + k],
            )

        def final_gateup(h, g, first):
            at = pl.ds((h * chunks + first) * unit, 2 * unit)
            return pltpu.make_async_copy(
                final_out.at[h, g], gateup_sum.at[:, g, at], final_out_sem.at[2 * h + g]
            )

        def final_rest(h, c):
            at = pl.ds((h * chunks + c) * unit, unit)
            return pltpu.make_async_copy(
                final_down.at[h, c % 2], down_sum.at[:, at], final_out_sem.at[4 + 2 * h + c % 2]
            )

        def finalize(first):
            for c in (first, first + 1):
                hidden[c].arrive()
                for h in range(2):
                    for k in range(terms):
                        final_load(h, c, k).start()
            for h in range(2):
                for c in (first, first + 1):
                    total = None
                    for k in range(terms):
                        final_load(h, c, k).wait()
                        start = ((2 * h + c % 2) * terms + k) * depth
                        one = product[0, start : start + depth].astype(WIDE)
                        total = one if total is None else total + one
                    for j in range(2 * unit // LANES):
                        to = (c % 2) * unit + (j // 2) * LANES
                        lanes = total[:, j * LANES : (j + 1) * LANES]
                        final_out[h, j % 2, :, to : to + LANES] = lanes
                    final_down[h, c % 2] = total[:, 2 * unit :]
                    final_rest(h, c).start()
                for g in range(2):
                    final_gateup(h, g, first).start()

        def final_wait(first):
            for h in range(2):
                for c in (first, first + 1):
                    final_rest(h, c).wait()
                for g in range(2):
                    final_gateup(h, g, first).wait()

        finalize(0)
        load_x = pltpu.make_async_copy(x_ref.at[quarter], low_grad, load_sem.at[1])
        load_x.start()
        for s in range(strips):
            copy = line_copy(3, s, 1, last_in)
            copy.wait_recv()
            copy.wait_send()
        load_x.wait()

        def grads_of(at):
            return jnp.concatenate(
                [keep[s, at] + last_in[s, 0, at].astype(WIDE) for s in range(strips)], axis=1
            )

        def store(at, there, grad_values):
            low_out[at] = (middle[at] + grad_values).astype(LOW)

        rms_back(lambda at: low_grad[at].astype(WIDE), gains_full[0:1], grads_of, store, 0)
        spread(3, low_out, input_grad_ref)
        for owner in range(devices):
            gain_blocks[owner] = gain_rows[:, owner * depth : (owner + 1) * depth]
        for mask in range(1, devices):
            gain_copy(mask).start()

        again = [
            pltpu.make_async_copy(
                saved_middle.at[:, pl.ds(s * strip, strip)], keep.at[s], strip_sem.at[s % 2, s // 2]
            )
            for s in range(strips)
        ]
        for copy in again:
            copy.start()
        proj.pump()
        for mask in range(1, devices):
            gain_copy(mask).wait_recv()
        total = gain_blocks[me]
        for mask in range(1, devices):
            total = total + gain_land[mask]
        gain_part[...] = total
        for mask in range(1, 4):
            tensor_copy(mask).start()
        from_pair(2)
        for s, copy in enumerate(again):
            columns = slice(s * strip, (s + 1) * strip)
            copy.wait()
            low_grad[:, columns] = (keep[s] + flat[:, columns]).astype(LOW)
        spread(6, low_grad, output_ref)
        final_wait(0)
        finalize(2)
        spread_on(3, input_grad_ref)
        for mask in range(1, 4):
            tensor_copy(mask).wait_recv()
        gains_sum[...] = gain_part[...] + tensor_land[1] + tensor_land[2] + tensor_land[3]
        spread_on(6, output_ref)
        for gather in [out, proj]:
            gather.arrive()
        for gather in hidden[chunks - 1 :] + [out, proj]:
            gather.free()
        final_wait(2)
        for gather in hidden + [out, proj]:
            gather.release()
        for base, source, target in ((3, low_out, input_grad_ref), (6, low_grad, output_ref)):
            spread_end(base, target)
            spread_release(base, source, target)
        for mask in range(1, devices):
            gain_copy(mask).wait_send()
        for mask in range(1, 4):
            tensor_copy(mask).wait_send()
        for index in (0, 1, 2, 3, 7, 8, 9, 10):
            token(index).wait_send()
        for one in [gains, proj_in, out_in] + hidden_in:
            one.drain()
        pl.semaphore_wait(credit, 2)

    pl.run_scoped(
        second_phase,
        pltpu.VMEM((rows, width), LOW),
        pltpu.VMEM(out_full.shape, LOW),
        pltpu.VMEM(proj_full.shape, LOW),
        pltpu.VMEM(saved_query.shape, LOW),
        pltpu.VMEM(saved_key.shape, LOW),
        pltpu.VMEM(saved_value.shape, LOW),
        pltpu.VMEM(saved_mixed.shape, LOW),
        pltpu.VMEM((rows, width), LOW),
        pltpu.VMEM(saved_query.shape, LOW),
        pltpu.VMEM(saved_query.shape, WIDE),
        pltpu.VMEM(saved_key.shape, WIDE),
        pltpu.VMEM(saved_key.shape, WIDE),
        pltpu.VMEM((rows, proj_full.shape[1]), LOW),
        pltpu.VMEM(out_full.shape, LOW),
        pltpu.VMEM(proj_full.shape, LOW),
        pltpu.VMEM(cosine_ref.shape, WIDE),
        pltpu.VMEM(sine_ref.shape, WIDE),
        pltpu.VMEM((piece, width), LOW),
        pltpu.VMEM((2, 2, depth, 2 * unit), WIDE),
        pltpu.VMEM((2, 2, depth, unit), WIDE),
    )


def whole_layer(x, cot, proj, out, gateup, down, gains, cosine, sine, kv, count):
    rows, width = cot.shape
    devices = lax.axis_size("dp")
    spans = devices // 2
    depth = proj.shape[0]
    chunks = CHUNKS
    assert chunks == 4
    unit = down.shape[1] // (2 * chunks)
    columns = 3 * unit
    query_width, proj_width = out.shape[1], proj.shape[1]
    half, piece = rows // 2, rows // 4
    strip = width // (2 * chunks)
    strips = width // strip
    vmem = pl.BlockSpec(memory_space=pltpu.VMEM)
    anywhere = pl.BlockSpec(memory_space=pl.ANY)
    shape = jax.ShapeDtypeStruct
    dma = pltpu.SemaphoreType.DMA
    low, wide = (lambda *sizes: pltpu.VMEM(sizes, LOW)), (lambda *sizes: pltpu.VMEM(sizes, WIDE))
    return pl.pallas_call(
        functools.partial(whole_kernel, (count, rows // count)),
        in_specs=[anywhere] * 6 + [vmem] + [anywhere] * 2,
        out_specs=[anywhere] * 5 + [vmem] + [anywhere] * 19,
        out_shape=[
            shape((2, chunks, spans // 2, depth, columns), LOW),
            shape((spans, depth, query_width), LOW),
            shape((spans, depth, proj_width), LOW),
            shape((rows, width), LOW),
            shape((rows, width), LOW),
            shape((gains.shape[0], depth), WIDE),
            shape(gateup.shape, WIDE),
            shape(down.shape, WIDE),
            shape((2, chunks, depth, columns), LOW),
            shape((chunks, width, columns), LOW),
            shape((width, proj_width), LOW),
            shape((width, query_width), LOW),
            shape((rows, width), LOW),
            shape((2, rows, width), LOW),
            shape((chunks, spans, depth, columns), LOW),
            shape((spans, depth, query_width), LOW),
            shape((spans, depth, proj_width), LOW),
            shape((rows, width), LOW),
            shape((strips, 2, piece, strip), LOW),
            shape((rows, width), LOW),
            shape((rows, query_width), LOW),
            shape((kv, rows, HD), LOW),
            shape((kv, rows, HD), LOW),
            shape((rows, query_width), LOW),
            shape((piece, width), WIDE),
        ],
        scratch_shapes=[
            low(SLOTS, width, columns),
            low(2, depth, columns),
            low(2, 2, half, strip),
            low(2, 2, half, strip),
            wide(2, half, strip),
            wide(strips, piece, strip),
            low(strips, 2, piece, strip),
            low(strips, 2, piece, strip),
            low(strips, 1, piece, strip),
            low(2, strips, piece, strip),
            wide(piece, width),
            wide(piece, width),
            low(piece, width),
            wide(kv, 8, rows),
            wide(devices, gains.shape[0], depth),
            wide(gains.shape[0], width),
            wide(gains.shape[0], width),
            wide(devices, gains.shape[0], depth),
            wide(devices, gains.shape[0], depth),
            wide(gains.shape[0], depth),
            wide(4, gains.shape[0], depth),
            dma((3, 2, spans)),
            dma((3, 2, spans)),
            dma((chunks, 2, spans)),
            dma((chunks, 2, spans)),
            dma((11,)),
            dma((11,)),
            dma((chunks + 2, 2, spans)),
            dma((chunks + 2, 2, spans)),
            dma((chunks + 2, 4)),
            dma((2,)),
            dma((2,)),
            dma((4, strips)),
            dma((4, strips)),
            dma((2, strips)),
            dma((2, strips)),
            dma((9,)),
            dma((9,)),
            dma((devices,)),
            dma((devices,)),
            dma((4,)),
            dma((4,)),
            dma((3 + chunks,)),
            dma((10,)),
            dma((6,)),
            dma((2, chunks)),
            dma((9,)),
            dma((max(8, spans * 2),)),
            dma((8,)),
            pltpu.SemaphoreType.REGULAR,
        ],
        compiler_params=pltpu.CompilerParams(
            collective_id=0, has_side_effects=True, vmem_limit_bytes=63 * MEGABYTE
        ),
        name="whole_layer",
    )(x, cot, proj, out, gateup, down, gains, cosine, sine)


def adamw(weight, grad, first, second, rate, decay):
    first = BETA_ONE * first + (1.0 - BETA_ONE) * grad
    second = BETA_TWO * second + (1.0 - BETA_TWO) * grad * grad
    fixed_first = first * (1.0 / (1.0 - BETA_ONE**STEP))
    fixed_second = second * (1.0 / (1.0 - BETA_TWO**STEP))
    weight = weight - rate * (fixed_first / (jnp.sqrt(fixed_second) + ADAM_EPS) + decay * weight)
    return (first, second, weight)


def matrix_step(weight, grad, first, second):
    return adamw(weight, grad, first, second, MATRIX_RATE, WEIGHT_DECAY)


def update_kernel(*refs):
    ins, outs = refs[:21], refs[21:]
    query, keyval, output, down, gateup = (ins[3 * k : 3 * k + 3] for k in range(5))
    proj_terms, out_terms, down_sum, gateup_sum, block_low, input_low = ins[15:]
    query_outs, keyval_outs, output_outs, down_outs, gateup_outs = (
        outs[4 * k : 4 * k + 4] for k in range(5)
    )
    block_output, input_grad = outs[20:]
    block_output[...] = block_low[...].astype(WIDE)
    input_grad[...] = input_low[...].astype(WIDE)

    def apply(parts, grad, targets, at=slice(None)):
        weight, first, second = (part[at] for part in parts)
        targets[0][at] = grad
        for target, value in zip(targets[1:], matrix_step(weight, grad, first, second)):
            target[at] = value

    proj = jnp.sum(proj_terms[...].astype(WIDE), axis=0)
    query_width = query[0].shape[1]
    key_width = keyval[0].shape[2]
    apply(query, proj[:, :query_width], query_outs)
    for g in range(2):
        start = query_width + g * key_width
        apply(keyval, proj[:, start : start + key_width], keyval_outs, (slice(None), g))
        apply(gateup, gateup_sum[:, g], gateup_outs, (slice(None), g))
    apply(output, jnp.sum(out_terms[...].astype(WIDE), axis=0), output_outs)
    apply(down, down_sum[...], down_outs)


def update(
    query, keyval, output, down, gateup, proj_terms, out_terms, down_sum, gateup_sum, block, grad
):
    depth = query[0].shape[0]
    rows = min(32, depth)
    steps = depth // rows
    tokens = block.shape[0] // steps

    def by_rows(array, dim=0, rows=rows):
        shape = array.shape[:dim] + (rows,) + array.shape[dim + 1 :]
        place = (0,) * array.ndim
        return pl.BlockSpec(shape, lambda i: place[:dim] + (i,) + place[dim + 1 :])

    matrices = (query, keyval, output, down, gateup)
    blocked = [part for parts in matrices for part in parts]
    made = [parts[0] for parts in matrices for _ in range(4)]
    results = pl.pallas_call(
        update_kernel,
        grid=(steps,),
        in_specs=[by_rows(array) for array in blocked]
        + [by_rows(proj_terms, 1), by_rows(out_terms, 1), by_rows(down_sum), by_rows(gateup_sum)]
        + [by_rows(block, rows=tokens), by_rows(grad, rows=tokens)],
        out_specs=[by_rows(array) for array in made] + [by_rows(block, rows=tokens)] * 2,
        out_shape=[jax.ShapeDtypeStruct(array.shape, WIDE) for array in made + [block, grad]],
        compiler_params=pltpu.CompilerParams(vmem_limit_bytes=56 * MEGABYTE),
        name="update",
    )(*blocked, proj_terms, out_terms, down_sum, gateup_sum, block, grad)
    return [results[4 * k : 4 * k + 4] for k in range(5)] + [results[20:]]


def body(
    block_input,
    cotangent,
    positions,
    query_weight,
    keyval_weight,
    output_weight,
    gateup_weight,
    down_weight,
    norm_gains,
    query_first,
    keyval_first,
    output_first,
    gateup_first,
    down_first,
    gains_first,
    query_second,
    keyval_second,
    output_second,
    gateup_second,
    down_second,
    gains_second,
):
    count, length, width = block_input.shape
    rows = count * length
    depth = query_weight.shape[0]
    query_width = query_weight.shape[1]
    key_width = keyval_weight.shape[2]
    me = lax.axis_index("dp")
    pair_bit = (me // PAIR) % 2

    proj_block = jnp.concatenate(
        [query_weight.astype(LOW), keyval_weight.reshape(depth, 2 * key_width).astype(LOW)], axis=1
    )
    gains_block = jnp.pad(norm_gains.astype(LOW).astype(WIDE), ((0, 6), (0, 0)))
    grad_out = cotangent.reshape(rows, width)
    heads, kv = query_width // HD, key_width // HD
    cosine_pair, sine_pair = angle_tables(positions.reshape(rows))
    _, output_terms, proj_terms, block_low, input_low, gains_sum, gateup_sum, down_sum = whole_layer(
        block_input.reshape(rows, width),
        grad_out,
        proj_block,
        output_weight.astype(LOW),
        gateup_weight,
        down_weight,
        gains_block,
        cosine_pair,
        sine_pair,
        kv,
        count,
    )[:8]
    gains_reduced = gains_sum[:2]
    (
        (query_reduced, query_mean, query_square, query_next),
        (keyval_reduced, keyval_mean, keyval_square, keyval_next),
        (output_reduced, output_mean, output_square, output_next),
        (down_reduced, down_mean, down_square, down_next),
        (gateup_reduced, gateup_mean, gateup_square, gateup_next),
        (block_output, input_grad),
    ) = update(
        (query_weight, query_first, query_second),
        (keyval_weight, keyval_first, keyval_second),
        (output_weight, output_first, output_second),
        (down_weight, down_first, down_second),
        (gateup_weight, gateup_first, gateup_second),
        proj_terms,
        output_terms,
        down_sum,
        gateup_sum,
        block_low,
        input_low,
    )
    gains_mean, gains_square, gains_next = adamw(
        norm_gains, gains_reduced, gains_first, gains_second, GAIN_RATE, 0.0
    )
    return (
        block_output.reshape(count, length, width),
        input_grad.reshape(count, length, width),
        query_reduced,
        keyval_reduced,
        output_reduced,
        gateup_reduced,
        down_reduced,
        gains_reduced,
        query_mean,
        keyval_mean,
        output_mean,
        gateup_mean,
        down_mean,
        gains_mean,
        query_square,
        keyval_square,
        output_square,
        gateup_square,
        down_square,
        gains_square,
        query_next,
        keyval_next,
        output_next,
        gateup_next,
        down_next,
        gains_next,
    )


def solution(mesh):
    in_specs = (
        P("dp", None, None),
        P("dp", None, None),
        P("dp", None),
        P("dp", "tensor"),
        P("dp", None, "tensor"),
        P("dp", "tensor"),
        P("dp", None, "tensor"),
        P("dp", "tensor"),
        P(None, "dp"),
        P("dp", "tensor"),
        P("dp", None, "tensor"),
        P("dp", "tensor"),
        P("dp", None, "tensor"),
        P("dp", "tensor"),
        P(None, "dp"),
        P("dp", "tensor"),
        P("dp", None, "tensor"),
        P("dp", "tensor"),
        P("dp", None, "tensor"),
        P("dp", "tensor"),
        P(None, "dp"),
    )
    out_specs = (
        P("dp", None, None),
        P("dp", None, None),
        P("dp", "tensor"),
        P("dp", None, "tensor"),
        P("dp", "tensor"),
        P("dp", None, "tensor"),
        P("dp", "tensor"),
        P(None, "dp"),
        P("dp", "tensor"),
        P("dp", None, "tensor"),
        P("dp", "tensor"),
        P("dp", None, "tensor"),
        P("dp", "tensor"),
        P(None, "dp"),
        P("dp", "tensor"),
        P("dp", None, "tensor"),
        P("dp", "tensor"),
        P("dp", None, "tensor"),
        P("dp", "tensor"),
        P(None, "dp"),
        P("dp", "tensor"),
        P("dp", None, "tensor"),
        P("dp", "tensor"),
        P("dp", None, "tensor"),
        P("dp", "tensor"),
        P(None, "dp"),
    )
    return jax.shard_map(body, mesh=mesh, in_specs=in_specs, out_specs=out_specs, check_vma=False)
```

```python
import functools
import math

import jax
import jax.numpy as jnp
from jax import lax
from jax.experimental import pallas as pl
from jax.experimental.pallas import tpu as pltpu
from jax.sharding import PartitionSpec as P

HD = 64
STEP = 10

NORM_EPS = 1e-05
ROPE_BASE = 500000.0
BETA_ONE = 0.9
BETA_TWO = 0.95
ADAM_EPS = 1e-08
MATRIX_RATE = 0.05
GAIN_RATE = 0.6
WEIGHT_DECAY = 0.1
MASKED = -1e30

PAIR = 2
CHUNKS = 4

LANES = 128

LOW = jnp.bfloat16
WIDE = jnp.float32
ROWS_BY_ROWS = (((1,), (1,)), ((), ()))
COLUMNS_BY_COLUMNS = (((0,), (0,)), ((), ()))


def dot(left, right, dims=(((1,), (0,)), ((), ()))):
    return lax.dot_general(left, right, dims, preferred_element_type=WIDE)


def swap(values, axis, mask):
    pairs = [(k, k ^ mask) for k in range(lax.axis_size(axis))]
    return lax.ppermute(values, axis, pairs)


def part(values, index, parts, dim):
    size = values.shape[dim] // parts
    return lax.dynamic_slice_in_dim(values, index * size, size, dim)


def join(mine, other, bit, dim):
    first = jnp.concatenate([mine, other], axis=dim)
    second = jnp.concatenate([other, mine], axis=dim)
    return jnp.where(bit == 0, first, second)


def rms_factor(values):
    return lax.rsqrt(jnp.mean(values * values, axis=-1, keepdims=True) + NORM_EPS)


def rms_backward(values, gain, grad):
    factor = rms_factor(values)
    scaled = grad * gain
    inner = jnp.mean(scaled * values, axis=-1, keepdims=True)
    grad_values = factor * scaled - values * (factor * factor * factor * inner)
    grad_gain = jnp.sum(grad * values * factor, axis=0)
    return grad_values, grad_gain


def attend_group(j, group, block, count, length, query_ref, key_ref, value_ref, mixed_ref, logsum_ref):
    row_index = lax.broadcasted_iota(jnp.int32, (block, block), 0)
    column_index = lax.broadcasted_iota(jnp.int32, (block, block), 1)
    allowed = column_index <= row_index
    for sequence in range(count):
        base = sequence * length
        for head in range(group):
            columns = slice((j * group + head) * HD, (j * group + head + 1) * HD)
            for start in range(base, base + length, block):
                rows = slice(start, start + block)
                before = slice(base, start)
                query = query_ref[rows, columns] * HD ** (-0.5)
                last = jnp.where(allowed, dot(query, key_ref[j, rows], ROWS_BY_ROWS), MASKED)
                highest = jnp.max(last, axis=-1, keepdims=True)
                if start > base:
                    early = dot(query, key_ref[j, before], ROWS_BY_ROWS)
                    highest = jnp.maximum(highest, jnp.max(early, axis=-1, keepdims=True))
                    early = jnp.exp(early - highest)
                last = jnp.exp(last - highest)
                total = jnp.sum(last, axis=-1, keepdims=True)
                if start > base:
                    total = total + jnp.sum(early, axis=-1, keepdims=True)
                share = 1.0 / total
                mixed = dot((last * share).astype(LOW), value_ref[j, rows])
                if start > base:
                    mixed = mixed + dot((early * share).astype(LOW), value_ref[j, before])
                mixed_ref[rows, columns] = mixed.astype(LOW)
                logsum_ref[j, rows, head : head + 1] = highest + jnp.log(total)


MESH = pl.DeviceIdType.MESH
MEGABYTE = 1 << 20


def flip(index, mask):
    bit = 1
    while bit <= mask:
        if mask & bit:
            index = index + bit - 2 * bit * lax.rem(lax.div(index, bit), 2)
        bit *= 2
    return index


def remote(source, target, sems, axis, mask):
    return pltpu.make_async_remote_copy(
        src_ref=source,
        dst_ref=target,
        send_sem=sems[0],
        recv_sem=sems[1],
        device_id={axis: flip(lax.axis_index(axis), mask)},
        device_id_type=MESH,
    )


def greet(partners):
    barrier = pltpu.get_barrier_semaphore()
    for axis, mask in partners:
        pl.semaphore_signal(
            barrier,
            inc=1,
            device_id={axis: flip(lax.axis_index(axis), mask)},
            device_id_type=MESH,
        )
    pl.semaphore_wait(barrier, len(partners))


class Gather:
    def __init__(self, masks, source, place, sems):
        self.masks, self.source, self.place, self.sems = masks, source, place, sems
        self.me = lax.axis_index("dp")

    def sem(self, phase, mask):
        send, recv = self.sems
        return send.at[phase, mask // 2], recv.at[phase, mask // 2]

    def far_copy(self, mask):
        return remote(self.source(mask), self.place(self.me), self.sem(0, mask), "dp", mask)

    def near_copy(self, mask):
        here = self.place(flip(self.me, mask))
        return remote(here if mask else self.source(0), here, self.sem(1, mask), "dp", 1)

    def start(self):
        for mask in self.masks[1:]:
            self.far_copy(mask).start()

    def start_own(self):
        self.near_copy(0).start()

    def forward(self, mask):
        here = self.place(flip(self.me, mask))
        remote(here, here, self.sem(0, mask), "dp", mask).wait_recv()
        self.near_copy(mask).start()

    def arrive(self):
        for mask in self.masks:
            here = self.place(flip(self.me, mask ^ 1))
            remote(here, here, self.sem(1, mask), "dp", 1).wait_recv()

    def drain(self):
        for mask in self.masks[1:]:
            self.far_copy(mask).wait_send()
        for mask in self.masks:
            self.near_copy(mask).wait_send()


def rotated(values, cosine, sine, first):
    width = values.shape[1]
    turned = jnp.where(
        first, pltpu.roll(values, width - HD // 2, 1), pltpu.roll(values, HD // 2, 1)
    )
    return values * cosine + turned * sine


SLOTS = 2


class Scatter:
    def __init__(self, masks, product, landing, target, landed, stage, sems):
        self.masks, self.product, self.landing = masks, product, landing
        self.target, self.landed, self.stage, self.sems = target, landed, stage, sems
        self.me = lax.axis_index("dp")
        self.depth = product.shape[0] // lax.axis_size("dp")

    def rows(self, owner):
        return pl.ds(pl.multiple_of(owner * self.depth, self.depth), self.depth)

    def copy(self, phase, mask, source, target):
        send, recv, _ = self.sems
        at = mask // 2
        axis_mask = 1 if phase == 0 else mask
        return remote(source, target, (send.at[phase, at], recv.at[phase, at]), "dp", axis_mask)

    def start(self):
        for mask in self.masks[1:] + [0]:
            self.near_copy(mask).start()

    def near_copy(self, mask):
        source = self.product.at[self.rows(flip(self.me, mask ^ 1))]
        return self.copy(0, mask, source, self.landing.at[mask // 2])

    def load_copy(self, index, mask):
        return pltpu.make_async_copy(
            self.landing.at[mask // 2], self.stage.at[index % 2], self.sems[2].at[index % 2]
        )

    def store_copy(self, index, mask):
        target = self.landing.at[mask // 2] if mask else self.target(0)
        return pltpu.make_async_copy(
            self.stage.at[index % 2], target, self.sems[2].at[2 + index % 2]
        )

    def far_copy(self, mask):
        return self.copy(1, mask, self.landing.at[mask // 2], self.target(mask))

    def steps(self):
        order = self.masks[1:] + [0]
        for step in range(len(order) + 2):
            if step >= 2:
                mask = order[step - 2]
                self.store_copy(step - 2, mask).wait()
                if mask:
                    self.far_copy(mask).start()
            if step < len(order):
                mask = order[step]
                landed = self.landing.at[mask // 2]
                self.copy(0, mask, landed, landed).wait_recv()
                self.load_copy(step, mask).start()
            if 1 <= step <= len(order):
                mask = order[step - 1]
                slot = (step - 1) % 2
                self.load_copy(step - 1, mask).wait()
                at = self.rows(flip(self.me, mask))
                total = self.product[at].astype(WIDE) + self.stage[slot].astype(WIDE)
                self.stage[slot] = total.astype(LOW)
                self.store_copy(step - 1, mask).start()
            yield

    def pump(self):
        for _ in self.steps():
            pass

    def free(self):
        for mask in self.masks:
            self.near_copy(mask).wait_send()

    def release(self):
        for mask in self.masks[1:]:
            self.far_copy(mask).wait_send()

    def arrive(self):
        for mask in self.masks[1:]:
            landed = self.landed(mask)
            self.copy(1, mask, landed, landed).wait_recv()


def attend_back_group(
    j,
    group,
    block,
    count,
    length,
    query_ref,
    key_ref,
    value_ref,
    logsum_ref,
    grad_ref,
    query_grad_ref,
    key_grad_ref,
    value_grad_ref,
):
    key_index = lax.broadcasted_iota(jnp.int32, (block, block), 0)
    query_index = lax.broadcasted_iota(jnp.int32, (block, block), 1)
    allowed = key_index <= query_index
    scale = HD ** (-0.5)
    for sequence in range(count):
        base = sequence * length
        for head in range(group):
            columns = slice((j * group + head) * HD, (j * group + head + 1) * HD)
            for start in range(base, base + length, block):
                rows = slice(start, start + block)
                query = query_ref[rows, columns] * scale
                grad = grad_ref[rows, columns]
                logsum = logsum_ref[j, head : head + 1, rows]
                spans = [(rows, True)]
                if start > base:
                    spans.append((slice(base, start), False))
                probs, grad_probs = [], []
                for span, masked in spans:
                    scores = dot(key_ref[j, span], query, ROWS_BY_ROWS)
                    if masked:
                        scores = jnp.where(allowed, scores, MASKED)
                    probs.append(jnp.exp(scores - logsum))
                    grad_probs.append(dot(value_ref[j, span], grad, ROWS_BY_ROWS))
                inner = sum(
                    jnp.sum(one * two, axis=0, keepdims=True)
                    for one, two in zip(probs, grad_probs)
                )
                query_grad = None
                for (span, _), one, two in zip(spans, probs, grad_probs):
                    grad_scores = (one * (two - inner)).astype(LOW)
                    term = dot(grad_scores, key_ref[j, span], COLUMNS_BY_COLUMNS)
                    query_grad = term if query_grad is None else query_grad + term
                    key_grad_ref[j, span] += dot(grad_scores, query)
                    value_grad_ref[j, span] += dot(one.astype(LOW), grad)
                query_grad_ref[rows, columns] = query_grad * scale


def whole_kernel(
    sizes,
    x_ref,
    cot_ref,
    places_ref,
    query_weight,
    keyval_weight,
    output_weight,
    gateup_ref,
    down_ref,
    gains_in,
    hidden_terms,
    out_terms,
    proj_terms,
    output_ref,
    input_grad_ref,
    gains_sum,
    gateup_sum,
    down_sum,
    hidden_ref,
    hidden_full,
    proj_full,
    out_full,
    other_cot,
    both_ref,
    hidden_land,
    out_land,
    proj_land,
    middle_low,
    line_land,
    saved_normalized,
    saved_query,
    saved_key,
    saved_value,
    saved_mixed,
    saved_middle,
    cosine_ref,
    sine_ref,
    product,
    stage,
    core_out,
    core_in,
    held,
    keep,
    line_out,
    line_in,
    last_in,
    pair_in,
    flat,
    middle,
    low_out,
    logsums,
    proj_ref,
    out_ref,
    gains_ref,
    gains_slots,
    gains_full,
    gain_rows,
    gain_blocks,
    gain_land,
    gain_part,
    tensor_land,
    gather_send,
    gather_recv,
    weight_send,
    weight_recv,
    token_send,
    token_recv,
    scatter_send,
    scatter_recv,
    scatter_local,
    core_send,
    core_recv,
    line_send,
    line_recv,
    pair_send,
    pair_recv,
    spread_send,
    spread_recv,
    gain_send,
    gain_recv,
    tensor_send,
    tensor_recv,
    own_sem,
    load_sem,
    save_sem,
    strip_sem,
    local_sem,
    final_sem,
    final_out_sem,
    credit,
):
    count, length = sizes
    rows, width = cot_ref.shape
    devices = lax.axis_size("dp")
    masks = list(range(0, devices, 2))
    me = lax.axis_index("dp")
    tensor = lax.axis_index("tensor")
    core, line = lax.rem(tensor, 2), lax.div(tensor, 2)
    pair_bit = lax.rem(lax.div(me, PAIR), 2)
    depth = proj_ref.shape[0]
    chunks = hidden_full.shape[0]
    unit = hidden_full.shape[2] // 3
    half, piece = rows // 2, rows // 4
    strips, strip = keep.shape[0], keep.shape[2]
    query_width = saved_query.shape[1]
    kv = saved_key.shape[0]
    group = query_width // (kv * HD)
    block = min(256, length)
    casts = [
        pltpu.make_async_copy(source, middle.at[pl.ds(0, depth), at], load_sem.at[index])
        for index, (source, at) in enumerate(
            [
                (query_weight, pl.ds(0, query_width)),
                (output_weight, pl.ds(query_width, query_width)),
                (keyval_weight.at[:, 0], pl.ds(2 * query_width, kv * HD)),
                (keyval_weight.at[:, 1], pl.ds(2 * query_width + kv * HD, kv * HD)),
            ]
        )
    ]
    for copy in casts:
        copy.start()
    greet(
        [("dp", mask) for mask in range(1, devices)] + [("tensor", mask) for mask in range(1, 4)]
    )

    def block_rows(ref):
        return lambda owner: ref.at[pl.ds(pl.multiple_of(owner * depth, depth), depth)]

    def pair_half(mask):
        return pair_bit if not mask & PAIR else 1 - pair_bit

    def gather(index, ref, place_of):
        sems = gather_send.at[index], gather_recv.at[index]
        return Gather(masks, lambda mask: ref, place_of, sems)

    gains = gather(0, gains_ref, lambda owner: gains_slots.at[owner])
    proj_in = gather(1, proj_ref, block_rows(proj_full))
    out_in = gather(2, out_ref, block_rows(out_full))
    hidden_in = [
        Gather(
            masks,
            lambda mask, c=c: hidden_ref.at[pair_half(mask), c],
            block_rows(hidden_full.at[c]),
            (weight_send.at[c], weight_recv.at[c]),
        )
        for c in range(chunks)
    ]

    def own_copy(index):
        one = ([gains, proj_in, out_in] + hidden_in)[index]
        return pltpu.make_async_copy(one.source(0), one.place(me), own_sem.at[index])

    def pump(c):
        for mask in masks[1:]:
            hidden_in[c].forward(mask)

    quarter = pl.ds(pl.multiple_of(core * half + line * piece, piece), piece)
    near_half = pl.multiple_of(core * half, half)
    far_half = pl.multiple_of((1 - core) * half, half)
    near_line = pl.ds(pl.multiple_of(line * piece, piece), piece)
    far_line = pl.ds(pl.multiple_of((1 - line) * piece, piece), piece)

    def place(ref, core_at, line_at):
        return ref.at[pl.ds(pl.multiple_of(core_at * half + line_at * piece, piece), piece)]

    near_ref, far_ref = both_ref.at[0], both_ref.at[1]

    def token_ends(index):
        cot_near, cot_there = place(other_cot, core, line), place(other_cot, core, 1 - line)
        near, near_there = place(near_ref, core, line), place(near_ref, core, 1 - line)
        far, far_there = place(far_ref, core, line), place(far_ref, core, 1 - line)
        return [
            lambda: (place(cot_ref, core, line), cot_near, "dp", PAIR, cot_near),
            lambda: (cot_near, cot_near, "tensor", 2, cot_there),
            lambda: (cot_near, cot_near, "tensor", 1, place(other_cot, 1 - core, line)),
            lambda: (cot_there, cot_there, "tensor", 1, place(other_cot, 1 - core, 1 - line)),
            lambda: (low_out, far, "dp", PAIR, far),
            lambda: (low_out, near, "tensor", 2, near_there),
            lambda: (low_out, near, "tensor", 1, place(near_ref, 1 - core, line)),
            lambda: (near_there, near_there, "tensor", 1, place(near_ref, 1 - core, 1 - line)),
            lambda: (far, far, "tensor", 2, far_there),
            lambda: (far, far, "tensor", 1, place(far_ref, 1 - core, line)),
            lambda: (far_there, far_there, "tensor", 1, place(far_ref, 1 - core, 1 - line)),
        ][index]()

    def token(index):
        source, target, axis, mask, _ = token_ends(index)
        sems = token_send.at[index], token_recv.at[index]
        return remote(source, target, sems, axis, mask)

    def token_arrive(*indices):
        for index in indices:
            _, _, axis, mask, landed = token_ends(index)
            sems = token_send.at[index], token_recv.at[index]
            remote(landed, landed, sems, axis, mask).wait_recv()

    def scatter(index, product_ref, landing, target, landed):
        columns = landing.shape[2]
        return Scatter(
            masks,
            product_ref,
            landing,
            target,
            landed,
            stage.at[:, :, :columns] if columns < stage.shape[2] else stage,
            (scatter_send.at[index], scatter_recv.at[index], scatter_local.at[index]),
        )

    hidden = [
        scatter(
            c,
            product.at[c % SLOTS],
            hidden_land.at[c],
            lambda mask, c=c: hidden_terms.at[pair_bit, c, mask // 4],
            lambda mask, c=c: hidden_terms.at[pair_half(mask), c, mask // 4],
        )
        for c in range(chunks)
    ]

    def core_copy(slot, parts):
        return remote(
            core_out.at[slot, pl.ds(0, parts)],
            core_in.at[slot, pl.ds(0, parts)],
            (core_send.at[slot], core_recv.at[slot]),
            "tensor",
            1,
        )

    def line_copy(turn, s, parts, landing, source=line_out):
        return remote(
            source.at[s, pl.ds(0, parts)],
            landing.at[s],
            (line_send.at[turn, s], line_recv.at[turn, s]),
            "tensor",
            2,
        )

    def pair_copy(turn, s, landing):
        return remote(
            line_out.at[s, 1],
            landing.at[s],
            (pair_send.at[turn, s], pair_recv.at[turn, s]),
            "dp",
            PAIR,
        )

    def reduce_strips(
        turn, parts, term, prepare, landing, source=line_out, kept=keep, between=()
    ):
        def finish(s, slot):
            core_copy(slot, parts).wait_recv()
            near = []
            for q in range(parts):
                source[s, q] = (
                    held[q, far_line] + core_in[slot, q, far_line].astype(WIDE)
                ).astype(LOW)
                near.append(held[q, near_line] + core_in[slot, q, near_line].astype(WIDE))
            kept[s] = near[0]
            if parts == 2:
                flat[:, pl.ds(pl.multiple_of(s * strip, strip), strip)] = near[1]
            pl.semaphore_signal(
                credit, inc=1, device_id={"tensor": flip(tensor, 1)}, device_id_type=MESH
            )
            line_copy(turn, s, parts, landing, source).start()

        def one_strip(s, carry):
            slot = lax.rem(s, 2)
            prepare(s, slot)

            @pl.when(s >= 2)
            def _():
                core_copy(slot, parts).wait_send()

            for q in range(parts):
                core_out[slot, q] = term(q, far_half, s, slot).astype(LOW)
            if turn:
                pl.semaphore_wait(credit, 1)
            else:

                @pl.when(s >= 2)
                def _():
                    pl.semaphore_wait(credit, 1)

            core_copy(slot, parts).start()

            @pl.when(s >= 1)
            def _():
                finish(s - 1, 1 - slot)

            for q in range(parts):
                held[q] = term(q, near_half, s, slot)
            return carry

        cuts = [strips * cut // (len(between) + 1) for cut in range(len(between) + 2)]
        for first, last, step in zip(cuts[:-1], cuts[1:], list(between) + [None]):
            lax.fori_loop(first, last, one_strip, 0)
            if step is not None:
                step()
        finish(strips - 1, (strips - 1) % 2)
        for slot in range(2):
            core_copy(slot, parts).wait_send()

    def strip_loads(s, slot):
        return [
            pltpu.make_async_copy(
                hidden_full.at[c, pl.ds(pl.multiple_of(s * strip, strip), strip)],
                weights.at[pl.ds(pl.multiple_of((slot * chunks + c) * strip, strip), strip)],
                strip_sem.at[slot, c],
            )
            for c in range(chunks)
        ]

    def start_strip(s, slot):
        for copy in strip_loads(s, slot):
            copy.start()

    def prepare_strip(s, slot):
        @pl.when(s + 1 < strips)
        def _():
            start_strip(s + 1, 1 - slot)

        for copy in strip_loads(s, slot):
            copy.wait()

    def hidden_term(ref, first, wide):
        def term(q, start, s, slot):
            at = pl.ds(pl.multiple_of(q * rows + start, half), half)
            total = None
            for c in range(chunks):
                block = weights[
                    pl.ds(pl.multiple_of((slot * chunks + c) * strip, strip), strip),
                    first : first + wide,
                ]
                one = dot(ref[at, c * wide : (c + 1) * wide], block, ROWS_BY_ROWS)
                total = one if total is None else total + one
            return total

        return term

    def to_pair_strip(turn, landing, s):
        copy = line_copy(turn, s, 2, landing)
        if landing is line_in:
            copy.wait_recv()
        copy.wait_send()
        columns = slice(s * strip, (s + 1) * strip)
        line_out[s, 1] = (flat[:, columns] + line_in[s, 1].astype(WIDE)).astype(LOW)
        pair_copy(turn - 1, s, pair_in.at[turn - 1]).start()
        flat[:, columns] = keep[s] + line_in[s, 0].astype(WIDE)

    def to_pair(turn, landing):
        if landing is not line_in:
            for s in range(strips):
                line_copy(turn, s, 2, landing).wait_recv()
            copy = pltpu.make_async_copy(landing, line_in, load_sem.at[0])
            copy.start()
            copy.wait()
        for s in range(strips):
            to_pair_strip(turn, landing, s)

    def from_pair(turn):
        for s in range(strips):
            copy = pair_copy(turn - 1, s, pair_in.at[turn - 1])
            copy.wait_recv()
            copy.wait_send()
            flat[:, s * strip : (s + 1) * strip] += pair_in[turn - 1, s].astype(WIDE)

    tile = min(64, piece)

    def rms_back(values_of, gain, grads_of, store, gain_row):
        def one_tile(index, total):
            at = pl.ds(pl.multiple_of(index * tile, tile), tile)
            there = pl.ds(pl.multiple_of(core * half + line * piece + index * tile, tile), tile)
            values, grads = values_of(at), grads_of(at)
            grad_values, grad_gain = rms_backward(values, gain, grads)
            store(at, there, grad_values)
            return total + grad_gain[None]

        zero = jnp.zeros((1, width), WIDE)
        gain_rows[gain_row : gain_row + 1] = lax.fori_loop(0, piece // tile, one_tile, zero)

    def spread_copy(index, source, target, mask):
        return remote(
            source, target, (spread_send.at[index], spread_recv.at[index]), "tensor", mask
        )

    def spread(base, source, target):
        here = place(target, core, line)
        spread_copy(base, source, here, 2).start()
        spread_copy(base + 1, source, here, 1).start()
        pltpu.make_async_copy(source, here, local_sem.at[base]).start()

    def spread_on(base, target):
        there = place(target, core, 1 - line)
        spread_copy(base, there, there, 2).wait_recv()
        spread_copy(base + 2, there, there, 1).start()

    def spread_release(base, source, target):
        here, there = place(target, core, line), place(target, core, 1 - line)
        spread_copy(base, source, here, 2).wait_send()
        spread_copy(base + 1, source, here, 1).wait_send()
        spread_copy(base + 2, there, there, 1).wait_send()
        pltpu.make_async_copy(source, here, local_sem.at[base]).wait()

    def spread_end(base, target):
        near, far = place(target, 1 - core, line), place(target, 1 - core, 1 - line)
        spread_copy(base + 1, near, near, 1).wait_recv()
        spread_copy(base + 2, far, far, 1).wait_recv()

    def gain_copy(mask):
        return remote(
            gain_blocks.at[flip(me, mask)],
            gain_land.at[mask],
            (gain_send.at[mask], gain_recv.at[mask]),
            "dp",
            mask,
        )

    def tensor_copy(mask):
        return remote(
            gain_part,
            tensor_land.at[mask],
            (tensor_send.at[mask], tensor_recv.at[mask]),
            "tensor",
            mask,
        )

    def lanes_turned(values, cosine, sine):
        times = values.shape[1] // cosine.shape[1]
        lanes = lax.broadcasted_iota(jnp.int32, values.shape, 1)
        return rotated(
            values,
            jnp.concatenate([cosine] * times, axis=1),
            jnp.concatenate([sine] * times, axis=1),
            lax.rem(lanes, HD) < HD // 2,
        ).astype(LOW)

    tokens = min(256, rows)

    def tile_at(index, size):
        return pl.ds(pl.multiple_of(index * size, size), size)

    for copy in casts:
        copy.wait()
    narrow = middle[:depth]
    proj_ref[:, :query_width] = narrow[:, :query_width].astype(LOW)
    proj_ref[:, query_width:] = narrow[:, 2 * query_width : 2 * query_width + 2 * kv * HD].astype(LOW)
    gains_ref[...] = jnp.zeros_like(gains_ref)
    gains_ref[0:2] = gains_in[...].astype(LOW).astype(WIDE)
    gains.start()
    proj_in.start()
    gains.start_own()
    proj_in.start_own()
    out_ref[...] = narrow[:, query_width : 2 * query_width].astype(LOW)
    for index in range(3):
        own_copy(index).start()

    def attention(
        x,
        normalized,
        proj,
        out,
        query,
        key,
        value,
        mixed,
        logsum,
        cosines,
        sines,
        gateup,
        down,
        blocks,
    ):
        loads = [
            pltpu.make_async_copy(source, target, load_sem.at[index])
            for index, (source, target) in enumerate(
                [
                    (x_ref, x),
                    (gateup_ref.at[:, 0], gateup.at[0]),
                    (gateup_ref.at[:, 1], gateup.at[1]),
                    (down_ref, down),
                ]
            )
        ]
        for copy in loads:
            copy.start()
        logsum[...] = jnp.zeros_like(logsum)
        for mask in masks[1:]:
            gains.forward(mask)
        proj_in.forward(masks[1])
        out_in.start()
        out_in.start_own()
        gains.arrive()
        own_copy(0).wait()
        gains_full[...] = jnp.concatenate([gains_slots[j] for j in range(devices)], axis=1)
        for copy in loads:
            copy.wait()

        def norm_tile(index, carry):
            at = tile_at(index, tokens)
            values = x[at].astype(WIDE)
            normalized[at] = (values * rms_factor(values) * gains_full[0:1]).astype(LOW)
            return carry

        lax.fori_loop(0, rows // tokens, norm_tile, 0)
        saves = [
            pltpu.make_async_copy(source, target, save_sem.at[index])
            for index, (source, target) in enumerate(
                [
                    (normalized, saved_normalized),
                    (query, saved_query),
                    (key, saved_key),
                    (value, saved_value),
                    (mixed, saved_mixed),
                    (middle, saved_middle),
                    (cosines, cosine_ref),
                    (sines, sine_ref),
                ]
            )
        ]
        saves[0].start()
        steps = lax.broadcasted_iota(jnp.int32, (2 * HD, rows), 0) % HD
        frequency = jnp.exp((steps % (HD // 2)).astype(WIDE) * (-2.0 / HD * math.log(ROPE_BASE)))
        angles = places_ref[...].astype(WIDE) * frequency
        cosines[...] = jnp.cos(angles).T
        sines[...] = jnp.where(steps < HD // 2, -jnp.sin(angles), jnp.sin(angles)).T
        saves[6].start()
        saves[7].start()
        tiles = 2 * unit // LANES
        stores = []
        for index in range(2 * chunks):
            h, c = index // chunks, index % chunks
            for j in range(tiles):
                first = index * unit + (j // 2) * LANES
                lanes = gateup[j % 2, :, first : first + LANES]
                blocks[h, c, :, j * LANES : (j + 1) * LANES] = lanes.astype(LOW)
            blocks[h, c, :, 2 * unit :] = down[:, index * unit : (index + 1) * unit].astype(LOW)
            copy = pltpu.make_async_copy(
                blocks.at[h, c], hidden_ref.at[h, c], final_sem.at[index]
            )
            copy.start()
            stores.append(copy)
        for copy in stores:
            copy.wait()
        for index in range(chunks):
            own_copy(3 + index).start()
        for mask in masks[2:]:
            proj_in.forward(mask)
            if mask == masks[2]:
                token(0).start()
                hidden_in[0].start()
        hidden_in[1].start()
        hidden_in[0].start_own()
        hidden_in[1].start_own()
        proj_in.arrive()
        own_copy(1).wait()
        load_proj = pltpu.make_async_copy(proj_full, proj, load_sem.at[6])
        load_proj.start()
        load_proj.wait()

        def project_tile(index, carry):
            at = tile_at(index, tokens)
            pre = dot(normalized[at], proj[...])
            cosine, sine = cosines[at], sines[at]
            query[at] = lanes_turned(pre[:, :query_width], cosine, sine)
            keys = lanes_turned(pre[:, query_width : query_width + kv * HD], cosine, sine)
            values = pre[:, query_width + kv * HD :].astype(LOW)
            for j in range(kv):
                key[j, at] = keys[:, j * HD : (j + 1) * HD]
                value[j, at] = values[:, j * HD : (j + 1) * HD]
            return carry

        lax.fori_loop(0, rows // tokens, project_tile, 0)
        for copy in saves[1:4]:
            copy.start()
        for j in range(kv):
            attend_group(j, group, block, count, length, query, key, value, mixed, logsum)
            if j == 0:
                token_arrive(0)
                token(1).start()
                token(2).start()
                for mask in masks[1:]:
                    out_in.forward(mask)
        saves[4].start()
        for j in range(kv):
            logsums[j] = logsum[j].T[: logsums.shape[1]]
        out_in.arrive()
        own_copy(2).wait()
        load_out = pltpu.make_async_copy(out_full, out, load_sem.at[7])
        load_out.start()
        load_out.wait()

        def out_term(q, start, s, slot):
            return dot(
                mixed[pl.ds(start, half)],
                out[pl.ds(pl.multiple_of(s * strip, strip), strip)],
                ROWS_BY_ROWS,
            )

        reduce_strips(0, 1, out_term, lambda s, slot: None, last_in)
        pump(0)
        for s in range(strips):
            copy = line_copy(0, s, 1, last_in)
            copy.wait_recv()
            copy.wait_send()
            columns = slice(s * strip, (s + 1) * strip)
            middle[:, columns] = (
                x[quarter, columns].astype(WIDE) + keep[s] + last_in[s, 0].astype(WIDE)
            )
        saves[5].start()
        values = middle[...]
        low_out[...] = (values * rms_factor(values) * gains_full[1:2]).astype(LOW)
        for index in (4, 5, 6):
            token(index).start()
        for c in range(2, chunks):
            hidden_in[c].start()
            hidden_in[c].start_own()
        for copy in saves:
            copy.wait()

    pl.run_scoped(
        attention,
        pltpu.VMEM((rows, width), LOW),
        pltpu.VMEM((rows, width), LOW),
        pltpu.VMEM(proj_full.shape, LOW),
        pltpu.VMEM(out_full.shape, LOW),
        pltpu.VMEM(saved_query.shape, LOW),
        pltpu.VMEM(saved_key.shape, LOW),
        pltpu.VMEM(saved_value.shape, LOW),
        pltpu.VMEM(saved_mixed.shape, LOW),
        pltpu.VMEM((kv, rows, 128), WIDE),
        pltpu.VMEM(cosine_ref.shape, WIDE),
        pltpu.VMEM(sine_ref.shape, WIDE),
        pltpu.VMEM((2,) + down_ref.shape, WIDE),
        pltpu.VMEM(down_ref.shape, WIDE),
        pltpu.VMEM(hidden_ref.shape, LOW),
    )

    weights = None

    def feed_forward(normed, grads, weights_ref, gate_ref, hidden_out):
        nonlocal weights
        weights = weights_ref
        load_cot = pltpu.make_async_copy(cot_ref, grads.at[pl.ds(0, rows)], load_sem.at[0])
        load_cot.start()
        place_own = pltpu.make_async_copy(low_out, place(near_ref, core, line), local_sem.at[1])
        place_own.start()
        pump(1)
        token_arrive(5)
        token(7).start()
        token_arrive(1)
        token(3).start()
        token_arrive(4)
        token(8).start()
        token(9).start()
        pump(2)
        place_own.wait()
        token_arrive(6, 7, 2, 3)
        loads = [
            load_cot,
            pltpu.make_async_copy(near_ref, normed.at[pl.ds(0, rows)], load_sem.at[1]),
            pltpu.make_async_copy(other_cot, grads.at[pl.ds(rows, rows)], load_sem.at[2]),
            pltpu.make_async_copy(far_ref, normed.at[pl.ds(rows, rows)], load_sem.at[3]),
        ]
        loads[1].start()
        loads[2].start()

        def load_weights(c):
            hidden_in[c].arrive()
            own_copy(3 + c).wait()
            copy = pltpu.make_async_copy(hidden_full.at[c], weights, load_sem.at[4])
            copy.start()
            return copy

        waiting = [load_weights(0)]
        token_arrive(8)
        token(10).start()
        token_arrive(9, 10)
        loads[3].start()
        for copy in loads:
            copy.wait()
        half_tokens = min(512, 2 * rows)

        def stage_one(c):
            (waiting.pop() if waiting else load_weights(c)).wait()

            def one_tile(index, carry):
                at = tile_at(index, half_tokens)
                gate_up = dot(normed[at], weights[:, : 2 * unit])
                grad_hidden = dot(grads[at], weights[:, 2 * unit :])
                spans = range(0, 2 * unit, 2 * LANES)
                gate = jnp.concatenate([gate_up[:, one : one + LANES] for one in spans], axis=1)
                upward = jnp.concatenate(
                    [gate_up[:, one + LANES : one + 2 * LANES] for one in spans], axis=1
                )
                sigma = jax.nn.sigmoid(gate)
                passed = gate * sigma
                hidden_out[at, c * unit : (c + 1) * unit] = (passed * upward).astype(LOW)
                grad_gate = grad_hidden * upward * sigma * (1.0 + gate * (1.0 - sigma))
                first = 2 * c * unit
                grad_gate = grad_gate.astype(LOW)
                grad_up = (grad_hidden * passed).astype(LOW)
                for one in range(0, unit, LANES):
                    to = first + 2 * one
                    gate_ref[at, to : to + LANES] = grad_gate[:, one : one + LANES]
                    gate_ref[at, to + LANES : to + 2 * LANES] = grad_up[:, one : one + LANES]
                return carry

            lax.fori_loop(0, 2 * rows // half_tokens, one_tile, 0)

        columns = min(512, width)

        def stage_two(c):
            if c >= SLOTS:
                hidden[c - SLOTS].free()

            def one_tile(index, carry):
                at = pl.ds(pl.multiple_of(index * columns, columns), columns)
                gate_up = dot(
                    normed[:, at], gate_ref[:, 2 * c * unit : 2 * (c + 1) * unit], COLUMNS_BY_COLUMNS
                )
                down = dot(grads[:, at], hidden_out[:, c * unit : (c + 1) * unit], COLUMNS_BY_COLUMNS)
                product[c % SLOTS, at, : 2 * unit] = gate_up.astype(LOW)
                product[c % SLOTS, at, 2 * unit :] = down.astype(LOW)
                return carry

            lax.fori_loop(0, width // columns, one_tile, 0)
            hidden[c].start()

        gain_rows[...] = jnp.zeros_like(gain_rows)
        stage_one(0)
        waiting.append(load_weights(1))
        hidden_in[3].forward(masks[1])
        stage_one(1)
        hidden_in[3].forward(masks[2])
        stage_one(2)
        for mask in masks[3:]:
            hidden_in[3].forward(mask)
        stage_two(0)
        stage_one(3)
        start_strip(0, 0)
        early = hidden[0].steps()

        def pump_step():
            next(early)

        reduce_strips(
            1,
            2,
            hidden_term(gate_ref, 0, 2 * unit),
            prepare_strip,
            line_in,
            between=[pump_step] * 3,
        )
        to_pair_strip(1, line_in, 0)
        to_pair_strip(1, line_in, 1)
        to_pair_strip(1, line_in, 2)
        for _ in early:
            pass
        stage_two(1)
        to_pair_strip(1, line_in, 3)
        to_pair_strip(1, line_in, 4)
        stage_two(2)
        for s in range(5, strips):
            to_pair_strip(1, line_in, s)
        from_pair(1)
        for index in (4, 5, 6):
            token(index).wait_send()

        def store(at, there, grad_values):
            total = grads[there].astype(WIDE) + grad_values
            middle[at] = total
            low_out[at] = total.astype(LOW)

        rms_back(lambda at: middle[at], gains_full[1:2], lambda at: flat[at], store, 1)
        spread(0, low_out, middle_low)
        start_strip(0, 0)
        hidden[1].pump()
        stage_two(3)
        reduce_strips(2, 2, hidden_term(hidden_out, 2 * unit, unit), prepare_strip, line_land)
        spread_on(0, middle_low)

    pl.run_scoped(
        feed_forward,
        pltpu.VMEM((2 * rows, width), LOW),
        pltpu.VMEM((2 * rows, width), LOW),
        pltpu.VMEM((width, 3 * unit), LOW),
        pltpu.VMEM((2 * rows, 2 * unit * chunks), LOW),
        pltpu.VMEM((2 * rows, unit * chunks), LOW),
    )

    def second_phase(
        grads,
        out_weight,
        proj_weight,
        query,
        key,
        value,
        mixed,
        normalized,
        grad_mixed,
        query_grad,
        key_grad,
        value_grad,
        projected,
        out_product,
        proj_product,
        cosines,
        sines,
        low_grad,
        final_out,
        final_down,
    ):
        sources = [out_full, saved_query, saved_key, saved_value, saved_mixed]
        sources += [proj_full, saved_normalized, cosine_ref, sine_ref]
        targets = [out_weight, query, key, value, mixed, proj_weight, normalized, cosines, sines]
        loads = [
            pltpu.make_async_copy(source, target, load_sem.at[index])
            for index, (source, target) in enumerate(zip(sources, targets))
        ]
        loads[0].start()
        key_grad[...] = jnp.zeros_like(key_grad)
        value_grad[...] = jnp.zeros_like(value_grad)
        spread_end(0, middle_low)
        spread_release(0, low_out, middle_low)
        hidden[2].pump()
        load_grads = pltpu.make_async_copy(middle_low, grads, load_sem.at[len(loads)])
        load_grads.start()
        for copy in loads[1:]:
            copy.start()
        loads[0].wait()
        load_grads.wait()
        def mixed_tile(index, carry):
            at = pl.ds(pl.multiple_of(index * tokens, tokens), tokens)
            grad_mixed[at] = dot(grads[at], out_weight[...]).astype(LOW)
            return carry

        lax.fori_loop(0, rows // tokens, mixed_tile, 0)
        for copy in loads[1:5]:
            copy.wait()
        columns = min(256, width)

        def out_tile(index, carry):
            at = pl.ds(pl.multiple_of(index * columns, columns), columns)
            out_product[at] = dot(grads[:, at], mixed[...], COLUMNS_BY_COLUMNS).astype(LOW)
            return carry

        lax.fori_loop(0, width // columns, out_tile, 0)
        out_place = lambda mask: out_terms.at[mask // 2]
        out = scatter(chunks, out_product, out_land, out_place, out_place)
        out.start()
        for j in range(kv):
            attend_back_group(
                j,
                group,
                block,
                count,
                length,
                query,
                key,
                value,
                logsums,
                grad_mixed,
                query_grad,
                key_grad,
                value_grad,
            )
        hidden[3].pump()
        for copy in loads[5:]:
            copy.wait()

        def turn_tile(index, carry):
            at = pl.ds(pl.multiple_of(index * tokens, tokens), tokens)
            cosine, sine = cosines[at], -sines[at]

            keys = jnp.concatenate([key_grad[j, at] for j in range(kv)], axis=1)
            values = jnp.concatenate([value_grad[j, at] for j in range(kv)], axis=1)
            projected[at, :query_width] = lanes_turned(query_grad[at], cosine, sine)
            projected[at, query_width : query_width + kv * HD] = lanes_turned(keys, cosine, sine)
            projected[at, query_width + kv * HD :] = values.astype(LOW)
            return carry

        lax.fori_loop(0, rows // tokens, turn_tile, 0)

        def proj_term(q, start, s, slot):
            return dot(
                projected[pl.ds(start, half)],
                proj_weight[pl.ds(pl.multiple_of(s * strip, strip), strip)],
                ROWS_BY_ROWS,
            )

        def proj_tile(index, carry):
            at = pl.ds(pl.multiple_of(index * columns, columns), columns)
            proj_product[at] = dot(normalized[:, at], projected[...], COLUMNS_BY_COLUMNS).astype(LOW)
            return carry

        lax.fori_loop(0, width // columns, proj_tile, 0)
        proj_place = lambda mask: proj_terms.at[mask // 2]
        proj = scatter(chunks + 1, proj_product, proj_land, proj_place, proj_place)
        proj.start()
        to_pair(2, line_land)
        reduce_strips(3, 1, proj_term, lambda s, slot: None, last_in)
        out.pump()
        hidden[chunks - 2].free()
        terms = hidden_terms.shape[2]

        def final_load(h, c, k):
            return pltpu.make_async_copy(
                hidden_terms.at[h, c, k],
                product.at[0, pl.ds(((2 * h + c % 2) * terms + k) * depth, depth)],
                final_sem.at[(2 * h + c % 2) * terms + k],
            )

        def final_gateup(h, g, first):
            at = pl.ds((h * chunks + first) * unit, 2 * unit)
            return pltpu.make_async_copy(
                final_out.at[g], gateup_sum.at[:, g, at], final_out_sem.at[2 * h + g]
            )

        def final_rest(h, c):
            at = pl.ds((h * chunks + c) * unit, unit)
            return pltpu.make_async_copy(
                final_down.at[h, c % 2], down_sum.at[:, at], final_out_sem.at[4 + 2 * h + c % 2]
            )

        def finalize(first):
            for c in (first, first + 1):
                hidden[c].arrive()
                for h in range(2):
                    for k in range(terms):
                        final_load(h, c, k).start()
            for h in range(2):
                if h:
                    for g in range(2):
                        final_gateup(0, g, first).wait()
                for c in (first, first + 1):
                    total = None
                    for k in range(terms):
                        final_load(h, c, k).wait()
                        start = ((2 * h + c % 2) * terms + k) * depth
                        one = product[0, start : start + depth].astype(WIDE)
                        total = one if total is None else total + one
                    for j in range(2 * unit // LANES):
                        to = (c % 2) * unit + (j // 2) * LANES
                        lanes = total[:, j * LANES : (j + 1) * LANES]
                        final_out[j % 2, :, to : to + LANES] = lanes
                    final_down[h, c % 2] = total[:, 2 * unit :]
                    final_rest(h, c).start()
                for g in range(2):
                    final_gateup(h, g, first).start()

        def final_wait(first):
            for h in range(2):
                for c in (first, first + 1):
                    final_rest(h, c).wait()
                if h:
                    for g in range(2):
                        final_gateup(h, g, first).wait()

        finalize(0)
        load_x = pltpu.make_async_copy(x_ref.at[quarter], low_grad, load_sem.at[1])
        load_x.start()
        for s in range(strips):
            copy = line_copy(3, s, 1, last_in)
            copy.wait_recv()
            copy.wait_send()
        load_x.wait()

        def grads_of(at):
            return jnp.concatenate(
                [keep[s, at] + last_in[s, 0, at].astype(WIDE) for s in range(strips)], axis=1
            )

        def store(at, there, grad_values):
            low_out[at] = (middle[at] + grad_values).astype(LOW)

        rms_back(lambda at: low_grad[at].astype(WIDE), gains_full[0:1], grads_of, store, 0)
        spread(3, low_out, input_grad_ref)
        for owner in range(devices):
            gain_blocks[owner] = gain_rows[:, owner * depth : (owner + 1) * depth]
        for mask in range(1, devices):
            gain_copy(mask).start()

        again = [
            pltpu.make_async_copy(
                saved_middle.at[:, pl.ds(s * strip, strip)], keep.at[s], strip_sem.at[s % 2, s // 2]
            )
            for s in range(strips)
        ]
        for copy in again:
            copy.start()
        proj.pump()
        for mask in range(1, devices):
            gain_copy(mask).wait_recv()
        total = gain_blocks[me]
        for mask in range(1, devices):
            total = total + gain_land[mask]
        gain_part[...] = total
        for mask in range(1, 4):
            tensor_copy(mask).start()
        from_pair(2)
        for s, copy in enumerate(again):
            columns = slice(s * strip, (s + 1) * strip)
            copy.wait()
            low_grad[:, columns] = (keep[s] + flat[:, columns]).astype(LOW)
        spread(6, low_grad, output_ref)
        final_wait(0)
        finalize(2)
        spread_on(3, input_grad_ref)
        for mask in range(1, 4):
            tensor_copy(mask).wait_recv()
        gains_sum[...] = gain_part[...] + tensor_land[1] + tensor_land[2] + tensor_land[3]
        spread_on(6, output_ref)
        for gather in [out, proj]:
            gather.arrive()
        for gather in hidden[chunks - 1 :] + [out, proj]:
            gather.free()
        final_wait(2)
        for gather in hidden + [out, proj]:
            gather.release()
        for base, source, target in ((3, low_out, input_grad_ref), (6, low_grad, output_ref)):
            spread_end(base, target)
            spread_release(base, source, target)
        for mask in range(1, devices):
            gain_copy(mask).wait_send()
        for mask in range(1, 4):
            tensor_copy(mask).wait_send()
        for index in (0, 1, 2, 3, 7, 8, 9, 10):
            token(index).wait_send()
        for one in [gains, proj_in, out_in] + hidden_in:
            one.drain()
        pl.semaphore_wait(credit, 2)

    pl.run_scoped(
        second_phase,
        pltpu.VMEM((rows, width), LOW),
        pltpu.VMEM(out_full.shape, LOW),
        pltpu.VMEM(proj_full.shape, LOW),
        pltpu.VMEM(saved_query.shape, LOW),
        pltpu.VMEM(saved_key.shape, LOW),
        pltpu.VMEM(saved_value.shape, LOW),
        pltpu.VMEM(saved_mixed.shape, LOW),
        pltpu.VMEM((rows, width), LOW),
        pltpu.VMEM(saved_query.shape, LOW),
        pltpu.VMEM(saved_query.shape, WIDE),
        pltpu.VMEM(saved_key.shape, WIDE),
        pltpu.VMEM(saved_key.shape, WIDE),
        pltpu.VMEM((rows, proj_full.shape[1]), LOW),
        pltpu.VMEM(out_full.shape, LOW),
        pltpu.VMEM(proj_full.shape, LOW),
        pltpu.VMEM(cosine_ref.shape, WIDE),
        pltpu.VMEM(sine_ref.shape, WIDE),
        pltpu.VMEM((piece, width), LOW),
        pltpu.VMEM((2, depth, 2 * unit), WIDE),
        pltpu.VMEM((2, 2, depth, unit), WIDE),
    )


def whole_layer(x, cot, places, query, keyval, output, gateup, down, gains, count):
    rows, width = cot.shape
    devices = lax.axis_size("dp")
    spans = devices // 2
    depth, query_width = query.shape
    key_width = keyval.shape[2]
    kv = key_width // HD
    proj_width = query_width + 2 * key_width
    chunks = CHUNKS
    assert chunks == 4
    unit = down.shape[1] // (2 * chunks)
    columns = 3 * unit
    half, piece = rows // 2, rows // 4
    strip = width // (2 * chunks)
    strips = width // strip
    vmem = pl.BlockSpec(memory_space=pltpu.VMEM)
    anywhere = pl.BlockSpec(memory_space=pl.ANY)
    shape = jax.ShapeDtypeStruct
    dma = pltpu.SemaphoreType.DMA
    low, wide = (lambda *sizes: pltpu.VMEM(sizes, LOW)), (lambda *sizes: pltpu.VMEM(sizes, WIDE))
    return pl.pallas_call(
        functools.partial(whole_kernel, (count, rows // count)),
        in_specs=[anywhere] * 2 + [vmem] + [anywhere] * 5 + [vmem],
        out_specs=[anywhere] * 5 + [vmem] + [anywhere] * 21,
        out_shape=[
            shape((2, chunks, spans // 2, depth, columns), LOW),
            shape((spans, depth, query_width), LOW),
            shape((spans, depth, proj_width), LOW),
            shape((rows, width), LOW),
            shape((rows, width), LOW),
            shape((8, depth), WIDE),
            shape(gateup.shape, WIDE),
            shape(down.shape, WIDE),
            shape((2, chunks, depth, columns), LOW),
            shape((chunks, width, columns), LOW),
            shape((width, proj_width), LOW),
            shape((width, query_width), LOW),
            shape((rows, width), LOW),
            shape((2, rows, width), LOW),
            shape((chunks, spans, depth, columns), LOW),
            shape((spans, depth, query_width), LOW),
            shape((spans, depth, proj_width), LOW),
            shape((rows, width), LOW),
            shape((strips, 2, piece, strip), LOW),
            shape((rows, width), LOW),
            shape((rows, query_width), LOW),
            shape((kv, rows, HD), LOW),
            shape((kv, rows, HD), LOW),
            shape((rows, query_width), LOW),
            shape((piece, width), WIDE),
            shape((rows, 2 * HD), WIDE),
            shape((rows, 2 * HD), WIDE),
        ],
        scratch_shapes=[
            low(SLOTS, width, columns),
            low(2, depth, columns),
            low(2, 2, half, strip),
            low(2, 2, half, strip),
            wide(2, half, strip),
            wide(strips, piece, strip),
            low(strips, 2, piece, strip),
            low(strips, 2, piece, strip),
            low(strips, 1, piece, strip),
            low(2, strips, piece, strip),
            wide(piece, width),
            wide(piece, width),
            low(piece, width),
            wide(kv, 8, rows),
            low(depth, proj_width),
            low(depth, query_width),
            wide(8, depth),
            wide(devices, 8, depth),
            wide(8, width),
            wide(8, width),
            wide(devices, 8, depth),
            wide(devices, 8, depth),
            wide(8, depth),
            wide(4, 8, depth),
            dma((3, 2, spans)),
            dma((3, 2, spans)),
            dma((chunks, 2, spans)),
            dma((chunks, 2, spans)),
            dma((11,)),
            dma((11,)),
            dma((chunks + 2, 2, spans)),
            dma((chunks + 2, 2, spans)),
            dma((chunks + 2, 4)),
            dma((2,)),
            dma((2,)),
            dma((4, strips)),
            dma((4, strips)),
            dma((2, strips)),
            dma((2, strips)),
            dma((9,)),
            dma((9,)),
            dma((devices,)),
            dma((devices,)),
            dma((4,)),
            dma((4,)),
            dma((3 + chunks,)),
            dma((10,)),
            dma((8,)),
            dma((2, chunks)),
            dma((9,)),
            dma((max(8, spans * 2),)),
            dma((8,)),
            pltpu.SemaphoreType.REGULAR,
        ],
        compiler_params=pltpu.CompilerParams(
            collective_id=0, has_side_effects=True, vmem_limit_bytes=63 * MEGABYTE
        ),
        name="whole_layer",
    )(x, cot, places, query, keyval, output, gateup, down, gains)


def adamw(weight, grad, first, second, rate, decay):
    first = BETA_ONE * first + (1.0 - BETA_ONE) * grad
    second = BETA_TWO * second + (1.0 - BETA_TWO) * grad * grad
    fixed_first = first * (1.0 / (1.0 - BETA_ONE**STEP))
    fixed_second = second * (1.0 / (1.0 - BETA_TWO**STEP))
    weight = weight - rate * (fixed_first / (jnp.sqrt(fixed_second) + ADAM_EPS) + decay * weight)
    return (first, second, weight)


def matrix_step(weight, grad, first, second):
    return adamw(weight, grad, first, second, MATRIX_RATE, WEIGHT_DECAY)


def update_kernel(*refs):
    ins, outs = refs[:21], refs[21:]
    query, keyval, output, down, gateup = (ins[3 * k : 3 * k + 3] for k in range(5))
    proj_terms, out_terms, down_sum, gateup_sum, block_low, input_low = ins[15:]
    query_outs, keyval_outs, output_outs, down_outs, gateup_outs = (
        outs[4 * k : 4 * k + 4] for k in range(5)
    )
    block_output, input_grad = outs[20:]
    block_output[...] = block_low[...].astype(WIDE)
    input_grad[...] = input_low[...].astype(WIDE)

    def apply(parts, grad, targets, at=slice(None)):
        weight, first, second = (part[at] for part in parts)
        targets[0][at] = grad
        for target, value in zip(targets[1:], matrix_step(weight, grad, first, second)):
            target[at] = value

    proj = jnp.sum(proj_terms[...].astype(WIDE), axis=0)
    query_width = query[0].shape[1]
    key_width = keyval[0].shape[2]
    apply(query, proj[:, :query_width], query_outs)
    for g in range(2):
        start = query_width + g * key_width
        apply(keyval, proj[:, start : start + key_width], keyval_outs, (slice(None), g))
        apply(gateup, gateup_sum[:, g], gateup_outs, (slice(None), g))
    apply(output, jnp.sum(out_terms[...].astype(WIDE), axis=0), output_outs)
    apply(down, down_sum[...], down_outs)


def update(
    query, keyval, output, down, gateup, proj_terms, out_terms, down_sum, gateup_sum, block, grad
):
    depth = query[0].shape[0]
    rows = min(32, depth)
    steps = depth // rows
    tokens = block.shape[0] // steps

    def by_rows(array, dim=0, rows=rows):
        shape = array.shape[:dim] + (rows,) + array.shape[dim + 1 :]
        place = (0,) * array.ndim
        return pl.BlockSpec(shape, lambda i: place[:dim] + (i,) + place[dim + 1 :])

    matrices = (query, keyval, output, down, gateup)
    blocked = [part for parts in matrices for part in parts]
    made = [parts[0] for parts in matrices for _ in range(4)]
    results = pl.pallas_call(
        update_kernel,
        grid=(steps,),
        in_specs=[by_rows(array) for array in blocked]
        + [by_rows(proj_terms, 1), by_rows(out_terms, 1), by_rows(down_sum), by_rows(gateup_sum)]
        + [by_rows(block, rows=tokens), by_rows(grad, rows=tokens)],
        out_specs=[by_rows(array) for array in made] + [by_rows(block, rows=tokens)] * 2,
        out_shape=[jax.ShapeDtypeStruct(array.shape, WIDE) for array in made + [block, grad]],
        compiler_params=pltpu.CompilerParams(vmem_limit_bytes=56 * MEGABYTE),
        name="update",
    )(*blocked, proj_terms, out_terms, down_sum, gateup_sum, block, grad)
    return [results[4 * k : 4 * k + 4] for k in range(5)] + [results[20:]]


def body(
    block_input,
    cotangent,
    positions,
    query_weight,
    keyval_weight,
    output_weight,
    gateup_weight,
    down_weight,
    norm_gains,
    query_first,
    keyval_first,
    output_first,
    gateup_first,
    down_first,
    gains_first,
    query_second,
    keyval_second,
    output_second,
    gateup_second,
    down_second,
    gains_second,
):
    count, length, width = block_input.shape
    rows = count * length
    depth = query_weight.shape[0]
    query_width = query_weight.shape[1]
    key_width = keyval_weight.shape[2]
    me = lax.axis_index("dp")
    pair_bit = (me // PAIR) % 2

    _, output_terms, proj_terms, block_low, input_low, gains_sum, gateup_sum, down_sum = whole_layer(
        block_input.reshape(rows, width),
        cotangent.reshape(rows, width),
        positions.reshape(1, rows),
        query_weight,
        keyval_weight,
        output_weight,
        gateup_weight,
        down_weight,
        norm_gains,
        count,
    )[:8]
    gains_reduced = gains_sum[:2]
    (
        (query_reduced, query_mean, query_square, query_next),
        (keyval_reduced, keyval_mean, keyval_square, keyval_next),
        (output_reduced, output_mean, output_square, output_next),
        (down_reduced, down_mean, down_square, down_next),
        (gateup_reduced, gateup_mean, gateup_square, gateup_next),
        (block_output, input_grad),
    ) = update(
        (query_weight, query_first, query_second),
        (keyval_weight, keyval_first, keyval_second),
        (output_weight, output_first, output_second),
        (down_weight, down_first, down_second),
        (gateup_weight, gateup_first, gateup_second),
        proj_terms,
        output_terms,
        down_sum,
        gateup_sum,
        block_low,
        input_low,
    )
    gains_mean, gains_square, gains_next = adamw(
        norm_gains, gains_reduced, gains_first, gains_second, GAIN_RATE, 0.0
    )
    return (
        block_output.reshape(count, length, width),
        input_grad.reshape(count, length, width),
        query_reduced,
        keyval_reduced,
        output_reduced,
        gateup_reduced,
        down_reduced,
        gains_reduced,
        query_mean,
        keyval_mean,
        output_mean,
        gateup_mean,
        down_mean,
        gains_mean,
        query_square,
        keyval_square,
        output_square,
        gateup_square,
        down_square,
        gains_square,
        query_next,
        keyval_next,
        output_next,
        gateup_next,
        down_next,
        gains_next,
    )


def solution(mesh):
    in_specs = (
        P("dp", None, None),
        P("dp", None, None),
        P("dp", None),
        P("dp", "tensor"),
        P("dp", None, "tensor"),
        P("dp", "tensor"),
        P("dp", None, "tensor"),
        P("dp", "tensor"),
        P(None, "dp"),
        P("dp", "tensor"),
        P("dp", None, "tensor"),
        P("dp", "tensor"),
        P("dp", None, "tensor"),
        P("dp", "tensor"),
        P(None, "dp"),
        P("dp", "tensor"),
        P("dp", None, "tensor"),
        P("dp", "tensor"),
        P("dp", None, "tensor"),
        P("dp", "tensor"),
        P(None, "dp"),
    )
    out_specs = (
        P("dp", None, None),
        P("dp", None, None),
        P("dp", "tensor"),
        P("dp", None, "tensor"),
        P("dp", "tensor"),
        P("dp", None, "tensor"),
        P("dp", "tensor"),
        P(None, "dp"),
        P("dp", "tensor"),
        P("dp", None, "tensor"),
        P("dp", "tensor"),
        P("dp", None, "tensor"),
        P("dp", "tensor"),
        P(None, "dp"),
        P("dp", "tensor"),
        P("dp", None, "tensor"),
        P("dp", "tensor"),
        P("dp", None, "tensor"),
        P("dp", "tensor"),
        P(None, "dp"),
        P("dp", "tensor"),
        P("dp", None, "tensor"),
        P("dp", "tensor"),
        P("dp", None, "tensor"),
        P("dp", "tensor"),
        P(None, "dp"),
    )
    return jax.shard_map(body, mesh=mesh, in_specs=in_specs, out_specs=out_specs, check_vma=False)
```
